32 devices in a mesh: seq: 8 (over y, x, core), head: 4 (over z).
Axes of the slice: x: 2, y: 2, z: 4, core: 2. Of those that a mesh axis runs over, the one named last changes fastest.
Arguments:
- queries: bfloat16 [1024, 512], P('seq', 'head'), may hold values from -108 to 108
- key_rows: bfloat16 [1024, 512], P('seq', 'head'), may hold values from -4.5 to 4.5
- value_rows: bfloat16 [1024, 512], P('seq', 'head'), may hold values from -6 to 6
- out_weight: bfloat16 [512, 2048], P('head'), may hold values from -4 to 4
- strided_index: int32 [8, 8], P('seq'), may hold values from 0 to 1
- cotangent: bfloat16 [1024, 2048], P('seq'), may hold values from -6 to 6
Outputs:
- mixed_output: bfloat16 [1024, 2048], P('seq', 'head')
- grad_queries: bfloat16 [1024, 512], P('seq', 'head')
- grad_keys: bfloat16 [1024, 512], P('seq', 'head')
- grad_values: bfloat16 [1024, 512], P('seq', 'head')
The draws below stay inside these ranges and needn't reach their ends.
All inputs are finite; a program needn't handle non-finite values.
Results may differ from the reference program's by a relative error of at most 0.023.
Values may be sent and summed in bfloat16 or wider, within the bound.
No kernel may reach another device: no remote copies, remote signals or barrier semaphores. Data moves between devices by JAX's collectives and lax.ppermute only.
A program may use at most 64 MiB of HBM per device.

```python
import jax
import jax.numpy as jnp
from jax import lax

HD = 128
D = 2048
BLK = 128
NSTR = 8
STRIDE_ROWS = 32
TOK_DEV = 128
HEADS = 4
TOKENS = 1024
NBLK = 8
NSB = 2


def draw_pair(key):
    base = jax.random.fold_in(key, 7)
    first, second = jax.random.split(base, 2)
    shaped = (TOKENS, HEADS * HD)
    key_values = jnp.clip(jax.random.normal(first, shaped, jnp.float32), -4.5, 4.5)
    query_values = jnp.clip(jax.random.normal(second, shaped, jnp.float32), -4.5, 4.5)
    return (query_values, key_values)


def draw_queries(key, part):
    return draw_pair(key)[0].astype(jnp.bfloat16)


def draw_key_rows(key, part):
    return draw_pair(key)[1].astype(jnp.bfloat16)


def place_ends(result, own_key, smallest, high):
    spot = [jax.random.randint(jax.random.fold_in(own_key, axis), (), 0, length) for axis, length in enumerate(result.shape)]
    longest = result.shape.index(max(result.shape))
    beside = spot[:longest] + [(spot[longest] + 1) % result.shape[longest]] + spot[longest + 1:]
    return result.at[tuple(spot)].set(smallest).at[tuple(beside)].set(high)


def level_of(rng, dims, cuts, low, largest):
    def one(dim, shards_of):
        draws = jax.random.uniform(jax.random.fold_in(jax.random.fold_in(rng, 6), dim), (shards_of,), jnp.float32, low / len(cuts), largest / len(cuts))
        return jnp.repeat(jnp.exp(draws), dims[dim] // shards_of).reshape((-1,) + (1,) * (len(dims) - dim - 1))

    loudness = one(*cuts[0])
    for cut in cuts[1:]:
        loudness = loudness * one(*cut)
    return loudness


def scatter_about(stream_key, shape, spread, most, cuts=(), kind=jnp.bfloat16):
    result = spread * jax.random.normal(stream_key, shape, jnp.float32)
    if cuts:
        result = result * level_of(stream_key, shape, cuts, -0.22, 0.18)
    return jnp.clip(result, -most, most).astype(kind)


def setup_inputs(seed: int = 0) -> dict:
    streams_of = jax.random.split(jax.random.key(seed), 7)
    return {
        "queries": draw_queries(jax.random.fold_in(streams_of[6], 71), 0),
        "key_rows": draw_key_rows(jax.random.fold_in(streams_of[6], 71), 0),
        "value_rows": scatter_about(streams_of[2], (TOKENS, HEADS * HD), 1.0, 6.0, ((0, 8), (1, 4))),
        "out_weight": scatter_about(streams_of[3], (HEADS * HD, D), 2 ** -0.5, 4.0, ((0, 4),)),
        "strided_index": place_ends(jax.random.randint(streams_of[4], (NBLK, NSTR), 0, NSB), jax.random.fold_in(streams_of[4], 1), 0, NSB - 1).astype(jnp.int32),
        "cotangent": scatter_about(streams_of[5], (TOKENS, D), 1.0, 6.0, ((0, 8),)),
    }


def strided_tokens():
    number = jnp.arange(NSB * BLK, dtype=jnp.int32)
    return (number // STRIDE_ROWS) * TOK_DEV + number % STRIDE_ROWS


def block_list(blocks, strided_blocks, index_row, position):
    count = blocks.shape[0]
    window = jnp.stack([blocks[(position - 1) % count], blocks[position], blocks[(position + 1) % count]])
    picked = strided_blocks[index_row]
    joined = jnp.concatenate([window, picked], axis=0)
    return joined.reshape(-1, blocks.shape[2], blocks.shape[3])


def probability_of(query_block, key_list):
    scores = jnp.einsum('qhd,khd->hqk', query_block.astype(jnp.float32), key_list.astype(jnp.float32)) * (HD ** -0.5)
    row_top = jnp.max(scores, axis=-1, keepdims=True)
    logsum = row_top + jnp.log(jnp.sum(jnp.exp(scores - row_top), axis=-1, keepdims=True))
    return jnp.exp(scores - logsum)


def reference(queries, key_rows, value_rows, out_weight, strided_index, cotangent):
    tokens = queries.shape[0]
    count = tokens // BLK
    shaped = (count, BLK, HEADS, HD)
    query_blocks = queries.reshape(shaped)
    key_blocks = key_rows.reshape(shaped)
    value_blocks = value_rows.reshape(shaped)
    chosen = strided_tokens()
    key_strided = key_rows.reshape(tokens, HEADS, HD)[chosen].reshape(NSB, BLK, HEADS, HD)
    value_strided = value_rows.reshape(tokens, HEADS, HD)[chosen].reshape(NSB, BLK, HEADS, HD)
    numbers = jnp.arange(count, dtype=jnp.int32)

    def forward(position):
        key_list = block_list(key_blocks, key_strided, strided_index[position], position)
        value_list = block_list(value_blocks, value_strided, strided_index[position], position)
        weights = probability_of(query_blocks[position], key_list).astype(jnp.bfloat16)
        output = jnp.einsum('hqk,khd->qhd', weights.astype(jnp.float32), value_list.astype(jnp.float32))
        return output.astype(jnp.bfloat16)

    attention = lax.map(forward, numbers).reshape(tokens, HEADS * HD)
    mixed_output = jnp.dot(attention, out_weight, preferred_element_type=jnp.float32).astype(jnp.bfloat16)
    grad_attention = jnp.dot(cotangent, out_weight.T, preferred_element_type=jnp.float32).astype(jnp.bfloat16)
    grad_blocks = grad_attention.reshape(shaped)

    def backward(state_pair, position):
        key_sum, value_sum, key_side, value_side = state_pair
        key_list = block_list(key_blocks, key_strided, strided_index[position], position)
        value_list = block_list(value_blocks, value_strided, strided_index[position], position)
        query_block = query_blocks[position].astype(jnp.float32)
        grad_block = grad_blocks[position].astype(jnp.float32)
        probability = probability_of(query_blocks[position], key_list)
        weights = probability.astype(jnp.bfloat16)
        grad_weights = jnp.einsum('qhd,khd->hqk', grad_block, value_list.astype(jnp.float32))
        row_delta = jnp.sum(probability * grad_weights, axis=-1, keepdims=True)
        grad_scores = (probability * (grad_weights - row_delta) * (HD ** -0.5)).astype(jnp.bfloat16)
        grad_query = jnp.einsum('hqk,khd->qhd', grad_scores.astype(jnp.float32), key_list.astype(jnp.float32)).astype(jnp.bfloat16)
        key_terms = jnp.einsum('hqk,qhd->khd', grad_scores.astype(jnp.float32), query_block)
        value_terms = jnp.einsum('hqk,qhd->khd', weights.astype(jnp.float32), grad_block)
        places = jnp.stack([(position - 1) % count, position, (position + 1) % count]).astype(jnp.int32)
        key_sum = key_sum.at[places].add(key_terms[:3 * BLK].reshape(3, BLK, HEADS, HD))
        value_sum = value_sum.at[places].add(value_terms[:3 * BLK].reshape(3, BLK, HEADS, HD))
        picks = strided_index[position]
        key_side = key_side.at[picks].add(key_terms[3 * BLK:].reshape(-1, BLK, HEADS, HD))
        value_side = value_side.at[picks].add(value_terms[3 * BLK:].reshape(-1, BLK, HEADS, HD))
        return (key_sum, value_sum, key_side, value_side), grad_query

    start_state = (jnp.zeros(shaped, jnp.float32), jnp.zeros(shaped, jnp.float32),
                   jnp.zeros((NSB, BLK, HEADS, HD), jnp.float32), jnp.zeros((NSB, BLK, HEADS, HD), jnp.float32))
    final_state, grad_parts = lax.scan(backward, start_state, numbers)
    key_sum, value_sum, key_side, value_side = final_state
    key_total = key_sum.reshape(tokens, HEADS, HD).at[chosen].add(key_side.reshape(NSB * BLK, HEADS, HD))
    value_total = value_sum.reshape(tokens, HEADS, HD).at[chosen].add(value_side.reshape(NSB * BLK, HEADS, HD))
    grad_queries = grad_parts.reshape(tokens, HEADS * HD)
    grad_keys = key_total.reshape(tokens, HEADS * HD).astype(jnp.bfloat16)
    grad_values = value_total.reshape(tokens, HEADS * HD).astype(jnp.bfloat16)
    return (mixed_output, grad_queries, grad_keys, grad_values)
```

```python
import jax
import jax.numpy as jnp
from jax import lax
from jax.experimental import pallas as pl
from jax.experimental.pallas import tpu as pltpu
from jax.sharding import PartitionSpec as P

HD = 128
BLK = 128
STRIDE_ROWS = 32
SCALE = HD ** (-0.5)
LOG2E = 1.4426950408889634
ABSENT = -1e30
VMEM = pl.BlockSpec(memory_space=pltpu.VMEM)
SMEM = pl.BlockSpec(memory_space=pltpu.SMEM)


def shift(array, axis, step):
    count = lax.axis_size(axis)
    return lax.ppermute(array, axis, [(i, (i + step) % count) for i in range(count)])


def dot_nt(a, b):
    return lax.dot_general(a, b, (((1,), (1,)), ((), ())), preferred_element_type=jnp.float32)


def dot_nn(a, b):
    return lax.dot_general(a, b, (((1,), (0,)), ((), ())), preferred_element_type=jnp.float32)


def dot_tn(a, b):
    return lax.dot_general(a, b, (((0,), (0,)), ((), ())), preferred_element_type=jnp.float32)


def attend_kernel(index_ref, q_ref, own_ref, left_ref, right_ref, side_ref, grad_ref,
                  att_ref, dq_ref, own_sum_ref, to_left_ref, to_right_ref, to_side_ref):
    side_count = side_ref.shape[0] // BLK
    slots = index_ref.shape[1]
    picks = [index_ref[0, i] for i in range(slots)]
    counts = []
    for j in range(side_count):
        total = jnp.int32(0)
        for pick in picks:
            total = total + jnp.where(pick == j, 1, 0)
        counts.append(total)
    parts = [(own_ref, 0, None), (left_ref, 0, None), (right_ref, 0, None)]
    parts += [(side_ref, j * BLK, counts[j]) for j in range(side_count)]
    keys = [ref[r:r + BLK, :HD] for ref, r, _ in parts]
    values = [ref[r:r + BLK, HD:] for ref, r, _ in parts]
    q = q_ref[...]
    grad = grad_ref[...]

    raw = []
    for k, (_, _, count) in zip(keys, parts):
        s = dot_nt(q, k)
        if count is not None:
            s = s + jnp.where(count > 0, 0.0, ABSENT)
        raw.append(s)
    top = raw[0]
    for s in raw[1:]:
        top = jnp.maximum(top, s)
    top = jnp.max(top, axis=1, keepdims=True)
    terms = []
    total = None
    for s, (_, _, count) in zip(raw, parts):
        e = jnp.exp2((s - top) * (SCALE * LOG2E))
        if count is not None:
            e = e * count.astype(jnp.float32)
        terms.append(e)
        total = e if total is None else total + e
    inverse = 1.0 / jnp.sum(total, axis=1, keepdims=True)
    probability = [e * inverse for e in terms]
    weights = [p.astype(jnp.bfloat16) for p in probability]
    att = None
    for w, v in zip(weights, values):
        term = dot_nn(w, v)
        att = term if att is None else att + term
    att_ref[...] = att.astype(jnp.bfloat16)

    grad_weights = [dot_nt(grad, v) for v in values]
    delta = None
    for p, g in zip(probability, grad_weights):
        delta = p * g if delta is None else delta + p * g
    delta = jnp.sum(delta, axis=1, keepdims=True)
    grad_scores = [(p * (g - delta) * SCALE).astype(jnp.bfloat16)
                   for p, g in zip(probability, grad_weights)]
    dq = None
    for g, k in zip(grad_scores, keys):
        term = dot_nn(g, k)
        dq = term if dq is None else dq + term
    dq_ref[...] = dq.astype(jnp.bfloat16)

    outs = [(own_sum_ref, 0), (to_left_ref, 0), (to_right_ref, 0)]
    outs += [(to_side_ref, j * BLK) for j in range(side_count)]
    for (ref, r), g, w in zip(outs, grad_scores, weights):
        ref[r:r + BLK, :HD] = dot_tn(g, q).astype(ref.dtype)
        ref[r:r + BLK, HD:] = dot_tn(w, grad).astype(ref.dtype)


def attend(index, q, own, left, right, side, grad):
    bf16 = jnp.bfloat16
    return pl.pallas_call(
        attend_kernel,
        out_shape=(
            jax.ShapeDtypeStruct((BLK, HD), bf16),
            jax.ShapeDtypeStruct((BLK, HD), bf16),
            jax.ShapeDtypeStruct((BLK, 2 * HD), jnp.float32),
            jax.ShapeDtypeStruct((BLK, 2 * HD), bf16),
            jax.ShapeDtypeStruct((BLK, 2 * HD), bf16),
            jax.ShapeDtypeStruct(side.shape, bf16),
        ),
        in_specs=[SMEM] + [VMEM] * 6,
        out_specs=(VMEM,) * 6,
        compiler_params=pltpu.CompilerParams(vmem_limit_bytes=40 * 1024 * 1024),
        name="attend",
    )(index, q, own, left, right, side, grad)


def prepare_kernel(me_ref, cot_ref, w_ref, grad_ref, *slice_refs):
    grad_ref[...] = dot_nt(cot_ref[...], w_ref[...]).astype(grad_ref.dtype)
    heads = len(slice_refs)
    width = slice_refs[0].shape[1]
    me = me_ref[0]
    for s, ref in enumerate(slice_refs):
        target = lax.rem(me + s, heads)
        start = pl.multiple_of(target * width, width)
        ref[...] = w_ref[:, pl.ds(start, width)]


def prepare(cotangent, out_weight, heads):
    me = lax.axis_index("head").astype(jnp.int32).reshape(1)
    width = out_weight.shape[1] // heads
    return pl.pallas_call(
        prepare_kernel,
        out_shape=(jax.ShapeDtypeStruct((BLK, HD), jnp.bfloat16),)
        + (jax.ShapeDtypeStruct((HD, width), jnp.bfloat16),) * heads,
        in_specs=[SMEM, VMEM, VMEM],
        out_specs=(VMEM,) * (1 + heads),
        compiler_params=pltpu.CompilerParams(vmem_limit_bytes=40 * 1024 * 1024),
        name="prepare",
    )(me, cotangent, out_weight)


def finish_kernel(heads, *refs):
    att_refs = refs[:heads]
    w_refs = refs[heads:2 * heads]
    own_ref, left_ref, right_ref, side_ref, mixed_ref, dk_ref, dv_ref = refs[2 * heads:]
    mixed = None
    for a, w in zip(att_refs, w_refs):
        term = dot_nn(a[...], w[...])
        mixed = term if mixed is None else mixed + term
    mixed_ref[...] = mixed.astype(mixed_ref.dtype)
    total = own_ref[...] + left_ref[...].astype(jnp.float32) + right_ref[...].astype(jnp.float32)
    lead = total[:STRIDE_ROWS]
    for i in range(side_ref.shape[0] // STRIDE_ROWS):
        lead = lead + side_ref[i * STRIDE_ROWS:(i + 1) * STRIDE_ROWS].astype(jnp.float32)
    for ref, c in ((dk_ref, 0), (dv_ref, HD)):
        ref[:STRIDE_ROWS] = lead[:, c:c + HD].astype(ref.dtype)
        ref[STRIDE_ROWS:] = total[STRIDE_ROWS:, c:c + HD].astype(ref.dtype)


def finish(attentions, slices, own, left, right, side):
    heads = len(attentions)
    width = slices[0].shape[1]

    def body(*refs):
        finish_kernel(heads, *refs)

    return pl.pallas_call(
        body,
        out_shape=(
            jax.ShapeDtypeStruct((BLK, width), jnp.bfloat16),
            jax.ShapeDtypeStruct((BLK, HD), jnp.bfloat16),
            jax.ShapeDtypeStruct((BLK, HD), jnp.bfloat16),
        ),
        in_specs=[VMEM] * (2 * heads + 4),
        out_specs=(VMEM,) * 3,
        compiler_params=pltpu.CompilerParams(vmem_limit_bytes=40 * 1024 * 1024),
        name="finish",
    )(*attentions, *slices, own, left, right, side)


def shards(queries, key_rows, value_rows, out_weight, strided_index, cotangent):
    seq = lax.axis_size("seq")
    heads = lax.axis_size("head")
    own = jnp.concatenate([key_rows, value_rows], axis=1)
    lead = jnp.broadcast_to(own[None, :STRIDE_ROWS], (seq, STRIDE_ROWS, 2 * HD))
    left = shift(own, "seq", 1)
    right = shift(own, "seq", -1)
    side = lax.all_to_all(lead, "seq", 0, 0).reshape(seq * STRIDE_ROWS, 2 * HD)
    grad, *slices = prepare(cotangent, out_weight, heads)
    slices = [slices[0]] + [shift(slices[s], "head", s) for s in range(1, heads)]
    att, dq, own_sum, to_left, to_right, to_side = attend(
        strided_index, queries, own, left, right, side, grad
    )
    attentions = [att] + [shift(att, "head", s) for s in range(1, heads)]
    from_right = shift(to_left, "seq", -1)
    from_left = shift(to_right, "seq", 1)
    from_side = lax.all_to_all(
        to_side.reshape(seq, STRIDE_ROWS, 2 * HD), "seq", 0, 0
    ).reshape(seq * STRIDE_ROWS, 2 * HD)
    mixed, dk, dv = finish(attentions, slices, own_sum, from_left, from_right, from_side)
    return (mixed, dq, dk, dv)


def solution(mesh):
    in_specs = (
        P("seq", "head"),
        P("seq", "head"),
        P("seq", "head"),
        P("head", None),
        P("seq", None),
        P("seq", None),
    )
    out_specs = (P("seq", "head"), P("seq", "head"), P("seq", "head"), P("seq", "head"))
    return jax.shard_map(shards, mesh=mesh, in_specs=in_specs, out_specs=out_specs, check_vma=False)
```

```python
import jax
import jax.numpy as jnp
from jax import lax
from jax.experimental import pallas as pl
from jax.experimental.pallas import tpu as pltpu
from jax.sharding import PartitionSpec as P

HD = 128
BLK = 128
STRIDE_ROWS = 32
PAIR = 2 * HD
SCALE = HD ** (-0.5)
LOG2E = 1.4426950408889634
ABSENT = -1e30
VMEM = pl.BlockSpec(memory_space=pltpu.VMEM)
SMEM = pl.BlockSpec(memory_space=pltpu.SMEM)
PARAMS = pltpu.CompilerParams(vmem_limit_bytes=40 * 1024 * 1024)
BF16 = jnp.bfloat16
F32 = jnp.float32


def dot_nt(a, b):
    return lax.dot_general(a, b, (((1,), (1,)), ((), ())), preferred_element_type=F32)


def dot_nn(a, b):
    return lax.dot_general(a, b, (((1,), (0,)), ((), ())), preferred_element_type=F32)


def dot_tn(a, b):
    return lax.dot_general(a, b, (((0,), (0,)), ((), ())), preferred_element_type=F32)


def shape(*dims, kind=BF16):
    return jax.ShapeDtypeStruct(dims, kind)


def trade(array, step):
    count = lax.axis_size("seq")
    return lax.ppermute(
        array, "seq", [(i, (i + (step if i % 2 == 0 else -step)) % count) for i in range(count)]
    )


def swap(array, mask):
    count = lax.axis_size("head")
    return lax.ppermute(array, "head", [(i, i ^ mask) for i in range(count)])


def own_counts(picks, group):
    total = jnp.zeros(group.shape, F32)
    for pick in picks:
        total = total + jnp.where(group == pick, 1.0, 0.0)
    return total


def prepare_kernel(ring, me_ref, index_ref, cot_ref, w_ref, grad_ref, mult_ref, *slice_refs):
    per_block = BLK // STRIDE_ROWS
    picks = [index_ref[0, i] for i in range(index_ref.shape[1])]
    rows, columns = mult_ref.shape
    lane = lax.broadcasted_iota(jnp.int32, (rows, columns), 1)
    if ring:
        b = me_ref[0]
        sign = 1 - 2 * lax.rem(b, 2)
        offsets = [(0, 0), (BLK, 1), (2 * BLK, -1), (3 * BLK, 3), (3 * BLK + 32, 2),
                   (3 * BLK + 64, 4), (3 * BLK + 96, -3), (3 * BLK + 128, -2)]
        owner = jnp.full((rows, columns), -per_block, jnp.int32)
        for start, offset in offsets:
            inside = (lane >= start) & (lane < start + STRIDE_ROWS)
            owner = jnp.where(inside, lax.rem(b + 16 + sign * offset, 8), owner)
        group = jnp.where(owner < 0, -1, owner // per_block)
    else:
        group = jnp.where(lane < 3 * BLK, -1, (lane - 3 * BLK) // BLK)
    mult_ref[...] = own_counts(picks, group) + jnp.where(lane < 3 * BLK, 1.0, 0.0)

    grad_ref[...] = dot_nt(cot_ref[...], w_ref[...]).astype(grad_ref.dtype)
    width = slice_refs[0].shape[1]
    head = me_ref[1]
    for r, ref in enumerate(slice_refs):
        start = pl.multiple_of((head ^ r) * width, width)
        ref[...] = w_ref[:, pl.ds(start, width)]


def prepare(ring, me, index, cotangent, out_weight, heads, columns):
    width = out_weight.shape[1] // heads

    def body(*refs):
        prepare_kernel(ring, *refs)

    return pl.pallas_call(
        body,
        out_shape=(shape(BLK, HD), shape(8, columns, kind=F32)) + (shape(HD, width),) * heads,
        in_specs=[SMEM, SMEM, VMEM, VMEM],
        out_specs=(VMEM,) * (2 + heads),
        compiler_params=PARAMS,
        name="prepare",
    )(me, index, cotangent, out_weight)


def attend_kernel(sides, mult_ref, q_ref, grad_ref, *refs):
    block_refs = refs[:3 + sides]
    att_ref, dq_ref = refs[3 + sides:5 + sides]
    sum_refs = refs[5 + sides:8 + 2 * sides]
    keys_ref = refs[-1]
    total_rows = keys_ref.shape[0]
    spans = []
    row = 0
    for ref in block_refs:
        spans.append((row, row + ref.shape[0]))
        keys_ref[row:row + ref.shape[0], :] = ref[...]
        row += ref.shape[0]
    if row < total_rows:
        keys_ref[row:, :] = jnp.zeros((total_rows - row, PAIR), BF16)
    keys = keys_ref[:, :HD]
    values = keys_ref[:, HD:]
    q = q_ref[...]
    grad = grad_ref[...]
    mult = mult_ref[0:1, :]

    scores = dot_nt(q, keys) + jnp.where(mult > 0.0, 0.0, ABSENT)
    top = jnp.max(scores, axis=1, keepdims=True)
    terms = jnp.exp2((scores - top) * (SCALE * LOG2E)) * mult
    probability = terms * (1.0 / jnp.sum(terms, axis=1, keepdims=True))
    weights = probability.astype(BF16)
    att_ref[...] = dot_nn(weights, values).astype(BF16)

    grad_weights = dot_nt(grad, values)
    delta = jnp.sum(probability * grad_weights, axis=1, keepdims=True)
    grad_scores = (probability * (grad_weights - delta) * SCALE).astype(BF16)
    dq_ref[...] = dot_nn(grad_scores, keys).astype(BF16)
    key_terms = dot_tn(grad_scores, q)
    value_terms = dot_tn(weights, grad)
    for (start, end), ref in zip(spans, sum_refs):
        ref[:, :HD] = key_terms[start:end].astype(ref.dtype)
        ref[:, HD:] = value_terms[start:end].astype(ref.dtype)


def attend(mult, q, grad, window, sides):
    def body(*refs):
        attend_kernel(len(sides), *refs)

    return pl.pallas_call(
        body,
        out_shape=(shape(BLK, HD), shape(BLK, HD))
        + (shape(BLK, PAIR, kind=F32),) * 3
        + tuple(shape(*s.shape) for s in sides),
        in_specs=[VMEM] * (6 + len(sides)),
        out_specs=(VMEM,) * (5 + len(sides)),
        scratch_shapes=[pltpu.VMEM((mult.shape[1], PAIR), BF16)],
        compiler_params=PARAMS,
        name="attend",
    )(mult, q, grad, *window, *sides)


def combine_kernel(own_ref, first_ref, second_ref, plus_ref, minus_ref, att_ref, other_ref,
                   own_out, first_out, second_out, att_out):
    plus = plus_ref[...].astype(F32)
    minus = minus_ref[...].astype(F32)
    n = STRIDE_ROWS
    own_out[n:] = own_ref[n:]
    own_out[:n] = own_ref[:n] + plus[:n] + minus[:n]
    first_out[n:] = first_ref[n:].astype(BF16)
    first_out[:n] = (first_ref[:n] + plus[n:2 * n]).astype(BF16)
    second_out[n:] = second_ref[n:].astype(BF16)
    second_out[:n] = (second_ref[:n] + plus[2 * n:] + minus[n:]).astype(BF16)
    att_out[:BLK] = att_ref[...]
    att_out[BLK:] = other_ref[...]


def combine(own, first, second, plus, minus, att, other):
    return pl.pallas_call(
        combine_kernel,
        out_shape=(shape(BLK, PAIR, kind=F32), shape(BLK, PAIR), shape(BLK, PAIR),
                   shape(2 * BLK, HD)),
        in_specs=[VMEM] * 7,
        out_specs=(VMEM,) * 4,
        compiler_params=PARAMS,
        name="combine",
    )(own, first, second, plus, minus, att, other)


def finish_kernel(heads, att_count, extra, *refs):
    att_refs = refs[:att_count]
    w_refs = refs[att_count:att_count + heads]
    rest = refs[att_count + heads:]
    own_ref, first_ref, second_ref = rest[:3]
    mixed_ref, dk_ref, dv_ref = rest[-3:]
    pieces = [(ref, r) for ref in att_refs for r in range(0, ref.shape[0], BLK)]
    mixed = None
    for (ref, r), w in zip(pieces, w_refs):
        term = dot_nn(ref[r:r + BLK], w[...])
        mixed = term if mixed is None else mixed + term
    mixed_ref[...] = mixed.astype(mixed_ref.dtype)
    total = own_ref[...] + first_ref[...].astype(F32) + second_ref[...].astype(F32)
    lead = total[:STRIDE_ROWS]
    if extra:
        side_ref = rest[3]
        for i in range(side_ref.shape[0] // STRIDE_ROWS):
            lead = lead + side_ref[i * STRIDE_ROWS:(i + 1) * STRIDE_ROWS].astype(F32)
    for ref, c in ((dk_ref, 0), (dv_ref, HD)):
        ref[:STRIDE_ROWS] = lead[:, c:c + HD].astype(ref.dtype)
        ref[STRIDE_ROWS:] = total[STRIDE_ROWS:, c:c + HD].astype(ref.dtype)


def finish(attentions, slices, own, first, second, *side):
    heads = len(slices)
    width = slices[0].shape[1]

    def body(*refs):
        finish_kernel(heads, len(attentions), len(side), *refs)

    return pl.pallas_call(
        body,
        out_shape=(shape(BLK, width), shape(BLK, HD), shape(BLK, HD)),
        in_specs=[VMEM] * (len(attentions) + heads + 3 + len(side)),
        out_specs=(VMEM,) * 3,
        compiler_params=PARAMS,
        name="finish",
    )(*attentions, *slices, own, first, second, *side)


def shards(queries, key_rows, value_rows, out_weight, strided_index, cotangent):
    seq = lax.axis_size("seq")
    heads = lax.axis_size("head")
    ring = seq == 8 and heads == 4
    n = STRIDE_ROWS
    me = jnp.stack([lax.axis_index("seq"), lax.axis_index("head")]).astype(jnp.int32)
    own = jnp.concatenate([key_rows, value_rows], axis=1)
    first = trade(own, 1)
    second = trade(own, -1)
    columns = 3 * BLK + (2 * BLK if ring else seq * n)
    grad, mult, *slices = prepare(ring, me, strided_index, cotangent, out_weight, heads, columns)
    slices = [slices[0]] + [swap(slices[r], r) for r in range(1, heads)]
    if ring:
        lead = jnp.concatenate([own[:n], first[:n], second[:n]], axis=0)
        plus = trade(lead, 3)
        minus = trade(jnp.concatenate([own[:n], second[:n]], axis=0), -3)
        att, dq, own_sum, first_sum, second_sum, to_plus, to_minus = attend(
            mult, queries, grad, (own, first, second), (plus, minus)
        )
        own_sum, to_first, to_second, pair = combine(
            own_sum, first_sum, second_sum, trade(to_plus, 3), trade(to_minus, -3),
            att, swap(att, 1),
        )
        mixed, dk, dv = finish(
            (pair, swap(pair, 2)), slices, own_sum, trade(to_first, 1), trade(to_second, -1)
        )
    else:
        spread = jnp.broadcast_to(own[None, :n], (seq, n, PAIR))
        side = lax.all_to_all(spread, "seq", 0, 0).reshape(seq * n, PAIR)
        att, dq, own_sum, first_sum, second_sum, to_side = attend(
            mult, queries, grad, (own, first, second), (side,)
        )
        from_side = lax.all_to_all(to_side.reshape(seq, n, PAIR), "seq", 0, 0)
        mixed, dk, dv = finish(
            [att] + [swap(att, r) for r in range(1, heads)], slices, own_sum,
            trade(first_sum.astype(BF16), 1), trade(second_sum.astype(BF16), -1),
            from_side.reshape(seq * n, PAIR),
        )
    return (mixed, dq, dk, dv)


def solution(mesh):
    in_specs = (
        P("seq", "head"),
        P("seq", "head"),
        P("seq", "head"),
        P("head", None),
        P("seq", None),
        P("seq", None),
    )
    out_specs = (P("seq", "head"), P("seq", "head"), P("seq", "head"), P("seq", "head"))
    return jax.shard_map(shards, mesh=mesh, in_specs=in_specs, out_specs=out_specs, check_vma=False)
```

```python
import jax
import jax.numpy as jnp
from jax import lax
from jax.experimental import pallas as pl
from jax.experimental.pallas import tpu as pltpu
from jax.sharding import PartitionSpec as P

HD = 128
BLK = 128
STRIDE_ROWS = 32
PAIR = 2 * HD
SCALE = HD ** (-0.5)
LOG2E = 1.4426950408889634
ABSENT = -1e30
VMEM = pl.BlockSpec(memory_space=pltpu.VMEM)
HBM = pl.BlockSpec(memory_space=pltpu.HBM)
PARAMS = pltpu.CompilerParams(vmem_limit_bytes=40 * 1024 * 1024)
FULL = pltpu.CompilerParams(vmem_limit_bytes=int(53.3 * 1024 * 1024))
BF16 = jnp.bfloat16
F32 = jnp.float32


def dot_nt(a, b):
    return lax.dot_general(a, b, (((1,), (1,)), ((), ())), preferred_element_type=F32)


def dot_nn(a, b):
    return lax.dot_general(a, b, (((1,), (0,)), ((), ())), preferred_element_type=F32)


def dot_tn(a, b):
    return lax.dot_general(a, b, (((0,), (0,)), ((), ())), preferred_element_type=F32)


def shape(*dims, kind=BF16):
    return jax.ShapeDtypeStruct(dims, kind)


def trade(array, step):
    count = lax.axis_size("seq")
    return lax.ppermute(
        array, "seq", [(i, (i + (step if i % 2 == 0 else -step)) % count) for i in range(count)]
    )


def swap(array, mask):
    count = lax.axis_size("head")
    return lax.ppermute(array, "head", [(i, i ^ mask) for i in range(count)])


def count_of(picks, group):
    total = jnp.int32(0)
    for pick in picks:
        total = total + jnp.where(pick == group, 1, 0)
    return total.astype(F32)


def fill_multiplicity(ring, index_ref, mult_ref):
    per_block = BLK // STRIDE_ROWS
    picks = [index_ref[0, i] for i in range(index_ref.shape[1])]
    shape_of = mult_ref.shape
    lane = lax.broadcasted_iota(jnp.int32, shape_of, 1)
    mult = jnp.where(lane < 3 * BLK, 1.0, 0.0)
    if ring:
        b = lax.axis_index("seq")
        sign = 1 - 2 * (b & 1)
        counts = [count_of(picks, j) for j in range(2)]
        offsets = [(0, 0), (BLK, 1), (2 * BLK, -1), (3 * BLK, 3), (3 * BLK + 32, 2),
                   (3 * BLK + 64, 4), (3 * BLK + 96, -3), (3 * BLK + 128, -2)]
        for start, offset in offsets:
            owner = (b + 16 + sign * offset) & 7
            count = jnp.where(owner < per_block, counts[0], counts[1])
            inside = (lane >= start) & (lane < start + STRIDE_ROWS)
            mult = mult + jnp.where(inside, count, 0.0)
    else:
        for j in range((shape_of[1] - 3 * BLK) // BLK):
            start = (3 + j) * BLK
            inside = (lane >= start) & (lane < start + BLK)
            mult = mult + jnp.where(inside, count_of(picks, j), 0.0)
    mult_ref[...] = mult


CHUNKS = 4


def prepare_kernel(ring, index_hbm, cot_hbm, w_hbm, grad_ref, mult_ref, *refs):
    index_ref, cot_ref, w_ref, sems = refs[-4:]
    slice_refs = refs[:-4]
    width = slice_refs[0].shape[1]
    head = lax.axis_index("head")
    core = lax.axis_index("seq") & 1

    def columns(h):
        return pl.ds(pl.multiple_of(h * width, width), width)

    if ring:
        half = HD // 2
        sources = [
            w_hbm.at[:, columns(head)],
            w_hbm.at[:, columns(head ^ (1 + core))],
            w_hbm.at[pl.ds(pl.multiple_of(core * half, half), half), columns(head ^ 3)],
        ]
    else:
        sources = [w_hbm.at[:, columns(head ^ r)] for r in range(len(slice_refs))]
    copies = [(index_hbm, index_ref)]
    copies += list(zip(sources, slice_refs))
    depth = cot_ref.shape[1] // CHUNKS
    for i in range(CHUNKS):
        span = pl.ds(i * depth, depth)
        copies.append((cot_hbm.at[:, span], cot_ref.at[:, span]))
        copies.append((w_hbm.at[:, span], w_ref.at[:, span]))
    copies = [pltpu.make_async_copy(src, dst, sems.at[i]) for i, (src, dst) in enumerate(copies)]
    for copy in copies:
        copy.start()
    copies[0].wait()
    fill_multiplicity(ring, index_ref, mult_ref)
    fixed = 1 + len(slice_refs)
    total = None
    for i in range(CHUNKS):
        copies[fixed + 2 * i].wait()
        copies[fixed + 2 * i + 1].wait()
        span = slice(i * depth, (i + 1) * depth)
        term = dot_nt(cot_ref[:, span], w_ref[:, span])
        total = term if total is None else total + term
    grad_ref[...] = total.astype(grad_ref.dtype)
    for copy in copies[1:fixed]:
        copy.wait()


def prepare(ring, index, cotangent, out_weight, heads, columns):
    width = out_weight.shape[1] // heads
    rows = (HD, HD, HD // 2) if ring else (HD,) * heads

    def body(*refs):
        prepare_kernel(ring, *refs)

    return pl.pallas_call(
        body,
        out_shape=(shape(BLK, HD), shape(8, columns, kind=F32))
        + tuple(shape(r, width) for r in rows),
        in_specs=[HBM] * 3,
        out_specs=(VMEM,) * (2 + len(rows)),
        scratch_shapes=[
            pltpu.SMEM(index.shape, jnp.int32),
            pltpu.VMEM(cotangent.shape, BF16),
            pltpu.VMEM(out_weight.shape, BF16),
            pltpu.SemaphoreType.DMA((1 + len(rows) + 2 * CHUNKS,)),
        ],
        compiler_params=FULL,
        name="prepare",
    )(index, cotangent, out_weight)


def attend_kernel(sides, mult_ref, q_ref, grad_ref, *refs):
    block_refs = refs[:3 + sides]
    att_ref, dq_ref = refs[3 + sides:5 + sides]
    sum_refs = refs[5 + sides:8 + 2 * sides]
    keys_ref = refs[-1]
    total_rows = keys_ref.shape[0]
    spans = []
    row = 0
    for ref in block_refs:
        spans.append((row, row + ref.shape[0]))
        keys_ref[row:row + ref.shape[0], :] = ref[...]
        row += ref.shape[0]
    if row < total_rows:
        keys_ref[row:, :] = jnp.zeros((total_rows - row, PAIR), BF16)
    keys = keys_ref[:, :HD]
    values = keys_ref[:, HD:]
    q = q_ref[...]
    grad = grad_ref[...]
    mult = mult_ref[0:1, :]

    scores = dot_nt(q, keys) + jnp.where(mult > 0.0, 0.0, ABSENT)
    top = jnp.max(scores, axis=1, keepdims=True)
    terms = jnp.exp2((scores - top) * (SCALE * LOG2E)) * mult
    probability = terms * (1.0 / jnp.sum(terms, axis=1, keepdims=True))
    weights = probability.astype(BF16)
    att_ref[...] = dot_nn(weights, values).astype(BF16)

    grad_weights = dot_nt(grad, values)
    delta = jnp.sum(probability * grad_weights, axis=1, keepdims=True)
    grad_scores = (probability * (grad_weights - delta) * SCALE).astype(BF16)
    dq_ref[...] = dot_nn(grad_scores, keys).astype(BF16)
    key_terms = dot_tn(grad_scores, q)
    value_terms = dot_tn(weights, grad)
    for (start, end), ref in zip(spans, sum_refs):
        ref[:, :HD] = key_terms[start:end].astype(ref.dtype)
        ref[:, HD:] = value_terms[start:end].astype(ref.dtype)


def attend(mult, q, grad, window, sides):
    def body(*refs):
        attend_kernel(len(sides), *refs)

    return pl.pallas_call(
        body,
        out_shape=(shape(BLK, HD), shape(BLK, HD))
        + (shape(BLK, PAIR, kind=F32),) * 3
        + tuple(shape(*s.shape) for s in sides),
        in_specs=[VMEM] * (6 + len(sides)),
        out_specs=(VMEM,) * (5 + len(sides)),
        scratch_shapes=[pltpu.VMEM((mult.shape[1], PAIR), BF16)],
        compiler_params=PARAMS,
        name="attend",
    )(mult, q, grad, *window, *sides)


def combine_kernel(own_ref, first_ref, second_ref, plus_ref, minus_ref,
                   mine_ref, whole_ref, half_ref, other_whole_ref, other_half_ref,
                   own_out, first_out, second_out, w_out):
    plus = plus_ref[...].astype(F32)
    minus = minus_ref[...].astype(F32)
    n = STRIDE_ROWS
    own_out[n:] = own_ref[n:]
    own_out[:n] = own_ref[:n] + plus[:n] + minus[:n]
    first_out[n:] = first_ref[n:].astype(BF16)
    first_out[:n] = (first_ref[:n] + plus[n:2 * n]).astype(BF16)
    second_out[n:] = second_ref[n:].astype(BF16)
    second_out[:n] = (second_ref[:n] + plus[2 * n:] + minus[n:]).astype(BF16)
    core = lax.axis_index("seq") & 1
    half = HD // 2
    w_out[:HD] = mine_ref[...]
    w_out[pl.ds(pl.multiple_of(HD + core * HD, HD), HD)] = whole_ref[...]
    w_out[pl.ds(pl.multiple_of(2 * HD - core * HD, HD), HD)] = other_whole_ref[...]
    w_out[pl.ds(pl.multiple_of(3 * HD + core * half, half), half)] = half_ref[...]
    w_out[pl.ds(pl.multiple_of(3 * HD + half - core * half, half), half)] = other_half_ref[...]


def combine(own, first, second, plus, minus, *slices):
    return pl.pallas_call(
        combine_kernel,
        out_shape=(shape(BLK, PAIR, kind=F32), shape(BLK, PAIR), shape(BLK, PAIR),
                   shape(4 * HD, slices[0].shape[1])),
        in_specs=[VMEM] * 10,
        out_specs=(VMEM,) * 4,
        compiler_params=PARAMS,
        name="combine",
    )(own, first, second, plus, minus, *slices)


def finish_kernel(heads, slices, extra, *refs):
    att_refs = refs[:heads]
    w_refs = refs[heads:heads + slices]
    rest = refs[heads + slices:]
    own_ref, first_ref, second_ref = rest[:3]
    mixed_ref, dk_ref, dv_ref = rest[-3:]
    pieces = [ref[r:r + HD] for ref in w_refs for r in range(0, ref.shape[0], HD)]
    mixed = None
    for ref, w in zip(att_refs, pieces):
        term = dot_nn(ref[...], w)
        mixed = term if mixed is None else mixed + term
    mixed_ref[...] = mixed.astype(mixed_ref.dtype)
    total = own_ref[...] + first_ref[...].astype(F32) + second_ref[...].astype(F32)
    lead = total[:STRIDE_ROWS]
    if extra:
        side_ref = rest[3]
        for i in range(side_ref.shape[0] // STRIDE_ROWS):
            lead = lead + side_ref[i * STRIDE_ROWS:(i + 1) * STRIDE_ROWS].astype(F32)
    for ref, c in ((dk_ref, 0), (dv_ref, HD)):
        ref[:STRIDE_ROWS] = lead[:, c:c + HD].astype(ref.dtype)
        ref[STRIDE_ROWS:] = total[STRIDE_ROWS:, c:c + HD].astype(ref.dtype)


def finish(attentions, slices, own, first, second, *side):
    width = slices[0].shape[1]

    def body(*refs):
        finish_kernel(len(attentions), len(slices), len(side), *refs)

    return pl.pallas_call(
        body,
        out_shape=(shape(BLK, width), shape(BLK, HD), shape(BLK, HD)),
        in_specs=[VMEM] * (len(attentions) + len(slices) + 3 + len(side)),
        out_specs=(VMEM,) * 3,
        compiler_params=PARAMS,
        name="finish",
    )(*attentions, *slices, own, first, second, *side)


def spread_slice(array):
    seq = lax.axis_size("seq")
    heads = lax.axis_size("head")
    pairs = [(b * heads + h, b * heads + (h ^ (1 + b % 2))) for b in range(seq)
             for h in range(heads)]
    return lax.ppermute(array, ("seq", "head"), pairs)


def shards(queries, key_rows, value_rows, out_weight, strided_index, cotangent):
    seq = lax.axis_size("seq")
    heads = lax.axis_size("head")
    ring = seq == 8 and heads == 4
    n = STRIDE_ROWS
    own = jnp.concatenate([key_rows, value_rows], axis=1)
    first = trade(own, 1)
    second = trade(own, -1)
    columns = 3 * BLK + (2 * BLK if ring else seq * n)
    grad, mult, *slices = prepare(ring, strided_index, cotangent, out_weight, heads, columns)
    if ring:
        mine, whole, half = slices
        whole = spread_slice(whole)
        half = swap(half, 3)
        lead = jnp.concatenate([own[:n], first[:n], second[:n]], axis=0)
        plus = trade(lead, 3)
        minus = trade(jnp.concatenate([own[:n], second[:n]], axis=0), -3)
        other_whole = trade(whole, 1)
        other_half = trade(half, 1)
        att, dq, own_sum, first_sum, second_sum, to_plus, to_minus = attend(
            mult, queries, grad, (own, first, second), (plus, minus)
        )
        attentions = [att] + [swap(att, r) for r in range(1, heads)]
        own_sum, to_first, to_second, weight = combine(
            own_sum, first_sum, second_sum, trade(to_plus, 3), trade(to_minus, -3),
            mine, whole, half, other_whole, other_half,
        )
        mixed, dk, dv = finish(
            attentions, [weight], own_sum, trade(to_first, 1), trade(to_second, -1)
        )
    else:
        slices = [slices[0]] + [swap(slices[r], r) for r in range(1, heads)]
        spread = jnp.broadcast_to(own[None, :n], (seq, n, PAIR))
        side = lax.all_to_all(spread, "seq", 0, 0).reshape(seq * n, PAIR)
        att, dq, own_sum, first_sum, second_sum, to_side = attend(
            mult, queries, grad, (own, first, second), (side,)
        )
        from_side = lax.all_to_all(to_side.reshape(seq, n, PAIR), "seq", 0, 0)
        mixed, dk, dv = finish(
            [att] + [swap(att, r) for r in range(1, heads)], slices, own_sum,
            trade(first_sum.astype(BF16), 1), trade(second_sum.astype(BF16), -1),
            from_side.reshape(seq * n, PAIR),
        )
    return (mixed, dq, dk, dv)


def solution(mesh):
    in_specs = (
        P("seq", "head"),
        P("seq", "head"),
        P("seq", "head"),
        P("head", None),
        P("seq", None),
        P("seq", None),
    )
    out_specs = (P("seq", "head"), P("seq", "head"), P("seq", "head"), P("seq", "head"))
    return jax.shard_map(shards, mesh=mesh, in_specs=in_specs, out_specs=out_specs, check_vma=False)
```

```python
import jax
import jax.numpy as jnp
from jax import lax
from jax.experimental import pallas as pl
from jax.experimental.pallas import tpu as pltpu
from jax.sharding import PartitionSpec as P

HD = 128
BLK = 128
STRIDE_ROWS = 32
PAIR = 2 * HD
SCALE = HD ** (-0.5)
LOG2E = 1.4426950408889634
ABSENT = -1e30
VMEM = pl.BlockSpec(memory_space=pltpu.VMEM)
HBM = pl.BlockSpec(memory_space=pltpu.HBM)
PARAMS = pltpu.CompilerParams(vmem_limit_bytes=40 * 1024 * 1024)
FULL = pltpu.CompilerParams(vmem_limit_bytes=int(53.3 * 1024 * 1024))
BF16 = jnp.bfloat16
PREPARE_COST = 10**10
ATTEND_COST = 10**9
COLLECT_COST = 10**10
F32 = jnp.float32


def dot_nt(a, b):
    return lax.dot_general(a, b, (((1,), (1,)), ((), ())), preferred_element_type=F32)


def dot_nn(a, b):
    return lax.dot_general(a, b, (((1,), (0,)), ((), ())), preferred_element_type=F32)


def dot_tn(a, b):
    return lax.dot_general(a, b, (((0,), (0,)), ((), ())), preferred_element_type=F32)


def shape(*dims, kind=BF16):
    return jax.ShapeDtypeStruct(dims, kind)


def trade(array, step):
    count = lax.axis_size("seq")
    return lax.ppermute(
        array, "seq", [(i, (i + (step if i % 2 == 0 else -step)) % count) for i in range(count)]
    )


def swap(array, mask):
    count = lax.axis_size("head")
    return lax.ppermute(array, "head", [(i, i ^ mask) for i in range(count)])


def count_of(picks, group):
    total = jnp.int32(0)
    for pick in picks:
        total = total + jnp.where(pick == group, 1, 0)
    return total.astype(F32)


def fill_multiplicity(ring, index_ref, mult_ref):
    per_block = BLK // STRIDE_ROWS
    picks = [index_ref[0, i] for i in range(index_ref.shape[1])]
    shape_of = mult_ref.shape
    lane = lax.broadcasted_iota(jnp.int32, shape_of, 1)
    mult = jnp.where(lane < 3 * BLK, 1.0, 0.0)
    if ring:
        b = lax.axis_index("seq")
        sign = 1 - 2 * (b & 1)
        counts = [count_of(picks, j) for j in range(2)]
        offsets = [(0, 0), (BLK, 1), (2 * BLK, -1), (3 * BLK, 3), (3 * BLK + 32, 2),
                   (3 * BLK + 64, 4), (3 * BLK + 96, -3), (3 * BLK + 128, -2)]
        for start, offset in offsets:
            owner = (b + 16 + sign * offset) & 7
            count = jnp.where(owner < per_block, counts[0], counts[1])
            inside = (lane >= start) & (lane < start + STRIDE_ROWS)
            mult = mult + jnp.where(inside, count, 0.0)
    else:
        for j in range((shape_of[1] - 3 * BLK) // BLK):
            start = (3 + j) * BLK
            inside = (lane >= start) & (lane < start + BLK)
            mult = mult + jnp.where(inside, count_of(picks, j), 0.0)
    mult_ref[...] = mult


def cost(flops):
    return pl.CostEstimate(flops=flops, bytes_accessed=0, transcendentals=0)


def slices_kernel(ring, w_hbm, *refs):
    slice_refs = refs[:-1]
    sems = refs[-1]
    width = slice_refs[0].shape[1]
    head = lax.axis_index("head")
    core = lax.axis_index("seq") & 1

    def columns(h):
        return pl.ds(pl.multiple_of(h * width, width), width)

    if ring:
        half = HD // 2
        sources = [
            w_hbm.at[:, columns(head)],
            w_hbm.at[:, columns(head ^ (1 + core))],
            w_hbm.at[pl.ds(pl.multiple_of(core * half, half), half), columns(head ^ 3)],
        ]
    else:
        sources = [w_hbm.at[:, columns(head ^ r)] for r in range(len(slice_refs))]
    copies = [pltpu.make_async_copy(src, dst, sems.at[i])
              for i, (src, dst) in enumerate(zip(sources, slice_refs))]
    for copy in copies:
        copy.start()
    for copy in copies:
        copy.wait()


def weight_slices(ring, out_weight, heads):
    width = out_weight.shape[1] // heads
    rows = (HD, HD, HD // 2) if ring else (HD,) * heads

    def body(*refs):
        slices_kernel(ring, *refs)

    return pl.pallas_call(
        body,
        out_shape=tuple(shape(r, width) for r in rows),
        in_specs=[HBM],
        out_specs=(VMEM,) * len(rows),
        scratch_shapes=[pltpu.SemaphoreType.DMA((len(rows),))],
        compiler_params=FULL,
        name="slices",
    )(out_weight)


CHUNKS = 4


def prepare_kernel(ring, index_hbm, cot_hbm, w_hbm, after_ref, grad_ref, mult_ref,
                   index_ref, cot_ref, w_ref, sems):
    del after_ref
    copies = [(index_hbm, index_ref)]
    depth = cot_ref.shape[1] // CHUNKS
    for i in range(CHUNKS):
        span = pl.ds(i * depth, depth)
        copies.append((cot_hbm.at[:, span], cot_ref.at[:, span]))
        copies.append((w_hbm.at[:, span], w_ref.at[:, span]))
    copies = [pltpu.make_async_copy(src, dst, sems.at[i]) for i, (src, dst) in enumerate(copies)]
    for copy in copies:
        copy.start()
    copies[0].wait()
    fill_multiplicity(ring, index_ref, mult_ref)
    total = None
    for i in range(CHUNKS):
        copies[1 + 2 * i].wait()
        copies[2 + 2 * i].wait()
        span = slice(i * depth, (i + 1) * depth)
        term = dot_nt(cot_ref[:, span], w_ref[:, span])
        total = term if total is None else total + term
    grad_ref[...] = total.astype(grad_ref.dtype)


def prepare(ring, index, cotangent, out_weight, columns, after):
    def body(*refs):
        prepare_kernel(ring, *refs)

    return pl.pallas_call(
        body,
        out_shape=(shape(BLK, HD), shape(8, columns, kind=F32)),
        in_specs=[HBM] * 3 + [VMEM],
        out_specs=(VMEM,) * 2,
        scratch_shapes=[
            pltpu.SMEM(index.shape, jnp.int32),
            pltpu.VMEM(cotangent.shape, BF16),
            pltpu.VMEM(out_weight.shape, BF16),
            pltpu.SemaphoreType.DMA((1 + 2 * CHUNKS,)),
        ],
        compiler_params=FULL,
        cost_estimate=cost(PREPARE_COST),
        name="prepare",
    )(index, cotangent, out_weight, after)


def lead_kernel(own_ref, first_ref, second_ref, plus_ref, minus_ref):
    n = STRIDE_ROWS
    plus_ref[:n] = own_ref[:n]
    plus_ref[n:2 * n] = first_ref[:n]
    plus_ref[2 * n:] = second_ref[:n]
    minus_ref[:n] = own_ref[:n]
    minus_ref[n:] = second_ref[:n]


def leads(own, first, second):
    n = STRIDE_ROWS
    return pl.pallas_call(
        lead_kernel,
        out_shape=(shape(3 * n, PAIR), shape(2 * n, PAIR)),
        in_specs=[VMEM] * 3,
        out_specs=(VMEM,) * 2,
        compiler_params=PARAMS,
        name="leads",
    )(own, first, second)


def attend_kernel(sides, mult_ref, q_ref, grad_ref, *refs):
    block_refs = refs[:3 + sides]
    att_ref, dq_ref = refs[3 + sides:5 + sides]
    sum_refs = refs[5 + sides:9 + sides]
    keys_ref = refs[-1]
    total_rows = keys_ref.shape[0]
    spans = []
    row = 0
    for ref in block_refs:
        spans.append((row, row + ref.shape[0]))
        keys_ref[row:row + ref.shape[0], :] = ref[...]
        row += ref.shape[0]
    if row < total_rows:
        keys_ref[row:, :] = jnp.zeros((total_rows - row, PAIR), BF16)
    keys = keys_ref[:, :HD]
    values = keys_ref[:, HD:]
    q = q_ref[...]
    grad = grad_ref[...]
    mult = mult_ref[0:1, :]

    scores = dot_nt(q, keys) + jnp.where(mult > 0.0, 0.0, ABSENT)
    top = jnp.max(scores, axis=1, keepdims=True)
    terms = jnp.exp2((scores - top) * (SCALE * LOG2E)) * mult
    probability = terms * (1.0 / jnp.sum(terms, axis=1, keepdims=True))
    weights = probability.astype(BF16)
    att_ref[...] = dot_nn(weights, values).astype(BF16)

    grad_weights = dot_nt(grad, values)
    delta = jnp.sum(probability * grad_weights, axis=1, keepdims=True)
    grad_scores = (probability * (grad_weights - delta) * SCALE).astype(BF16)
    dq_ref[...] = dot_nn(grad_scores, keys).astype(BF16)
    key_terms = dot_tn(grad_scores, q)
    value_terms = dot_tn(weights, grad)
    for (start, end), ref in zip(spans, sum_refs[:3]):
        ref[:, :HD] = key_terms[start:end].astype(ref.dtype)
        ref[:, HD:] = value_terms[start:end].astype(ref.dtype)
    side_ref = sum_refs[3]
    if sides == 1:
        side_ref[:, :HD] = key_terms[3 * BLK:].astype(BF16)
        side_ref[:, HD:] = value_terms[3 * BLK:].astype(BF16)
    else:
        b = lax.axis_index("seq")
        sign = 1 - 2 * (b & 1)
        side_ref[...] = jnp.zeros(side_ref.shape, BF16)
        for i, offset in enumerate((3, 2, 4, -3, -2)):
            owner = (b + 16 + sign * offset) & 7
            start = 3 * BLK + i * STRIDE_ROWS
            rows = pl.ds(pl.multiple_of(owner * STRIDE_ROWS, STRIDE_ROWS), STRIDE_ROWS)
            side_ref[rows, :HD] = key_terms[start:start + STRIDE_ROWS].astype(BF16)
            side_ref[rows, HD:] = value_terms[start:start + STRIDE_ROWS].astype(BF16)


def attend(mult, q, grad, window, sides, side_rows):
    def body(*refs):
        attend_kernel(len(sides), *refs)

    return pl.pallas_call(
        body,
        out_shape=(shape(BLK, HD), shape(BLK, HD), shape(BLK, PAIR, kind=F32),
                   shape(BLK, PAIR), shape(BLK, PAIR), shape(side_rows, PAIR)),
        in_specs=[VMEM] * (6 + len(sides)),
        out_specs=(VMEM,) * 6,
        scratch_shapes=[pltpu.VMEM((mult.shape[1], PAIR), BF16)],
        compiler_params=PARAMS,
        cost_estimate=cost(ATTEND_COST),
        name="attend",
    )(mult, q, grad, *window, *sides)


def join_kernel(whole_ref, half_ref, after_ref, out_ref):
    del after_ref
    out_ref[:HD] = whole_ref[...]
    out_ref[HD:] = half_ref[...]


def join(whole, half, after):
    return pl.pallas_call(
        join_kernel,
        out_shape=shape(HD + HD // 2, whole.shape[1]),
        in_specs=[VMEM] * 3,
        out_specs=VMEM,
        compiler_params=PARAMS,
        name="join",
    )(whole, half, after)


def collect_kernel(mine_ref, here_ref, there_ref, own_ref, first_ref, second_ref, *refs):
    att_refs = refs[:-3]
    att_out, w_out, sum_out = refs[-3:]
    for r, ref in enumerate(att_refs):
        att_out[:, r * HD:(r + 1) * HD] = ref[...]
    core = lax.axis_index("seq") & 1
    half = HD // 2
    w_out[:HD] = mine_ref[...]
    w_out[pl.ds(pl.multiple_of(HD + core * HD, HD), HD)] = here_ref[:HD]
    w_out[pl.ds(pl.multiple_of(2 * HD - core * HD, HD), HD)] = there_ref[:HD]
    w_out[pl.ds(pl.multiple_of(3 * HD + core * half, half), half)] = here_ref[HD:]
    w_out[pl.ds(pl.multiple_of(3 * HD + half - core * half, half), half)] = there_ref[HD:]
    sum_out[...] = own_ref[...] + first_ref[...].astype(F32) + second_ref[...].astype(F32)


def collect(mine, here, there, own, first, second, attentions):
    return pl.pallas_call(
        collect_kernel,
        out_shape=(shape(BLK, 4 * HD), shape(4 * HD, mine.shape[1]), shape(BLK, PAIR, kind=F32)),
        in_specs=[VMEM] * (6 + len(attentions)),
        out_specs=(VMEM,) * 3,
        compiler_params=PARAMS,
        cost_estimate=cost(COLLECT_COST),
        name="collect",
    )(mine, here, there, own, first, second, *attentions)


def finish_kernel(count, *refs):
    att_refs = refs[:count]
    w_refs = refs[count:2 * count]
    sum_refs = refs[2 * count:-4]
    side_ref, mixed_ref, dk_ref, dv_ref = refs[-4:]
    mixed = None
    for ref, w in zip(att_refs, w_refs):
        term = dot_nn(ref[...], w[...])
        mixed = term if mixed is None else mixed + term
    mixed_ref[...] = mixed.astype(mixed_ref.dtype)
    total = sum_refs[0][...]
    for ref in sum_refs[1:]:
        total = total + ref[...].astype(F32)
    lead = total[:STRIDE_ROWS]
    for i in range(side_ref.shape[0] // STRIDE_ROWS):
        lead = lead + side_ref[i * STRIDE_ROWS:(i + 1) * STRIDE_ROWS].astype(F32)
    for ref, c in ((dk_ref, 0), (dv_ref, HD)):
        ref[:STRIDE_ROWS] = lead[:, c:c + HD].astype(ref.dtype)
        ref[STRIDE_ROWS:] = total[STRIDE_ROWS:, c:c + HD].astype(ref.dtype)


def finish(attentions, slices, sums, side):
    width = slices[0].shape[1]
    count = len(attentions)

    def body(*refs):
        finish_kernel(count, *refs)

    return pl.pallas_call(
        body,
        out_shape=(shape(BLK, width), shape(BLK, HD), shape(BLK, HD)),
        in_specs=[VMEM] * (2 * count + len(sums) + 1),
        out_specs=(VMEM,) * 3,
        compiler_params=PARAMS,
        name="finish",
    )(*attentions, *slices, *sums, side)


def spread_slice(array):
    seq = lax.axis_size("seq")
    heads = lax.axis_size("head")
    pairs = [(b * heads + h, b * heads + (h ^ (1 + b % 2))) for b in range(seq)
             for h in range(heads)]
    return lax.ppermute(array, ("seq", "head"), pairs)


def shards(queries, key_rows, value_rows, out_weight, strided_index, cotangent):
    seq = lax.axis_size("seq")
    heads = lax.axis_size("head")
    ring = seq == 8 and heads == 4
    n = STRIDE_ROWS
    side_rows = seq * n
    columns = 3 * BLK + side_rows
    own = jnp.concatenate([key_rows, value_rows], axis=1)
    first = trade(own, 1)
    second = trade(own, -1)
    slices = weight_slices(ring, out_weight, heads)
    if ring:
        mine, whole, half = slices
        whole = spread_slice(whole)
        half = swap(half, 3)
        plus, minus = leads(own, first, second)
        grad, mult = prepare(ring, strided_index, cotangent, out_weight, columns, minus)
        sides = (trade(plus, 3), trade(minus, -3))
    else:
        slices = [slices[0]] + [swap(slices[r], r) for r in range(1, heads)]
        grad, mult = prepare(ring, strided_index, cotangent, out_weight, columns, own)
        spread = jnp.broadcast_to(own[None, :n], (seq, n, PAIR))
        sides = (lax.all_to_all(spread, "seq", 0, 0).reshape(side_rows, PAIR),)
    att, dq, own_sum, to_first, to_second, to_side = attend(
        mult, queries, grad, (own, first, second), sides, side_rows
    )
    attentions = [att] + [swap(att, r) for r in range(1, heads)]
    sums = (own_sum, trade(to_first, 1), trade(to_second, -1))
    from_side = lax.all_to_all(to_side.reshape(seq, n, PAIR), "seq", 0, 0)
    from_side = from_side.reshape(side_rows, PAIR)
    if ring:
        here = join(whole, half, att)
        gathered, weight, total = collect(mine, here, trade(here, 1), *sums, attentions)
        mixed, dk, dv = finish([gathered], [weight], [total], from_side)
    else:
        mixed, dk, dv = finish(attentions, slices, sums, from_side)
    return (mixed, dq, dk, dv)


def solution(mesh):
    in_specs = (
        P("seq", "head"),
        P("seq", "head"),
        P("seq", "head"),
        P("head", None),
        P("seq", None),
        P("seq", None),
    )
    out_specs = (P("seq", "head"), P("seq", "head"), P("seq", "head"), P("seq", "head"))
    return jax.shard_map(shards, mesh=mesh, in_specs=in_specs, out_specs=out_specs, check_vma=False)
```

```python
import jax
import jax.numpy as jnp
from jax import lax
from jax.experimental import pallas as pl
from jax.experimental.pallas import tpu as pltpu
from jax.sharding import PartitionSpec as P

HD = 128
BLK = 128
STRIDE_ROWS = 32
PAIR = 2 * HD
SCALE = HD ** (-0.5)
LOG2E = 1.4426950408889634
ABSENT = -1e30
VMEM = pl.BlockSpec(memory_space=pltpu.VMEM)
HBM = pl.BlockSpec(memory_space=pltpu.HBM)
PARAMS = pltpu.CompilerParams(vmem_limit_bytes=40 * 1024 * 1024)
FULL = pltpu.CompilerParams(vmem_limit_bytes=int(53.3 * 1024 * 1024))
BF16 = jnp.bfloat16
PREPARE_COST = 10**10
ATTEND_COST = 10**9
COMBINE_COST = 10**10
GATHER_COST = 10**10
F32 = jnp.float32


def dot_nt(a, b):
    return lax.dot_general(a, b, (((1,), (1,)), ((), ())), preferred_element_type=F32)


def dot_nn(a, b):
    return lax.dot_general(a, b, (((1,), (0,)), ((), ())), preferred_element_type=F32)


def dot_tn(a, b):
    return lax.dot_general(a, b, (((0,), (0,)), ((), ())), preferred_element_type=F32)


def shape(*dims, kind=BF16):
    return jax.ShapeDtypeStruct(dims, kind)


def trade(array, step):
    count = lax.axis_size("seq")
    return lax.ppermute(
        array, "seq", [(i, (i + (step if i % 2 == 0 else -step)) % count) for i in range(count)]
    )


def swap(array, mask):
    count = lax.axis_size("head")
    return lax.ppermute(array, "head", [(i, i ^ mask) for i in range(count)])


def count_of(picks, group):
    total = jnp.int32(0)
    for pick in picks:
        total = total + jnp.where(pick == group, 1, 0)
    return total.astype(F32)


def fill_multiplicity(ring, index_ref, mult_ref):
    per_block = BLK // STRIDE_ROWS
    picks = [index_ref[0, i] for i in range(index_ref.shape[1])]
    shape_of = mult_ref.shape
    lane = lax.broadcasted_iota(jnp.int32, shape_of, 1)
    mult = jnp.where(lane < 3 * BLK, 1.0, 0.0)
    if ring:
        b = lax.axis_index("seq")
        sign = 1 - 2 * (b & 1)
        counts = [count_of(picks, j) for j in range(2)]
        offsets = [(0, 0), (BLK, 1), (2 * BLK, -1), (3 * BLK, 3), (3 * BLK + 32, 2),
                   (3 * BLK + 64, 4), (3 * BLK + 96, -3), (3 * BLK + 128, -2)]
        for start, offset in offsets:
            owner = (b + 16 + sign * offset) & 7
            count = jnp.where(owner < per_block, counts[0], counts[1])
            inside = (lane >= start) & (lane < start + STRIDE_ROWS)
            mult = mult + jnp.where(inside, count, 0.0)
    else:
        for j in range((shape_of[1] - 3 * BLK) // BLK):
            start = (3 + j) * BLK
            inside = (lane >= start) & (lane < start + BLK)
            mult = mult + jnp.where(inside, count_of(picks, j), 0.0)
    mult_ref[...] = mult


def cost(flops):
    return pl.CostEstimate(flops=flops, bytes_accessed=0, transcendentals=0)


CHUNKS = 4


def prepare_kernel(ring, index_hbm, cot_hbm, w_hbm, after_ref, grad_ref, mult_ref, *refs):
    del after_ref
    index_ref, cot_ref, w_ref, sems = refs[-4:]
    slice_refs = refs[:-4]
    copies = [(index_hbm, index_ref)]
    depth = cot_ref.shape[1] // CHUNKS
    for i in range(CHUNKS):
        span = pl.ds(i * depth, depth)
        copies.append((w_hbm.at[:, span], w_ref.at[:, span]))
        copies.append((cot_hbm.at[:, span], cot_ref.at[:, span]))
    copies = [pltpu.make_async_copy(src, dst, sems.at[i]) for i, (src, dst) in enumerate(copies)]
    for copy in copies:
        copy.start()
    copies[0].wait()
    fill_multiplicity(ring, index_ref, mult_ref)
    total = None
    for i in range(CHUNKS):
        copies[1 + 2 * i].wait()
        copies[2 + 2 * i].wait()
        span = slice(i * depth, (i + 1) * depth)
        term = dot_nt(cot_ref[:, span], w_ref[:, span])
        total = term if total is None else total + term
    grad_ref[...] = total.astype(grad_ref.dtype)

    width = slice_refs[0].shape[1]
    head = lax.axis_index("head")

    def columns(h):
        return pl.ds(pl.multiple_of(h * width, width), width)

    if ring:
        core = lax.axis_index("seq") & 1
        half = HD // 2
        mine_ref, whole_ref, half_ref = slice_refs
        mine_ref[...] = w_ref[:, columns(head)]
        whole_ref[...] = w_ref[:, columns(head ^ (1 + core))]
        rows = pl.ds(pl.multiple_of(core * half, half), half)
        half_ref[...] = w_ref[rows, columns(head ^ 3)]
    else:
        for r, ref in enumerate(slice_refs):
            ref[...] = w_ref[:, columns(head ^ r)]


def prepare(ring, index, cotangent, out_weight, heads, columns, after):
    width = out_weight.shape[1] // heads
    rows = (HD, HD, HD // 2) if ring else (HD,) * heads

    def body(*refs):
        prepare_kernel(ring, *refs)

    return pl.pallas_call(
        body,
        out_shape=(shape(BLK, HD), shape(8, columns, kind=F32))
        + tuple(shape(r, width) for r in rows),
        in_specs=[HBM] * 3 + [VMEM],
        out_specs=(VMEM,) * (2 + len(rows)),
        scratch_shapes=[
            pltpu.SMEM(index.shape, jnp.int32),
            pltpu.VMEM(cotangent.shape, BF16),
            pltpu.VMEM(out_weight.shape, BF16),
            pltpu.SemaphoreType.DMA((1 + 2 * CHUNKS,)),
        ],
        compiler_params=FULL,
        cost_estimate=cost(PREPARE_COST),
        name="prepare",
    )(index, cotangent, out_weight, after)


def lead_kernel(own_ref, first_ref, second_ref, mult_ref, whole_ref,
                plus_ref, minus_ref, whole_out):
    del mult_ref
    n = STRIDE_ROWS
    plus_ref[:n] = own_ref[:n]
    plus_ref[n:2 * n] = first_ref[:n]
    plus_ref[2 * n:] = second_ref[:n]
    minus_ref[:n] = own_ref[:n]
    minus_ref[n:] = second_ref[:n]
    whole_out[...] = whole_ref[...]


def leads(own, first, second, mult, whole):
    n = STRIDE_ROWS
    return pl.pallas_call(
        lead_kernel,
        out_shape=(shape(3 * n, PAIR), shape(2 * n, PAIR), shape(*whole.shape)),
        in_specs=[VMEM] * 5,
        out_specs=(VMEM,) * 3,
        compiler_params=PARAMS,
        name="leads",
    )(own, first, second, mult, whole)


def attend_kernel(sides, mult_ref, q_ref, grad_ref, *refs):
    block_refs = refs[:3 + sides]
    att_ref, dq_ref = refs[3 + sides:5 + sides]
    sum_refs = refs[5 + sides:8 + 2 * sides]
    keys_ref = refs[-1]
    total_rows = keys_ref.shape[0]
    spans = []
    row = 0
    for ref in block_refs:
        spans.append((row, row + ref.shape[0]))
        keys_ref[row:row + ref.shape[0], :] = ref[...]
        row += ref.shape[0]
    if row < total_rows:
        keys_ref[row:, :] = jnp.zeros((total_rows - row, PAIR), BF16)
    keys = keys_ref[:, :HD]
    values = keys_ref[:, HD:]
    q = q_ref[...]
    grad = grad_ref[...]
    mult = mult_ref[0:1, :]

    scores = dot_nt(q, keys) + jnp.where(mult > 0.0, 0.0, ABSENT)
    top = jnp.max(scores, axis=1, keepdims=True)
    terms = jnp.exp2((scores - top) * (SCALE * LOG2E)) * mult
    probability = terms * (1.0 / jnp.sum(terms, axis=1, keepdims=True))
    weights = probability.astype(BF16)
    att_ref[...] = dot_nn(weights, values).astype(BF16)

    grad_weights = dot_nt(grad, values)
    delta = jnp.sum(probability * grad_weights, axis=1, keepdims=True)
    grad_scores = (probability * (grad_weights - delta) * SCALE).astype(BF16)
    dq_ref[...] = dot_nn(grad_scores, keys).astype(BF16)
    key_terms = dot_tn(grad_scores, q)
    value_terms = dot_tn(weights, grad)
    for (start, end), ref in zip(spans, sum_refs):
        ref[:, :HD] = key_terms[start:end].astype(ref.dtype)
        ref[:, HD:] = value_terms[start:end].astype(ref.dtype)


def attend(mult, q, grad, window, sides):
    def body(*refs):
        attend_kernel(len(sides), *refs)

    return pl.pallas_call(
        body,
        out_shape=(shape(BLK, HD), shape(BLK, HD))
        + (shape(BLK, PAIR, kind=F32),) * 3
        + tuple(shape(*s.shape) for s in sides),
        in_specs=[VMEM] * (6 + len(sides)),
        out_specs=(VMEM,) * (5 + len(sides)),
        scratch_shapes=[pltpu.VMEM((mult.shape[1], PAIR), BF16)],
        compiler_params=PARAMS,
        cost_estimate=cost(ATTEND_COST),
        name="attend",
    )(mult, q, grad, *window, *sides)


def combine_kernel(own_ref, first_ref, second_ref, plus_ref, minus_ref, whole_ref, half_ref,
                   own_out, first_out, second_out):
    plus = plus_ref[...].astype(F32)
    minus = minus_ref[...].astype(F32)
    n = STRIDE_ROWS
    own_out[n:] = own_ref[n:]
    own_out[:n] = own_ref[:n] + plus[:n] + minus[:n]
    second_out[n:] = second_ref[n:].astype(BF16)
    second_out[:n] = (second_ref[:n] + plus[2 * n:] + minus[n:]).astype(BF16)
    first_out[n:BLK] = first_ref[n:].astype(BF16)
    first_out[:n] = (first_ref[:n] + plus[n:2 * n]).astype(BF16)
    row = BLK
    for ref in (whole_ref, half_ref):
        for c in range(0, ref.shape[1], PAIR):
            first_out[row:row + ref.shape[0]] = ref[:, c:c + PAIR]
            row += ref.shape[0]


def combine(own, first, second, plus, minus, whole, half):
    extra = (whole.size + half.size) // PAIR
    return pl.pallas_call(
        combine_kernel,
        out_shape=(shape(BLK, PAIR, kind=F32), shape(BLK + extra, PAIR), shape(BLK, PAIR)),
        in_specs=[VMEM] * 7,
        out_specs=(VMEM,) * 3,
        compiler_params=PARAMS,
        cost_estimate=cost(COMBINE_COST),
        name="combine",
    )(own, first, second, plus, minus, whole, half)


def gather_kernel(*refs):
    for r, ref in enumerate(refs[:-1]):
        refs[-1][:, r * HD:(r + 1) * HD] = ref[...]


def gather(attentions):
    return pl.pallas_call(
        gather_kernel,
        out_shape=shape(BLK, len(attentions) * HD),
        in_specs=[VMEM] * len(attentions),
        out_specs=VMEM,
        compiler_params=PARAMS,
        cost_estimate=cost(GATHER_COST),
        name="gather",
    )(*attentions)


def settle(total, lead, dk_ref, dv_ref):
    for ref, c in ((dk_ref, 0), (dv_ref, HD)):
        ref[:STRIDE_ROWS] = lead[:, c:c + HD].astype(ref.dtype)
        ref[STRIDE_ROWS:] = total[STRIDE_ROWS:, c:c + HD].astype(ref.dtype)


def finish_ring_kernel(att_ref, mine_ref, whole_ref, half_ref, first_ref, own_ref, second_ref,
                       mixed_ref, dk_ref, dv_ref):
    core = lax.axis_index("seq") & 1
    half = HD // 2
    att = [att_ref[:, r * HD:(r + 1) * HD] for r in range(4)]
    here = jnp.where(core == 0, att[1], att[2])
    there = jnp.where(core == 0, att[2], att[1])
    here_half = jnp.where(core == 0, att[3][:, :half], att[3][:, half:])
    there_half = jnp.where(core == 0, att[3][:, half:], att[3][:, :half])
    whole_row = BLK
    half_row = BLK + (mine_ref.shape[1] // PAIR) * HD
    for i, c in enumerate(range(0, mine_ref.shape[1], PAIR)):
        span = slice(c, c + PAIR)
        other_whole = first_ref[whole_row + i * HD:whole_row + (i + 1) * HD]
        other_half = first_ref[half_row + i * half:half_row + (i + 1) * half]
        mixed = dot_nn(att[0], mine_ref[:, span]) + dot_nn(here, whole_ref[:, span])
        mixed = mixed + dot_nn(there, other_whole) + dot_nn(here_half, half_ref[:, span])
        mixed = mixed + dot_nn(there_half, other_half)
        mixed_ref[:, span] = mixed.astype(mixed_ref.dtype)
    total = own_ref[...] + first_ref[:BLK].astype(F32) + second_ref[...].astype(F32)
    settle(total, total[:STRIDE_ROWS], dk_ref, dv_ref)


def finish_ring(att, mine, whole, half, first, own, second):
    return pl.pallas_call(
        finish_ring_kernel,
        out_shape=(shape(BLK, mine.shape[1]), shape(BLK, HD), shape(BLK, HD)),
        in_specs=[VMEM] * 7,
        out_specs=(VMEM,) * 3,
        compiler_params=PARAMS,
        name="finish",
    )(att, mine, whole, half, first, own, second)


def finish_kernel(count, *refs):
    att_refs = refs[:count]
    w_refs = refs[count:2 * count]
    own_ref, first_ref, second_ref, side_ref, mixed_ref, dk_ref, dv_ref = refs[2 * count:]
    mixed = None
    for ref, w in zip(att_refs, w_refs):
        term = dot_nn(ref[...], w[...])
        mixed = term if mixed is None else mixed + term
    mixed_ref[...] = mixed.astype(mixed_ref.dtype)
    total = own_ref[...] + first_ref[...].astype(F32) + second_ref[...].astype(F32)
    lead = total[:STRIDE_ROWS]
    for i in range(side_ref.shape[0] // STRIDE_ROWS):
        lead = lead + side_ref[i * STRIDE_ROWS:(i + 1) * STRIDE_ROWS].astype(F32)
    settle(total, lead, dk_ref, dv_ref)


def finish(attentions, slices, own, first, second, side):
    width = slices[0].shape[1]
    count = len(attentions)

    def body(*refs):
        finish_kernel(count, *refs)

    return pl.pallas_call(
        body,
        out_shape=(shape(BLK, width), shape(BLK, HD), shape(BLK, HD)),
        in_specs=[VMEM] * (2 * count + 4),
        out_specs=(VMEM,) * 3,
        compiler_params=PARAMS,
        name="finish",
    )(*attentions, *slices, own, first, second, side)


def spread_slice(array):
    seq = lax.axis_size("seq")
    heads = lax.axis_size("head")
    pairs = [(b * heads + h, b * heads + (h ^ (1 + b % 2))) for b in range(seq)
             for h in range(heads)]
    return lax.ppermute(array, ("seq", "head"), pairs)


def shards(queries, key_rows, value_rows, out_weight, strided_index, cotangent):
    seq = lax.axis_size("seq")
    heads = lax.axis_size("head")
    ring = seq == 8 and heads == 4
    n = STRIDE_ROWS
    side_rows = seq * n
    columns = 3 * BLK + side_rows
    own = jnp.concatenate([key_rows, value_rows], axis=1)
    first = trade(own, 1)
    second = trade(own, -1)
    grad, mult, *slices = prepare(
        ring, strided_index, cotangent, out_weight, heads, columns, own
    )
    if ring:
        mine, whole, half = slices
        half = swap(half, 3)
        plus, minus, whole = leads(own, first, second, mult, whole)
        whole = spread_slice(whole)
        att, dq, own_sum, first_sum, second_sum, to_plus, to_minus = attend(
            mult, queries, grad, (own, first, second), (trade(plus, 3), trade(minus, -3))
        )
        attentions = [att] + [swap(att, r) for r in range(1, heads)]
        own_sum, to_first, to_second = combine(
            own_sum, first_sum, second_sum, trade(to_plus, 3), trade(to_minus, -3), whole, half
        )
        mixed, dk, dv = finish_ring(
            gather(attentions), mine, whole, half, trade(to_first, 1), own_sum,
            trade(to_second, -1),
        )
    else:
        slices = [slices[0]] + [swap(slices[r], r) for r in range(1, heads)]
        spread = jnp.broadcast_to(own[None, :n], (seq, n, PAIR))
        side = lax.all_to_all(spread, "seq", 0, 0).reshape(side_rows, PAIR)
        att, dq, own_sum, first_sum, second_sum, to_side = attend(
            mult, queries, grad, (own, first, second), (side,)
        )
        from_side = lax.all_to_all(to_side.reshape(seq, n, PAIR), "seq", 0, 0)
        mixed, dk, dv = finish(
            [att] + [swap(att, r) for r in range(1, heads)], slices, own_sum,
            trade(first_sum.astype(BF16), 1), trade(second_sum.astype(BF16), -1),
            from_side.reshape(side_rows, PAIR),
        )
    return (mixed, dq, dk, dv)


def solution(mesh):
    in_specs = (
        P("seq", "head"),
        P("seq", "head"),
        P("seq", "head"),
        P("head", None),
        P("seq", None),
        P("seq", None),
    )
    out_specs = (P("seq", "head"), P("seq", "head"), P("seq", "head"), P("seq", "head"))
    return jax.shard_map(shards, mesh=mesh, in_specs=in_specs, out_specs=out_specs, check_vma=False)
```

```python
import jax
import jax.numpy as jnp
from jax import lax
from jax.experimental import pallas as pl
from jax.experimental.pallas import tpu as pltpu
from jax.sharding import PartitionSpec as P

HD = 128
BLK = 128
STRIDE_ROWS = 32
PAIR = 2 * HD
SCALE = HD ** (-0.5)
LOG2E = 1.4426950408889634
ABSENT = -1e30
VMEM = pl.BlockSpec(memory_space=pltpu.VMEM)
HBM = pl.BlockSpec(memory_space=pltpu.HBM)
PARAMS = pltpu.CompilerParams(vmem_limit_bytes=40 * 1024 * 1024)
FULL = pltpu.CompilerParams(vmem_limit_bytes=int(53.3 * 1024 * 1024))
BF16 = jnp.bfloat16
PREPARE_COST = 10**10
ATTEND_COST = 10**9
COMBINE_COST = 10**10
GATHER_COST = 10**10
F32 = jnp.float32


def dot_nt(a, b):
    return lax.dot_general(a, b, (((1,), (1,)), ((), ())), preferred_element_type=F32)


def dot_nn(a, b):
    return lax.dot_general(a, b, (((1,), (0,)), ((), ())), preferred_element_type=F32)


def dot_tn(a, b):
    return lax.dot_general(a, b, (((0,), (0,)), ((), ())), preferred_element_type=F32)


def shape(*dims, kind=BF16):
    return jax.ShapeDtypeStruct(dims, kind)


def trade(array, step):
    count = lax.axis_size("seq")
    return lax.ppermute(
        array, "seq", [(i, (i + (step if i % 2 == 0 else -step)) % count) for i in range(count)]
    )


def swap(array, mask):
    count = lax.axis_size("head")
    return lax.ppermute(array, "head", [(i, i ^ mask) for i in range(count)])


def count_of(picks, group):
    total = jnp.int32(0)
    for pick in picks:
        total = total + jnp.where(pick == group, 1, 0)
    return total.astype(F32)


def fill_multiplicity(ring, index_ref, mult_ref):
    per_block = BLK // STRIDE_ROWS
    picks = [index_ref[0, i] for i in range(index_ref.shape[1])]
    shape_of = mult_ref.shape
    lane = lax.broadcasted_iota(jnp.int32, shape_of, 1)
    mult = jnp.where(lane < 3 * BLK, 1.0, 0.0)
    if ring:
        b = lax.axis_index("seq")
        sign = 1 - 2 * (b & 1)
        counts = [count_of(picks, j) for j in range(2)]
        offsets = [(0, 0), (BLK, 1), (2 * BLK, -1), (3 * BLK, 3), (3 * BLK + 32, 2),
                   (3 * BLK + 64, 4), (3 * BLK + 96, -3), (3 * BLK + 128, -2)]
        for start, offset in offsets:
            owner = (b + 16 + sign * offset) & 7
            count = jnp.where(owner < per_block, counts[0], counts[1])
            inside = (lane >= start) & (lane < start + STRIDE_ROWS)
            mult = mult + jnp.where(inside, count, 0.0)
    else:
        for j in range((shape_of[1] - 3 * BLK) // BLK):
            start = (3 + j) * BLK
            inside = (lane >= start) & (lane < start + BLK)
            mult = mult + jnp.where(inside, count_of(picks, j), 0.0)
    mult_ref[...] = mult


def cost(flops):
    return pl.CostEstimate(flops=flops, bytes_accessed=0, transcendentals=0)


CHUNKS = 4


def prepare_kernel(ring, index_hbm, cot_hbm, w_hbm, after_ref, grad_ref, mult_ref, *refs):
    del after_ref
    index_ref, cot_ref, w_ref, sems = refs[-4:]
    slice_refs = refs[:-4]
    copies = [(index_hbm, index_ref)]
    depth = cot_ref.shape[1] // CHUNKS
    for i in range(CHUNKS):
        span = pl.ds(i * depth, depth)
        copies.append((w_hbm.at[:, span], w_ref.at[:, span]))
        copies.append((cot_hbm.at[:, span], cot_ref.at[:, span]))
    copies = [pltpu.make_async_copy(src, dst, sems.at[i]) for i, (src, dst) in enumerate(copies)]
    for copy in copies:
        copy.start()
    copies[0].wait()
    fill_multiplicity(ring, index_ref, mult_ref)
    total = None
    for i in range(CHUNKS):
        copies[1 + 2 * i].wait()
        copies[2 + 2 * i].wait()
        span = slice(i * depth, (i + 1) * depth)
        term = dot_nt(cot_ref[:, span], w_ref[:, span])
        total = term if total is None else total + term
    grad_ref[...] = total.astype(grad_ref.dtype)

    width = slice_refs[0].shape[1]
    head = lax.axis_index("head")

    def columns(h):
        return pl.ds(pl.multiple_of(h * width, width), width)

    if ring:
        core = lax.axis_index("seq") & 1
        half = HD // 2
        mine_ref, whole_ref, half_ref = slice_refs
        mine_ref[...] = w_ref[:, columns(head)]
        whole_ref[...] = w_ref[:, columns(head ^ (1 + core))]
        rows = pl.ds(pl.multiple_of(core * half, half), half)
        half_ref[...] = w_ref[rows, columns(head ^ 3)]
    else:
        for r, ref in enumerate(slice_refs):
            ref[...] = w_ref[:, columns(head ^ r)]


def prepare(ring, index, cotangent, out_weight, heads, columns, after):
    width = out_weight.shape[1] // heads
    rows = (HD, HD, HD // 2) if ring else (HD,) * heads

    def body(*refs):
        prepare_kernel(ring, *refs)

    return pl.pallas_call(
        body,
        out_shape=(shape(BLK, HD), shape(8, columns, kind=F32))
        + tuple(shape(r, width) for r in rows),
        in_specs=[HBM] * 3 + [VMEM],
        out_specs=(VMEM,) * (2 + len(rows)),
        scratch_shapes=[
            pltpu.SMEM(index.shape, jnp.int32),
            pltpu.VMEM(cotangent.shape, BF16),
            pltpu.VMEM(out_weight.shape, BF16),
            pltpu.SemaphoreType.DMA((1 + 2 * CHUNKS,)),
        ],
        compiler_params=FULL,
        cost_estimate=cost(PREPARE_COST),
        name="prepare",
    )(index, cotangent, out_weight, after)


def lead_kernel(own_ref, second_ref, first_ref, mult_ref, whole_ref,
                plus_ref, minus_ref, whole_out):
    del mult_ref
    n = STRIDE_ROWS
    plus_ref[:n] = own_ref[:n]
    plus_ref[n:2 * n] = first_ref[:n]
    plus_ref[2 * n:] = second_ref[:n]
    minus_ref[:n] = own_ref[:n]
    minus_ref[n:] = second_ref[:n]
    whole_out[...] = whole_ref[...]


def leads(own, first, second, mult, whole):
    n = STRIDE_ROWS
    return pl.pallas_call(
        lead_kernel,
        out_shape=(shape(3 * n, PAIR), shape(2 * n, PAIR), shape(*whole.shape)),
        in_specs=[VMEM] * 5,
        out_specs=(VMEM,) * 3,
        compiler_params=PARAMS,
        name="leads",
    )(own, second, first, mult, whole)


def attend_kernel(sides, mult_ref, q_ref, grad_ref, *refs):
    block_refs = refs[:3 + sides]
    att_ref, dq_ref = refs[3 + sides:5 + sides]
    sum_refs = refs[5 + sides:8 + 2 * sides]
    keys_ref = refs[-1]
    total_rows = keys_ref.shape[0]
    spans = []
    row = 0
    for ref in block_refs:
        spans.append((row, row + ref.shape[0]))
        keys_ref[row:row + ref.shape[0], :] = ref[...]
        row += ref.shape[0]
    if row < total_rows:
        keys_ref[row:, :] = jnp.zeros((total_rows - row, PAIR), BF16)
    keys = keys_ref[:, :HD]
    values = keys_ref[:, HD:]
    q = q_ref[...]
    grad = grad_ref[...]
    mult = mult_ref[0:1, :]

    scores = dot_nt(q, keys) + jnp.where(mult > 0.0, 0.0, ABSENT)
    top = jnp.max(scores, axis=1, keepdims=True)
    terms = jnp.exp2((scores - top) * (SCALE * LOG2E)) * mult
    probability = terms * (1.0 / jnp.sum(terms, axis=1, keepdims=True))
    weights = probability.astype(BF16)
    att_ref[...] = dot_nn(weights, values).astype(BF16)

    grad_weights = dot_nt(grad, values)
    delta = jnp.sum(probability * grad_weights, axis=1, keepdims=True)
    grad_scores = (probability * (grad_weights - delta) * SCALE).astype(BF16)
    dq_ref[...] = dot_nn(grad_scores, keys).astype(BF16)
    key_terms = dot_tn(grad_scores, q)
    value_terms = dot_tn(weights, grad)
    for (start, end), ref in zip(spans, sum_refs):
        ref[:, :HD] = key_terms[start:end].astype(ref.dtype)
        ref[:, HD:] = value_terms[start:end].astype(ref.dtype)


def attend(mult, q, grad, window, sides):
    def body(*refs):
        attend_kernel(len(sides), *refs)

    return pl.pallas_call(
        body,
        out_shape=(shape(BLK, HD), shape(BLK, HD))
        + (shape(BLK, PAIR, kind=F32),) * 3
        + tuple(shape(*s.shape) for s in sides),
        in_specs=[VMEM] * (6 + len(sides)),
        out_specs=(VMEM,) * (5 + len(sides)),
        scratch_shapes=[pltpu.VMEM((mult.shape[1], PAIR), BF16)],
        compiler_params=PARAMS,
        cost_estimate=cost(ATTEND_COST),
        name="attend",
    )(mult, q, grad, *window, *sides)


def combine_kernel(own_ref, first_ref, second_ref, plus_ref, minus_ref, whole_ref, half_ref,
                   att_ref, own_out, first_out, second_out, att_out):
    plus = plus_ref[...].astype(F32)
    minus = minus_ref[...].astype(F32)
    n = STRIDE_ROWS
    own_out[n:] = own_ref[n:]
    own_out[:n] = own_ref[:n] + plus[:n] + minus[:n]
    second_out[n:] = second_ref[n:].astype(BF16)
    second_out[:n] = (second_ref[:n] + plus[2 * n:] + minus[n:]).astype(BF16)
    first_out[n:BLK] = first_ref[n:].astype(BF16)
    first_out[:n] = (first_ref[:n] + plus[n:2 * n]).astype(BF16)
    att_out[...] = att_ref[...]
    row = BLK
    for ref in (whole_ref, half_ref):
        for c in range(0, ref.shape[1], PAIR):
            first_out[row:row + ref.shape[0]] = ref[:, c:c + PAIR]
            row += ref.shape[0]


def combine(own, first, second, plus, minus, whole, half, att):
    extra = (whole.size + half.size) // PAIR
    return pl.pallas_call(
        combine_kernel,
        out_shape=(shape(BLK, PAIR, kind=F32), shape(BLK + extra, PAIR), shape(BLK, PAIR),
                   shape(BLK, HD)),
        in_specs=[VMEM] * 8,
        out_specs=(VMEM,) * 4,
        compiler_params=PARAMS,
        cost_estimate=cost(COMBINE_COST),
        name="combine",
    )(own, first, second, plus, minus, whole, half, att)


def gather_kernel(*refs):
    for r, ref in enumerate(refs[:-1]):
        refs[-1][:, r * HD:(r + 1) * HD] = ref[...]


def gather(attentions):
    return pl.pallas_call(
        gather_kernel,
        out_shape=shape(BLK, len(attentions) * HD),
        in_specs=[VMEM] * len(attentions),
        out_specs=VMEM,
        compiler_params=PARAMS,
        cost_estimate=cost(GATHER_COST),
        name="gather",
    )(*attentions)


def settle(total, lead, dk_ref, dv_ref):
    for ref, c in ((dk_ref, 0), (dv_ref, HD)):
        ref[:STRIDE_ROWS] = lead[:, c:c + HD].astype(ref.dtype)
        ref[STRIDE_ROWS:] = total[STRIDE_ROWS:, c:c + HD].astype(ref.dtype)


def finish_ring_kernel(*refs):
    att_ref, near_ref, far_ref = refs[:3]
    att = [att_ref[...], near_ref[...], far_ref[:, :HD], far_ref[:, HD:]]
    mine_ref, whole_ref, half_ref, first_ref, own_ref, second_ref = refs[3:9]
    mixed_ref, dk_ref, dv_ref = refs[9:]
    core = lax.axis_index("seq") & 1
    half = HD // 2
    here = jnp.where(core == 0, att[1], att[2])
    there = jnp.where(core == 0, att[2], att[1])
    here_half = jnp.where(core == 0, att[3][:, :half], att[3][:, half:])
    there_half = jnp.where(core == 0, att[3][:, half:], att[3][:, :half])
    whole_row = BLK
    half_row = BLK + (mine_ref.shape[1] // PAIR) * HD
    for i, c in enumerate(range(0, mine_ref.shape[1], PAIR)):
        span = slice(c, c + PAIR)
        other_whole = first_ref[whole_row + i * HD:whole_row + (i + 1) * HD]
        other_half = first_ref[half_row + i * half:half_row + (i + 1) * half]
        mixed = dot_nn(att[0], mine_ref[:, span]) + dot_nn(here, whole_ref[:, span])
        mixed = mixed + dot_nn(there, other_whole) + dot_nn(here_half, half_ref[:, span])
        mixed = mixed + dot_nn(there_half, other_half)
        mixed_ref[:, span] = mixed.astype(mixed_ref.dtype)
    total = own_ref[...] + first_ref[:BLK].astype(F32) + second_ref[...].astype(F32)
    settle(total, total[:STRIDE_ROWS], dk_ref, dv_ref)


def finish_ring(attentions, mine, whole, half, first, own, second):
    return pl.pallas_call(
        finish_ring_kernel,
        out_shape=(shape(BLK, mine.shape[1]), shape(BLK, HD), shape(BLK, HD)),
        in_specs=[VMEM] * 9,
        out_specs=(VMEM,) * 3,
        compiler_params=PARAMS,
        name="finish",
    )(*attentions, mine, whole, half, first, own, second)


def finish_kernel(count, *refs):
    att_refs = refs[:count]
    w_refs = refs[count:2 * count]
    own_ref, first_ref, second_ref, side_ref, mixed_ref, dk_ref, dv_ref = refs[2 * count:]
    mixed = None
    for ref, w in zip(att_refs, w_refs):
        term = dot_nn(ref[...], w[...])
        mixed = term if mixed is None else mixed + term
    mixed_ref[...] = mixed.astype(mixed_ref.dtype)
    total = own_ref[...] + first_ref[...].astype(F32) + second_ref[...].astype(F32)
    lead = total[:STRIDE_ROWS]
    for i in range(side_ref.shape[0] // STRIDE_ROWS):
        lead = lead + side_ref[i * STRIDE_ROWS:(i + 1) * STRIDE_ROWS].astype(F32)
    settle(total, lead, dk_ref, dv_ref)


def finish(attentions, slices, own, first, second, side):
    width = slices[0].shape[1]
    count = len(attentions)

    def body(*refs):
        finish_kernel(count, *refs)

    return pl.pallas_call(
        body,
        out_shape=(shape(BLK, width), shape(BLK, HD), shape(BLK, HD)),
        in_specs=[VMEM] * (2 * count + 4),
        out_specs=(VMEM,) * 3,
        compiler_params=PARAMS,
        name="finish",
    )(*attentions, *slices, own, first, second, side)


def spread_slice(array):
    seq = lax.axis_size("seq")
    heads = lax.axis_size("head")
    pairs = [(b * heads + h, b * heads + (h ^ (1 + b % 2))) for b in range(seq)
             for h in range(heads)]
    return lax.ppermute(array, ("seq", "head"), pairs)


def shards(queries, key_rows, value_rows, out_weight, strided_index, cotangent):
    seq = lax.axis_size("seq")
    heads = lax.axis_size("head")
    ring = seq == 8 and heads == 4
    n = STRIDE_ROWS
    side_rows = seq * n
    columns = 3 * BLK + side_rows
    own = jnp.concatenate([key_rows, value_rows], axis=1)
    second = trade(own, -1)
    first = trade(own, 1)
    grad, mult, *slices = prepare(
        ring, strided_index, cotangent, out_weight, heads, columns, own
    )
    if ring:
        mine, whole, half = slices
        half = swap(half, 3)
        plus, minus, whole = leads(own, first, second, mult, whole)
        whole = spread_slice(whole)
        att, dq, own_sum, first_sum, second_sum, to_plus, to_minus = attend(
            mult, queries, grad, (own, first, second), (trade(plus, 3), trade(minus, -3))
        )
        far = gather([swap(att, 2), swap(att, 3)])
        own_sum, to_first, to_second, last = combine(
            own_sum, first_sum, second_sum, trade(to_plus, 3), trade(to_minus, -3), whole, half,
            att,
        )
        mixed, dk, dv = finish_ring(
            [att, swap(last, 1), far], mine, whole, half, trade(to_first, 1), own_sum,
            trade(to_second, -1),
        )
    else:
        slices = [slices[0]] + [swap(slices[r], r) for r in range(1, heads)]
        spread = jnp.broadcast_to(own[None, :n], (seq, n, PAIR))
        side = lax.all_to_all(spread, "seq", 0, 0).reshape(side_rows, PAIR)
        att, dq, own_sum, first_sum, second_sum, to_side = attend(
            mult, queries, grad, (own, first, second), (side,)
        )
        from_side = lax.all_to_all(to_side.reshape(seq, n, PAIR), "seq", 0, 0)
        mixed, dk, dv = finish(
            [att] + [swap(att, r) for r in range(1, heads)], slices, own_sum,
            trade(first_sum.astype(BF16), 1), trade(second_sum.astype(BF16), -1),
            from_side.reshape(side_rows, PAIR),
        )
    return (mixed, dq, dk, dv)


def solution(mesh):
    in_specs = (
        P("seq", "head"),
        P("seq", "head"),
        P("seq", "head"),
        P("head", None),
        P("seq", None),
        P("seq", None),
    )
    out_specs = (P("seq", "head"), P("seq", "head"), P("seq", "head"), P("seq", "head"))
    return jax.shard_map(shards, mesh=mesh, in_specs=in_specs, out_specs=out_specs, check_vma=False)
```

```python
import jax
import jax.numpy as jnp
from jax import lax
from jax.experimental import pallas as pl
from jax.experimental.pallas import tpu as pltpu
from jax.sharding import PartitionSpec as P

HD = 128
BLK = 128
STRIDE_ROWS = 32
PAIR = 2 * HD
SCALE = HD ** (-0.5)
LOG2E = 1.4426950408889634
ABSENT = -1e30
VMEM = pl.BlockSpec(memory_space=pltpu.VMEM)
HBM = pl.BlockSpec(memory_space=pltpu.HBM)
PARAMS = pltpu.CompilerParams(vmem_limit_bytes=40 * 1024 * 1024)
FULL = pltpu.CompilerParams(vmem_limit_bytes=int(53.3 * 1024 * 1024))
BF16 = jnp.bfloat16
PREPARE_COST = 10**10
ATTEND_COST = 10**9
COMBINE_COST = 10**10
GATHER_COST = 10**10
F32 = jnp.float32


def dot_nt(a, b):
    return lax.dot_general(a, b, (((1,), (1,)), ((), ())), preferred_element_type=F32)


def dot_nn(a, b):
    return lax.dot_general(a, b, (((1,), (0,)), ((), ())), preferred_element_type=F32)


def dot_tn(a, b):
    return lax.dot_general(a, b, (((0,), (0,)), ((), ())), preferred_element_type=F32)


def shape(*dims, kind=BF16):
    return jax.ShapeDtypeStruct(dims, kind)


def trade(array, step):
    count = lax.axis_size("seq")
    return lax.ppermute(
        array, "seq", [(i, (i + (step if i % 2 == 0 else -step)) % count) for i in range(count)]
    )


def swap(array, mask):
    count = lax.axis_size("head")
    return lax.ppermute(array, "head", [(i, i ^ mask) for i in range(count)])


def count_of(picks, group):
    total = jnp.int32(0)
    for pick in picks:
        total = total + jnp.where(pick == group, 1, 0)
    return total.astype(F32)


def fill_multiplicity(ring, index_ref, mult_ref):
    per_block = BLK // STRIDE_ROWS
    picks = [index_ref[0, i] for i in range(index_ref.shape[1])]
    shape_of = mult_ref.shape
    lane = lax.broadcasted_iota(jnp.int32, shape_of, 1)
    mult = jnp.where(lane < 3 * BLK, 1.0, 0.0)
    if ring:
        b = lax.axis_index("seq")
        sign = 1 - 2 * (b & 1)
        counts = [count_of(picks, j) for j in range(2)]
        offsets = [(0, 0), (BLK, 1), (2 * BLK, -1), (3 * BLK, 3), (3 * BLK + 32, 2),
                   (3 * BLK + 64, 4), (3 * BLK + 96, -3), (3 * BLK + 128, -2)]
        for start, offset in offsets:
            owner = (b + 16 + sign * offset) & 7
            count = jnp.where(owner < per_block, counts[0], counts[1])
            inside = (lane >= start) & (lane < start + STRIDE_ROWS)
            mult = mult + jnp.where(inside, count, 0.0)
    else:
        for j in range((shape_of[1] - 3 * BLK) // BLK):
            start = (3 + j) * BLK
            inside = (lane >= start) & (lane < start + BLK)
            mult = mult + jnp.where(inside, count_of(picks, j), 0.0)
    mult_ref[...] = mult


def cost(flops):
    return pl.CostEstimate(flops=flops, bytes_accessed=0, transcendentals=0)


CHUNKS = 4


def prepare_kernel(ring, index_hbm, cot_hbm, w_hbm, after_ref, grad_ref, mult_ref, *refs):
    del after_ref
    index_ref, cot_ref, w_ref, sems = refs[-4:]
    slice_refs = refs[:-4]
    copies = [(index_hbm, index_ref)]
    depth = cot_ref.shape[1] // CHUNKS
    for i in range(CHUNKS):
        span = pl.ds(i * depth, depth)
        copies.append((w_hbm.at[:, span], w_ref.at[:, span]))
        copies.append((cot_hbm.at[:, span], cot_ref.at[:, span]))
    copies = [pltpu.make_async_copy(src, dst, sems.at[i]) for i, (src, dst) in enumerate(copies)]
    for copy in copies:
        copy.start()
    copies[0].wait()
    fill_multiplicity(ring, index_ref, mult_ref)
    total = None
    for i in range(CHUNKS):
        copies[1 + 2 * i].wait()
        copies[2 + 2 * i].wait()
        span = slice(i * depth, (i + 1) * depth)
        term = dot_nt(cot_ref[:, span], w_ref[:, span])
        total = term if total is None else total + term
    grad_ref[...] = total.astype(grad_ref.dtype)

    width = slice_refs[0].shape[1]
    head = lax.axis_index("head")

    def columns(h):
        return pl.ds(pl.multiple_of(h * width, width), width)

    if ring:
        core = lax.axis_index("seq") & 1
        half = HD // 2
        mine_ref, whole_ref, half_ref = slice_refs
        mine_ref[...] = w_ref[:, columns(head)]
        whole_ref[...] = w_ref[:, columns(head ^ (1 + core))]
        rows = pl.ds(pl.multiple_of(core * half, half), half)
        half_ref[...] = w_ref[rows, columns(head ^ 3)]
    else:
        for r, ref in enumerate(slice_refs):
            ref[...] = w_ref[:, columns(head ^ r)]


def prepare(ring, index, cotangent, out_weight, heads, columns, after):
    width = out_weight.shape[1] // heads
    rows = (HD, HD, HD // 2) if ring else (HD,) * heads

    def body(*refs):
        prepare_kernel(ring, *refs)

    return pl.pallas_call(
        body,
        out_shape=(shape(BLK, HD), shape(8, columns, kind=F32))
        + tuple(shape(r, width) for r in rows),
        in_specs=[HBM] * 3 + [VMEM],
        out_specs=(VMEM,) * (2 + len(rows)),
        scratch_shapes=[
            pltpu.SMEM(index.shape, jnp.int32),
            pltpu.VMEM(cotangent.shape, BF16),
            pltpu.VMEM(out_weight.shape, BF16),
            pltpu.SemaphoreType.DMA((1 + 2 * CHUNKS,)),
        ],
        compiler_params=FULL,
        cost_estimate=cost(PREPARE_COST),
        name="prepare",
    )(index, cotangent, out_weight, after)


def lead_kernel(own_ref, second_ref, first_ref, mult_ref, whole_ref,
                plus_ref, minus_ref, whole_out):
    del mult_ref
    n = STRIDE_ROWS
    plus_ref[:n] = own_ref[:n]
    plus_ref[n:2 * n] = first_ref[:n]
    plus_ref[2 * n:] = second_ref[:n]
    minus_ref[:n] = own_ref[:n]
    minus_ref[n:] = second_ref[:n]
    whole_out[...] = whole_ref[...]


def leads(own, first, second, mult, whole):
    n = STRIDE_ROWS
    return pl.pallas_call(
        lead_kernel,
        out_shape=(shape(3 * n, PAIR), shape(2 * n, PAIR), shape(*whole.shape)),
        in_specs=[VMEM] * 5,
        out_specs=(VMEM,) * 3,
        compiler_params=PARAMS,
        name="leads",
    )(own, second, first, mult, whole)


def attend_kernel(sides, mult_ref, q_ref, grad_ref, *refs):
    block_refs = refs[:3 + sides]
    att_ref, dq_ref = refs[3 + sides:5 + sides]
    sum_refs = refs[5 + sides:8 + 2 * sides]
    keys_ref = refs[-1]
    total_rows = keys_ref.shape[0]
    spans = []
    row = 0
    for ref in block_refs:
        spans.append((row, row + ref.shape[0]))
        keys_ref[row:row + ref.shape[0], :] = ref[...]
        row += ref.shape[0]
    if row < total_rows:
        keys_ref[row:, :] = jnp.zeros((total_rows - row, PAIR), BF16)
    keys = keys_ref[:, :HD]
    values = keys_ref[:, HD:]
    q = q_ref[...]
    grad = grad_ref[...]
    mult = mult_ref[0:1, :]

    scores = dot_nt(q, keys) + jnp.where(mult > 0.0, 0.0, ABSENT)
    top = jnp.max(scores, axis=1, keepdims=True)
    terms = jnp.exp2((scores - top) * (SCALE * LOG2E)) * mult
    probability = terms * (1.0 / jnp.sum(terms, axis=1, keepdims=True))
    weights = probability.astype(BF16)
    att_ref[...] = dot_nn(weights, values).astype(BF16)

    grad_weights = dot_nt(grad, values)
    delta = jnp.sum(probability * grad_weights, axis=1, keepdims=True)
    grad_scores = (probability * (grad_weights - delta) * SCALE).astype(BF16)
    dq_ref[...] = dot_nn(grad_scores, keys).astype(BF16)
    key_terms = dot_tn(grad_scores, q)
    value_terms = dot_tn(weights, grad)
    for (start, end), ref in zip(spans, sum_refs):
        ref[:, :HD] = key_terms[start:end].astype(ref.dtype)
        ref[:, HD:] = value_terms[start:end].astype(ref.dtype)


def attend(mult, q, grad, window, sides):
    def body(*refs):
        attend_kernel(len(sides), *refs)

    return pl.pallas_call(
        body,
        out_shape=(shape(BLK, HD), shape(BLK, HD))
        + (shape(BLK, PAIR, kind=F32),) * 3
        + tuple(shape(*s.shape) for s in sides),
        in_specs=[VMEM] * (6 + len(sides)),
        out_specs=(VMEM,) * (5 + len(sides)),
        scratch_shapes=[pltpu.VMEM((mult.shape[1], PAIR), BF16)],
        compiler_params=PARAMS,
        cost_estimate=cost(ATTEND_COST),
        name="attend",
    )(mult, q, grad, *window, *sides)


def combine_kernel(own_ref, first_ref, second_ref, plus_ref, minus_ref, whole_ref, half_ref,
                   att_ref, own_out, first_out, second_out, att_out):
    plus = plus_ref[...].astype(F32)
    minus = minus_ref[...].astype(F32)
    n = STRIDE_ROWS
    own_out[n:] = own_ref[n:]
    own_out[:n] = own_ref[:n] + plus[:n] + minus[:n]
    second_out[n:] = second_ref[n:].astype(BF16)
    second_out[:n] = (second_ref[:n] + plus[2 * n:] + minus[n:]).astype(BF16)
    first_out[n:BLK] = first_ref[n:].astype(BF16)
    first_out[:n] = (first_ref[:n] + plus[n:2 * n]).astype(BF16)
    att_out[...] = att_ref[...]
    row = BLK
    for ref in (whole_ref, half_ref):
        for c in range(0, ref.shape[1], PAIR):
            first_out[row:row + ref.shape[0]] = ref[:, c:c + PAIR]
            row += ref.shape[0]


def combine(own, first, second, plus, minus, whole, half, att):
    extra = (whole.size + half.size) // PAIR
    return pl.pallas_call(
        combine_kernel,
        out_shape=(shape(BLK, PAIR, kind=F32), shape(BLK + extra, PAIR), shape(BLK, PAIR),
                   shape(BLK, HD)),
        in_specs=[VMEM] * 8,
        out_specs=(VMEM,) * 4,
        compiler_params=PARAMS,
        cost_estimate=cost(COMBINE_COST),
        name="combine",
    )(own, first, second, plus, minus, whole, half, att)


def gather_kernel(*refs):
    for r, ref in enumerate(refs[:-1]):
        refs[-1][:, r * HD:(r + 1) * HD] = ref[...]


def gather(attentions):
    return pl.pallas_call(
        gather_kernel,
        out_shape=shape(BLK, len(attentions) * HD),
        in_specs=[VMEM] * len(attentions),
        out_specs=VMEM,
        compiler_params=PARAMS,
        cost_estimate=cost(GATHER_COST),
        name="gather",
    )(*attentions)


def settle(total, lead, dk_ref, dv_ref):
    for ref, c in ((dk_ref, 0), (dv_ref, HD)):
        ref[:STRIDE_ROWS] = lead[:, c:c + HD].astype(ref.dtype)
        ref[STRIDE_ROWS:] = total[STRIDE_ROWS:, c:c + HD].astype(ref.dtype)


def finish_ring_kernel(*refs):
    att_ref, near_ref, far_ref, mine_ref, whole_ref, half_ref = refs[:6]
    first_ref, own_ref, second_ref, dq_ref = refs[6:10]
    mixed_hbm, dq_hbm, dk_hbm, dv_hbm, mixed_ref, dk_ref, dv_ref, sems = refs[10:]
    copies = []

    def send(src, dst):
        copy = pltpu.make_async_copy(src, dst, sems.at[len(copies)])
        copy.start()
        copies.append(copy)

    send(dq_ref, dq_hbm)
    total = own_ref[...] + first_ref[:BLK].astype(F32) + second_ref[...].astype(F32)
    settle(total, total[:STRIDE_ROWS], dk_ref, dv_ref)
    send(dk_ref, dk_hbm)
    send(dv_ref, dv_hbm)
    att = [att_ref[...], near_ref[...], far_ref[:, :HD], far_ref[:, HD:]]
    core = lax.axis_index("seq") & 1
    half = HD // 2
    here = jnp.where(core == 0, att[1], att[2])
    there = jnp.where(core == 0, att[2], att[1])
    here_half = jnp.where(core == 0, att[3][:, :half], att[3][:, half:])
    there_half = jnp.where(core == 0, att[3][:, half:], att[3][:, :half])
    whole_row = BLK
    half_row = BLK + (mine_ref.shape[1] // PAIR) * HD
    for i, c in enumerate(range(0, mine_ref.shape[1], PAIR)):
        span = slice(c, c + PAIR)
        other_whole = first_ref[whole_row + i * HD:whole_row + (i + 1) * HD]
        other_half = first_ref[half_row + i * half:half_row + (i + 1) * half]
        mixed = dot_nn(att[0], mine_ref[:, span]) + dot_nn(here, whole_ref[:, span])
        mixed = mixed + dot_nn(there, other_whole) + dot_nn(here_half, half_ref[:, span])
        mixed = mixed + dot_nn(there_half, other_half)
        mixed_ref[:, span] = mixed.astype(mixed_ref.dtype)
        send(mixed_ref.at[:, pl.ds(c, PAIR)], mixed_hbm.at[:, pl.ds(c, PAIR)])
    for copy in copies:
        copy.wait()


def finish_ring(attentions, mine, whole, half, first, own, second, dq):
    width = mine.shape[1]
    return pl.pallas_call(
        finish_ring_kernel,
        out_shape=(shape(BLK, width),) + (shape(BLK, HD),) * 3,
        in_specs=[VMEM] * 10,
        out_specs=(HBM,) * 4,
        scratch_shapes=[
            pltpu.VMEM((BLK, width), BF16),
            pltpu.VMEM((BLK, HD), BF16),
            pltpu.VMEM((BLK, HD), BF16),
            pltpu.SemaphoreType.DMA((3 + width // PAIR,)),
        ],
        compiler_params=PARAMS,
        name="finish",
    )(*attentions, mine, whole, half, first, own, second, dq)


def finish_kernel(count, *refs):
    att_refs = refs[:count]
    w_refs = refs[count:2 * count]
    own_ref, first_ref, second_ref, side_ref, mixed_ref, dk_ref, dv_ref = refs[2 * count:]
    mixed = None
    for ref, w in zip(att_refs, w_refs):
        term = dot_nn(ref[...], w[...])
        mixed = term if mixed is None else mixed + term
    mixed_ref[...] = mixed.astype(mixed_ref.dtype)
    total = own_ref[...] + first_ref[...].astype(F32) + second_ref[...].astype(F32)
    lead = total[:STRIDE_ROWS]
    for i in range(side_ref.shape[0] // STRIDE_ROWS):
        lead = lead + side_ref[i * STRIDE_ROWS:(i + 1) * STRIDE_ROWS].astype(F32)
    settle(total, lead, dk_ref, dv_ref)


def finish(attentions, slices, own, first, second, side):
    width = slices[0].shape[1]
    count = len(attentions)

    def body(*refs):
        finish_kernel(count, *refs)

    return pl.pallas_call(
        body,
        out_shape=(shape(BLK, width), shape(BLK, HD), shape(BLK, HD)),
        in_specs=[VMEM] * (2 * count + 4),
        out_specs=(VMEM,) * 3,
        compiler_params=PARAMS,
        name="finish",
    )(*attentions, *slices, own, first, second, side)


def spread_slice(array):
    seq = lax.axis_size("seq")
    heads = lax.axis_size("head")
    pairs = [(b * heads + h, b * heads + (h ^ (1 + b % 2))) for b in range(seq)
             for h in range(heads)]
    return lax.ppermute(array, ("seq", "head"), pairs)


def shards(queries, key_rows, value_rows, out_weight, strided_index, cotangent):
    seq = lax.axis_size("seq")
    heads = lax.axis_size("head")
    ring = seq == 8 and heads == 4
    n = STRIDE_ROWS
    side_rows = seq * n
    columns = 3 * BLK + side_rows
    own = jnp.concatenate([key_rows, value_rows], axis=1)
    second = trade(own, -1)
    first = trade(own, 1)
    grad, mult, *slices = prepare(
        ring, strided_index, cotangent, out_weight, heads, columns, own
    )
    if ring:
        mine, whole, half = slices
        half = swap(half, 3)
        plus, minus, whole = leads(own, first, second, mult, whole)
        whole = spread_slice(whole)
        att, dq, own_sum, first_sum, second_sum, to_plus, to_minus = attend(
            mult, queries, grad, (own, first, second), (trade(plus, 3), trade(minus, -3))
        )
        far = gather([swap(att, 2), swap(att, 3)])
        own_sum, to_first, to_second, last = combine(
            own_sum, first_sum, second_sum, trade(to_plus, 3), trade(to_minus, -3), whole, half,
            att,
        )
        mixed, dq, dk, dv = finish_ring(
            [att, swap(last, 1), far], mine, whole, half, trade(to_first, 1), own_sum,
            trade(to_second, -1), dq,
        )
    else:
        slices = [slices[0]] + [swap(slices[r], r) for r in range(1, heads)]
        spread = jnp.broadcast_to(own[None, :n], (seq, n, PAIR))
        side = lax.all_to_all(spread, "seq", 0, 0).reshape(side_rows, PAIR)
        att, dq, own_sum, first_sum, second_sum, to_side = attend(
            mult, queries, grad, (own, first, second), (side,)
        )
        from_side = lax.all_to_all(to_side.reshape(seq, n, PAIR), "seq", 0, 0)
        mixed, dk, dv = finish(
            [att] + [swap(att, r) for r in range(1, heads)], slices, own_sum,
            trade(first_sum.astype(BF16), 1), trade(second_sum.astype(BF16), -1),
            from_side.reshape(side_rows, PAIR),
        )
    return (mixed, dq, dk, dv)


def solution(mesh):
    in_specs = (
        P("seq", "head"),
        P("seq", "head"),
        P("seq", "head"),
        P("head", None),
        P("seq", None),
        P("seq", None),
    )
    out_specs = (P("seq", "head"), P("seq", "head"), P("seq", "head"), P("seq", "head"))
    return jax.shard_map(shards, mesh=mesh, in_specs=in_specs, out_specs=out_specs, check_vma=False)
```

```python
import jax
import jax.numpy as jnp
from jax import lax
from jax.experimental import pallas as pl
from jax.experimental.pallas import tpu as pltpu
from jax.sharding import PartitionSpec as P

HD = 128
BLK = 128
STRIDE_ROWS = 32
MARGIN = 16
PAIR = 2 * HD
SCALE = HD ** (-0.5)
LOG2E = 1.4426950408889634
ABSENT = -1e30
VMEM = pl.BlockSpec(memory_space=pltpu.VMEM)
HBM = pl.BlockSpec(memory_space=pltpu.HBM)
PARAMS = pltpu.CompilerParams(vmem_limit_bytes=40 * 1024 * 1024)
FULL = pltpu.CompilerParams(vmem_limit_bytes=int(53.3 * 1024 * 1024))
BF16 = jnp.bfloat16
PREPARE_COST = 10**10
ATTEND_COST = 10**10
COMBINE_COST = 10**10
GATHER_COST = 10**10
F32 = jnp.float32


def dot_nt(a, b):
    return lax.dot_general(a, b, (((1,), (1,)), ((), ())), preferred_element_type=F32)


def dot_nn(a, b):
    return lax.dot_general(a, b, (((1,), (0,)), ((), ())), preferred_element_type=F32)


def dot_tn(a, b):
    return lax.dot_general(a, b, (((0,), (0,)), ((), ())), preferred_element_type=F32)


def shape(*dims, kind=BF16):
    return jax.ShapeDtypeStruct(dims, kind)


def trade(array, step):
    count = lax.axis_size("seq")
    return lax.ppermute(
        array, "seq", [(i, (i + (step if i % 2 == 0 else -step)) % count) for i in range(count)]
    )


def swap(array, mask):
    count = lax.axis_size("head")
    return lax.ppermute(array, "head", [(i, i ^ mask) for i in range(count)])


def count_of(picks, group):
    total = jnp.int32(0)
    for pick in picks:
        total = total + jnp.where(pick == group, 1, 0)
    return total.astype(F32)


def fill_multiplicity(ring, index_ref, mult_ref):
    per_block = BLK // STRIDE_ROWS
    picks = [index_ref[0, i] for i in range(index_ref.shape[1])]
    shape_of = mult_ref.shape
    lane = lax.broadcasted_iota(jnp.int32, shape_of, 1)
    mult = jnp.where(lane < 3 * BLK, 1.0, 0.0)
    if ring:
        b = lax.axis_index("seq")
        sign = 1 - 2 * (b & 1)
        counts = [count_of(picks, j) for j in range(2)]
        places = [(0, 0), (BLK, 1), (2 * BLK, -1)]
        places += [(3 * BLK + i * STRIDE_ROWS, o) for i, o in enumerate((-2, 3, 2, 4, 5))]
        for start, offset in places:
            owner = (b + 16 + sign * offset) & 7
            count = jnp.where(owner < per_block, counts[0], counts[1])
            inside = (lane >= start) & (lane < start + STRIDE_ROWS)
            mult = mult + jnp.where(inside, count, 0.0)
    else:
        for j in range((shape_of[1] - 3 * BLK) // BLK):
            start = (3 + j) * BLK
            inside = (lane >= start) & (lane < start + BLK)
            mult = mult + jnp.where(inside, count_of(picks, j), 0.0)
    mult_ref[...] = mult


def cost(flops):
    return pl.CostEstimate(flops=flops, bytes_accessed=0, transcendentals=0)


CHUNKS = 4


def prepare_kernel(ring, index_hbm, cot_hbm, w_hbm, after_ref, grad_ref, mult_ref, *refs):
    del after_ref
    index_ref, cot_ref, w_ref, sems = refs[-4:]
    slice_refs = refs[:-4]
    copies = [(index_hbm, index_ref)]
    depth = cot_ref.shape[1] // CHUNKS
    for i in range(CHUNKS):
        span = pl.ds(i * depth, depth)
        copies.append((w_hbm.at[:, span], w_ref.at[:, span]))
        copies.append((cot_hbm.at[:, span], cot_ref.at[:, span]))
    copies = [pltpu.make_async_copy(src, dst, sems.at[i]) for i, (src, dst) in enumerate(copies)]
    for copy in copies:
        copy.start()
    copies[0].wait()
    fill_multiplicity(ring, index_ref, mult_ref)
    total = None
    for i in range(CHUNKS):
        copies[1 + 2 * i].wait()
        copies[2 + 2 * i].wait()
        span = slice(i * depth, (i + 1) * depth)
        term = dot_nt(cot_ref[:, span], w_ref[:, span])
        total = term if total is None else total + term
    grad_ref[...] = total.astype(grad_ref.dtype)

    width = slice_refs[0].shape[1]
    head = lax.axis_index("head")

    def columns(h):
        return pl.ds(pl.multiple_of(h * width, width), width)

    if ring:
        core = lax.axis_index("seq") & 1
        half = HD // 2
        mine_ref, whole_ref, half_ref = slice_refs
        mine_ref[...] = w_ref[:, columns(head)]
        whole_ref[...] = w_ref[:, columns(head ^ (1 + core))]
        rows = pl.ds(pl.multiple_of(core * (half - MARGIN), MARGIN), half + MARGIN)
        half_ref[...] = w_ref[rows, columns(head ^ 3)]
    else:
        for r, ref in enumerate(slice_refs):
            ref[...] = w_ref[:, columns(head ^ r)]


def prepare(ring, index, cotangent, out_weight, heads, columns, after):
    width = out_weight.shape[1] // heads
    rows = (HD, HD, HD // 2 + MARGIN) if ring else (HD,) * heads

    def body(*refs):
        prepare_kernel(ring, *refs)

    return pl.pallas_call(
        body,
        out_shape=(shape(BLK, HD), shape(8, columns, kind=F32))
        + tuple(shape(r, width) for r in rows),
        in_specs=[HBM] * 3 + [VMEM],
        out_specs=(VMEM,) * (2 + len(rows)),
        scratch_shapes=[
            pltpu.SMEM(index.shape, jnp.int32),
            pltpu.VMEM(cotangent.shape, BF16),
            pltpu.VMEM(out_weight.shape, BF16),
            pltpu.SemaphoreType.DMA((1 + 2 * CHUNKS,)),
        ],
        compiler_params=FULL,
        cost_estimate=cost(PREPARE_COST),
        name="prepare",
    )(index, cotangent, out_weight, after)


def lead_kernel(own_ref, first_ref, mult_ref, whole_ref, near_ref, pair_ref, whole_out):
    del mult_ref
    n = STRIDE_ROWS
    near_ref[:BLK] = own_ref[...]
    near_ref[BLK:] = first_ref[:n]
    pair_ref[:n] = own_ref[:n]
    pair_ref[n:] = first_ref[:n]
    whole_out[...] = whole_ref[...]


def leads(own, first, mult, whole):
    n = STRIDE_ROWS
    return pl.pallas_call(
        lead_kernel,
        out_shape=(shape(BLK + n, PAIR), shape(2 * n, PAIR), shape(*whole.shape)),
        in_specs=[VMEM] * 4,
        out_specs=(VMEM,) * 3,
        compiler_params=PARAMS,
        name="leads",
    )(own, first, mult, whole)


def attend_kernel(blocks, mult_ref, q_ref, grad_ref, *refs):
    block_refs = refs[:blocks]
    att_ref, dq_ref = refs[blocks:blocks + 2]
    sum_refs = refs[blocks + 2:2 * blocks + 2]
    keys_ref = refs[-1]
    total_rows = keys_ref.shape[0]
    spans = []
    row = 0
    for ref in block_refs:
        spans.append((row, row + ref.shape[0]))
        keys_ref[row:row + ref.shape[0], :] = ref[...]
        row += ref.shape[0]
    if row < total_rows:
        keys_ref[row:, :] = jnp.zeros((total_rows - row, PAIR), BF16)
    keys = keys_ref[:, :HD]
    values = keys_ref[:, HD:]
    q = q_ref[...]
    grad = grad_ref[...]
    mult = mult_ref[0:1, :]

    scores = dot_nt(q, keys) + jnp.where(mult > 0.0, 0.0, ABSENT)
    top = jnp.max(scores, axis=1, keepdims=True)
    terms = jnp.exp2((scores - top) * (SCALE * LOG2E)) * mult
    probability = terms * (1.0 / jnp.sum(terms, axis=1, keepdims=True))
    weights = probability.astype(BF16)
    att_ref[...] = dot_nn(weights, values).astype(BF16)

    grad_weights = dot_nt(grad, values)
    delta = jnp.sum(probability * grad_weights, axis=1, keepdims=True)
    grad_scores = (probability * (grad_weights - delta) * SCALE).astype(BF16)
    dq_ref[...] = dot_nn(grad_scores, keys).astype(BF16)
    key_terms = dot_tn(grad_scores, q)
    value_terms = dot_tn(weights, grad)
    for (start, end), ref in zip(spans, sum_refs):
        ref[:, :HD] = key_terms[start:end].astype(ref.dtype)
        ref[:, HD:] = value_terms[start:end].astype(ref.dtype)


def attend(mult, q, grad, blocks, wide):
    def body(*refs):
        attend_kernel(len(blocks), *refs)

    return pl.pallas_call(
        body,
        out_shape=(shape(BLK, HD), shape(BLK, HD))
        + tuple(shape(*b.shape, kind=F32 if i < wide else BF16) for i, b in enumerate(blocks)),
        in_specs=[VMEM] * (3 + len(blocks)),
        out_specs=(VMEM,) * (2 + len(blocks)),
        scratch_shapes=[pltpu.VMEM((mult.shape[1], PAIR), BF16)],
        compiler_params=PARAMS,
        cost_estimate=cost(ATTEND_COST),
        name="attend",
    )(mult, q, grad, *blocks)


def half_rows():
    core = lax.axis_index("seq") & 1
    return pl.ds(pl.multiple_of(core * MARGIN, MARGIN), HD // 2)


def combine_kernel(own_ref, first_ref, near_ref, plus_ref, across_ref, whole_ref, half_ref,
                   own_out, first_out):
    near = near_ref[...].astype(F32)
    plus = plus_ref[...].astype(F32)
    across = across_ref[...].astype(F32)
    n = STRIDE_ROWS
    own_out[n:] = own_ref[n:] + near[n:BLK]
    own_out[:n] = own_ref[:n] + near[:n] + plus[:n] + across[:n]
    first_out[n:BLK] = first_ref[n:].astype(BF16)
    first_out[:n] = (first_ref[:n] + near[BLK:] + plus[n:] + across[n:]).astype(BF16)
    row = BLK
    for ref, rows in ((whole_ref, slice(0, HD)), (half_ref, half_rows())):
        for c in range(0, ref.shape[1], PAIR):
            piece = ref[rows, c:c + PAIR]
            first_out[row:row + piece.shape[0]] = piece
            row += piece.shape[0]


def combine(own, first, near, plus, across, whole, half):
    extra = (HD + HD // 2) * whole.shape[1] // PAIR
    return pl.pallas_call(
        combine_kernel,
        out_shape=(shape(BLK, PAIR, kind=F32), shape(BLK + extra, PAIR)),
        in_specs=[VMEM] * 7,
        out_specs=(VMEM,) * 2,
        compiler_params=PARAMS,
        cost_estimate=cost(COMBINE_COST),
        name="combine",
    )(own, first, near, plus, across, whole, half)


def gather_kernel(*refs):
    for r, ref in enumerate(refs[:-1]):
        refs[-1][:, r * HD:(r + 1) * HD] = ref[...]


def gather(attentions):
    return pl.pallas_call(
        gather_kernel,
        out_shape=shape(BLK, len(attentions) * HD),
        in_specs=[VMEM] * len(attentions),
        out_specs=VMEM,
        compiler_params=PARAMS,
        cost_estimate=cost(GATHER_COST),
        name="gather",
    )(*attentions)


def settle(total, lead, dk_ref, dv_ref):
    for ref, c in ((dk_ref, 0), (dv_ref, HD)):
        ref[:STRIDE_ROWS] = lead[:, c:c + HD].astype(ref.dtype)
        ref[STRIDE_ROWS:] = total[STRIDE_ROWS:, c:c + HD].astype(ref.dtype)


def finish_ring_kernel(*refs):
    att_ref, mine_ref, whole_ref, half_ref, first_ref, own_ref, dq_ref = refs[:7]
    mixed_hbm, dq_hbm, dk_hbm, dv_hbm, mixed_ref, dk_ref, dv_ref, sems = refs[7:]
    copies = []

    def send(src, dst):
        copy = pltpu.make_async_copy(src, dst, sems.at[len(copies)])
        copy.start()
        copies.append(copy)

    send(dq_ref, dq_hbm)
    total = own_ref[...] + first_ref[:BLK].astype(F32)
    settle(total, total[:STRIDE_ROWS], dk_ref, dv_ref)
    send(dk_ref, dk_hbm)
    send(dv_ref, dv_hbm)
    att = [att_ref[:, r * HD:(r + 1) * HD] for r in range(4)]
    core = lax.axis_index("seq") & 1
    half = HD // 2
    here = jnp.where(core == 0, att[1], att[2])
    there = jnp.where(core == 0, att[2], att[1])
    here_half = jnp.where(core == 0, att[3][:, :half], att[3][:, half:])
    there_half = jnp.where(core == 0, att[3][:, half:], att[3][:, :half])
    whole_row = BLK
    half_row = BLK + (mine_ref.shape[1] // PAIR) * HD
    for i, c in enumerate(range(0, mine_ref.shape[1], PAIR)):
        span = slice(c, c + PAIR)
        other_whole = first_ref[whole_row + i * HD:whole_row + (i + 1) * HD]
        other_half = first_ref[half_row + i * half:half_row + (i + 1) * half]
        mixed = dot_nn(att[0], mine_ref[:, span]) + dot_nn(here, whole_ref[:, span])
        mixed = mixed + dot_nn(there, other_whole) + dot_nn(here_half, half_ref[half_rows(), span])
        mixed = mixed + dot_nn(there_half, other_half)
        mixed_ref[:, span] = mixed.astype(mixed_ref.dtype)
        send(mixed_ref.at[:, pl.ds(c, PAIR)], mixed_hbm.at[:, pl.ds(c, PAIR)])
    for copy in copies:
        copy.wait()


def finish_ring(attentions, mine, whole, half, first, own, dq):
    width = mine.shape[1]
    return pl.pallas_call(
        finish_ring_kernel,
        out_shape=(shape(BLK, width),) + (shape(BLK, HD),) * 3,
        in_specs=[VMEM] * 7,
        out_specs=(HBM,) * 4,
        scratch_shapes=[
            pltpu.VMEM((BLK, width), BF16),
            pltpu.VMEM((BLK, HD), BF16),
            pltpu.VMEM((BLK, HD), BF16),
            pltpu.SemaphoreType.DMA((3 + width // PAIR,)),
        ],
        compiler_params=PARAMS,
        name="finish",
    )(attentions, mine, whole, half, first, own, dq)


def finish_kernel(count, *refs):
    att_refs = refs[:count]
    w_refs = refs[count:2 * count]
    own_ref, first_ref, second_ref, side_ref, mixed_ref, dk_ref, dv_ref = refs[2 * count:]
    mixed = None
    for ref, w in zip(att_refs, w_refs):
        term = dot_nn(ref[...], w[...])
        mixed = term if mixed is None else mixed + term
    mixed_ref[...] = mixed.astype(mixed_ref.dtype)
    total = own_ref[...] + first_ref[...].astype(F32) + second_ref[...].astype(F32)
    lead = total[:STRIDE_ROWS]
    for i in range(side_ref.shape[0] // STRIDE_ROWS):
        lead = lead + side_ref[i * STRIDE_ROWS:(i + 1) * STRIDE_ROWS].astype(F32)
    settle(total, lead, dk_ref, dv_ref)


def finish(attentions, slices, own, first, second, side):
    width = slices[0].shape[1]
    count = len(attentions)

    def body(*refs):
        finish_kernel(count, *refs)

    return pl.pallas_call(
        body,
        out_shape=(shape(BLK, width), shape(BLK, HD), shape(BLK, HD)),
        in_specs=[VMEM] * (2 * count + 4),
        out_specs=(VMEM,) * 3,
        compiler_params=PARAMS,
        name="finish",
    )(*attentions, *slices, own, first, second, side)


def spread_slice(array):
    seq = lax.axis_size("seq")
    heads = lax.axis_size("head")
    pairs = [(b * heads + h, b * heads + (h ^ (1 + b % 2))) for b in range(seq)
             for h in range(heads)]
    return lax.ppermute(array, ("seq", "head"), pairs)


def shards(queries, key_rows, value_rows, out_weight, strided_index, cotangent):
    seq = lax.axis_size("seq")
    heads = lax.axis_size("head")
    ring = seq == 8 and heads == 4
    n = STRIDE_ROWS
    side_rows = seq * n
    columns = 3 * BLK + side_rows
    own = jnp.concatenate([key_rows, value_rows], axis=1)
    first = trade(own, 1)
    grad, mult, *slices = prepare(
        ring, strided_index, cotangent, out_weight, heads, columns, own
    )
    if ring:
        mine, whole, half = slices
        half = swap(half, 3)
        near, pair, whole = leads(own, first, mult, whole)
        whole = spread_slice(whole)
        near = trade(near, -1)
        blocks = (own, first, near, trade(pair, 3), trade(pair, 4))
        att, dq, own_sum, first_sum, to_near, to_plus, to_across = attend(
            mult, queries, grad, blocks, 2
        )
        attentions = gather([att] + [swap(att, r) for r in range(1, heads)])
        own_sum, to_first = combine(
            own_sum, first_sum, trade(to_near, -1), trade(to_plus, 3), trade(to_across, 4),
            whole, half,
        )
        mixed, dq, dk, dv = finish_ring(
            attentions, mine, whole, half, trade(to_first, 1), own_sum, dq
        )
    else:
        second = trade(own, -1)
        slices = [slices[0]] + [swap(slices[r], r) for r in range(1, heads)]
        spread = jnp.broadcast_to(own[None, :n], (seq, n, PAIR))
        side = lax.all_to_all(spread, "seq", 0, 0).reshape(side_rows, PAIR)
        att, dq, own_sum, to_first, to_second, to_side = attend(
            mult, queries, grad, (own, first, second, side), 1
        )
        from_side = lax.all_to_all(to_side.reshape(seq, n, PAIR), "seq", 0, 0)
        mixed, dk, dv = finish(
            [att] + [swap(att, r) for r in range(1, heads)], slices, own_sum,
            trade(to_first, 1), trade(to_second, -1), from_side.reshape(side_rows, PAIR),
        )
    return (mixed, dq, dk, dv)


def solution(mesh):
    in_specs = (
        P("seq", "head"),
        P("seq", "head"),
        P("seq", "head"),
        P("head", None),
        P("seq", None),
        P("seq", None),
    )
    out_specs = (P("seq", "head"), P("seq", "head"), P("seq", "head"), P("seq", "head"))
    return jax.shard_map(shards, mesh=mesh, in_specs=in_specs, out_specs=out_specs, check_vma=False)
```

```python
import jax
import jax.numpy as jnp
from jax import lax
from jax.experimental import pallas as pl
from jax.experimental.pallas import tpu as pltpu
from jax.sharding import PartitionSpec as P

HD = 128
BLK = 128
STRIDE_ROWS = 32
MARGIN = 16
PAIR = 2 * HD
SCALE = HD ** (-0.5)
LOG2E = 1.4426950408889634
ABSENT = -1e30
VMEM = pl.BlockSpec(memory_space=pltpu.VMEM)
HBM = pl.BlockSpec(memory_space=pltpu.HBM)
PARAMS = pltpu.CompilerParams(vmem_limit_bytes=40 * 1024 * 1024)
FULL = pltpu.CompilerParams(vmem_limit_bytes=int(53.3 * 1024 * 1024))
BF16 = jnp.bfloat16
PREPARE_COST = 10**10
ATTEND_COST = 10**10
COMBINE_COST = 10**10
F32 = jnp.float32


def dot_nt(a, b):
    return lax.dot_general(a, b, (((1,), (1,)), ((), ())), preferred_element_type=F32)


def dot_nn(a, b):
    return lax.dot_general(a, b, (((1,), (0,)), ((), ())), preferred_element_type=F32)


def dot_tn(a, b):
    return lax.dot_general(a, b, (((0,), (0,)), ((), ())), preferred_element_type=F32)


def shape(*dims, kind=BF16):
    return jax.ShapeDtypeStruct(dims, kind)


def trade(array, step):
    count = lax.axis_size("seq")
    return lax.ppermute(
        array, "seq", [(i, (i + (step if i % 2 == 0 else -step)) % count) for i in range(count)]
    )


def swap(array, mask):
    count = lax.axis_size("head")
    return lax.ppermute(array, "head", [(i, i ^ mask) for i in range(count)])


def count_of(picks, group):
    total = jnp.int32(0)
    for pick in picks:
        total = total + jnp.where(pick == group, 1, 0)
    return total.astype(F32)


def fill_multiplicity(ring, index_ref, mult_ref):
    per_block = BLK // STRIDE_ROWS
    picks = [index_ref[0, i] for i in range(index_ref.shape[1])]
    shape_of = mult_ref.shape
    lane = lax.broadcasted_iota(jnp.int32, shape_of, 1)
    mult = jnp.where(lane < 3 * BLK, 1.0, 0.0)
    if ring:
        b = lax.axis_index("seq")
        sign = 1 - 2 * (b & 1)
        counts = [count_of(picks, j) for j in range(2)]
        places = [(0, 0), (BLK, 1), (2 * BLK, -1)]
        places += [(3 * BLK + i * STRIDE_ROWS, o) for i, o in enumerate((-2, 3, 2, 4, 5))]
        for start, offset in places:
            owner = (b + 16 + sign * offset) & 7
            count = jnp.where(owner < per_block, counts[0], counts[1])
            inside = (lane >= start) & (lane < start + STRIDE_ROWS)
            mult = mult + jnp.where(inside, count, 0.0)
    else:
        for j in range((shape_of[1] - 3 * BLK) // BLK):
            start = (3 + j) * BLK
            inside = (lane >= start) & (lane < start + BLK)
            mult = mult + jnp.where(inside, count_of(picks, j), 0.0)
    mult_ref[...] = mult


def cost(flops):
    return pl.CostEstimate(flops=flops, bytes_accessed=0, transcendentals=0)


CHUNKS = 4


def prepare_kernel(ring, index_hbm, cot_hbm, w_hbm, after_ref, grad_ref, mult_ref, *refs):
    del after_ref
    index_ref, cot_ref, w_ref, sems = refs[-4:]
    slice_refs = refs[:-4]
    copies = [(index_hbm, index_ref)]
    depth = cot_ref.shape[1] // CHUNKS
    for i in range(CHUNKS):
        span = pl.ds(i * depth, depth)
        copies.append((w_hbm.at[:, span], w_ref.at[:, span]))
        copies.append((cot_hbm.at[:, span], cot_ref.at[:, span]))
    copies = [pltpu.make_async_copy(src, dst, sems.at[i]) for i, (src, dst) in enumerate(copies)]
    for copy in copies:
        copy.start()
    copies[0].wait()
    fill_multiplicity(ring, index_ref, mult_ref)
    total = None
    for i in range(CHUNKS):
        copies[1 + 2 * i].wait()
        copies[2 + 2 * i].wait()
        span = slice(i * depth, (i + 1) * depth)
        term = dot_nt(cot_ref[:, span], w_ref[:, span])
        total = term if total is None else total + term
    grad_ref[...] = total.astype(grad_ref.dtype)

    width = slice_refs[0].shape[1]
    head = lax.axis_index("head")

    def columns(h):
        return pl.ds(pl.multiple_of(h * width, width), width)

    if ring:
        core = lax.axis_index("seq") & 1
        half = HD // 2
        mine_ref, whole_ref, half_ref = slice_refs
        mine_ref[...] = w_ref[:, columns(head)]
        whole_ref[...] = w_ref[:, columns(head ^ (1 + core))]
        rows = pl.ds(pl.multiple_of(core * (half - MARGIN), MARGIN), half + MARGIN)
        half_ref[...] = w_ref[rows, columns(head ^ 3)]
    else:
        for r, ref in enumerate(slice_refs):
            ref[...] = w_ref[:, columns(head ^ r)]


def prepare(ring, index, cotangent, out_weight, heads, columns, after):
    width = out_weight.shape[1] // heads
    rows = (HD, HD, HD // 2 + MARGIN) if ring else (HD,) * heads

    def body(*refs):
        prepare_kernel(ring, *refs)

    return pl.pallas_call(
        body,
        out_shape=(shape(BLK, HD), shape(8, columns, kind=F32))
        + tuple(shape(r, width) for r in rows),
        in_specs=[HBM] * 3 + [VMEM],
        out_specs=(VMEM,) * (2 + len(rows)),
        scratch_shapes=[
            pltpu.SMEM(index.shape, jnp.int32),
            pltpu.VMEM(cotangent.shape, BF16),
            pltpu.VMEM(out_weight.shape, BF16),
            pltpu.SemaphoreType.DMA((1 + 2 * CHUNKS,)),
        ],
        compiler_params=FULL,
        cost_estimate=cost(PREPARE_COST),
        name="prepare",
    )(index, cotangent, out_weight, after)


def lead_kernel(own_ref, first_ref, mult_ref, whole_ref, near_ref, pair_ref, whole_out):
    del mult_ref
    n = STRIDE_ROWS
    near_ref[:BLK] = own_ref[...]
    near_ref[BLK:] = first_ref[:n]
    pair_ref[:n] = own_ref[:n]
    pair_ref[n:] = first_ref[:n]
    whole_out[...] = whole_ref[...]


def leads(own, first, mult, whole):
    n = STRIDE_ROWS
    return pl.pallas_call(
        lead_kernel,
        out_shape=(shape(BLK + n, PAIR), shape(2 * n, PAIR), shape(*whole.shape)),
        in_specs=[VMEM] * 4,
        out_specs=(VMEM,) * 3,
        compiler_params=PARAMS,
        name="leads",
    )(own, first, mult, whole)


def attend_kernel(blocks, mult_ref, q_ref, grad_ref, *refs):
    block_refs = refs[:blocks]
    att_ref, dq_ref = refs[blocks:blocks + 2]
    sum_refs = refs[blocks + 2:2 * blocks + 2]
    keys_ref = refs[-1]
    total_rows = keys_ref.shape[0]
    spans = []
    row = 0
    for ref in block_refs:
        spans.append((row, row + ref.shape[0]))
        keys_ref[row:row + ref.shape[0], :] = ref[...]
        row += ref.shape[0]
    if row < total_rows:
        keys_ref[row:, :] = jnp.zeros((total_rows - row, PAIR), BF16)
    keys = keys_ref[:, :HD]
    values = keys_ref[:, HD:]
    q = q_ref[...]
    grad = grad_ref[...]
    mult = mult_ref[0:1, :]

    scores = dot_nt(q, keys) + jnp.where(mult > 0.0, 0.0, ABSENT)
    top = jnp.max(scores, axis=1, keepdims=True)
    terms = jnp.exp2((scores - top) * (SCALE * LOG2E)) * mult
    probability = terms * (1.0 / jnp.sum(terms, axis=1, keepdims=True))
    weights = probability.astype(BF16)
    att = dot_nn(weights, values).astype(BF16)
    for r in range(0, att_ref.shape[0], BLK):
        att_ref[r:r + BLK] = att

    grad_weights = dot_nt(grad, values)
    delta = jnp.sum(probability * grad_weights, axis=1, keepdims=True)
    grad_scores = (probability * (grad_weights - delta) * SCALE).astype(BF16)
    dq_ref[...] = dot_nn(grad_scores, keys).astype(BF16)
    key_terms = dot_tn(grad_scores, q)
    value_terms = dot_tn(weights, grad)
    for (start, end), ref in zip(spans, sum_refs):
        ref[:, :HD] = key_terms[start:end].astype(ref.dtype)
        ref[:, HD:] = value_terms[start:end].astype(ref.dtype)


def attend(mult, q, grad, blocks, wide, copies):
    def body(*refs):
        attend_kernel(len(blocks), *refs)

    return pl.pallas_call(
        body,
        out_shape=(shape(copies * BLK, HD), shape(BLK, HD))
        + tuple(shape(*b.shape, kind=F32 if i < wide else BF16) for i, b in enumerate(blocks)),
        in_specs=[VMEM] * (3 + len(blocks)),
        out_specs=(VMEM,) * (2 + len(blocks)),
        scratch_shapes=[pltpu.VMEM((mult.shape[1], PAIR), BF16)],
        compiler_params=PARAMS,
        cost_estimate=cost(ATTEND_COST),
        name="attend",
    )(mult, q, grad, *blocks)


def half_rows():
    core = lax.axis_index("seq") & 1
    return pl.ds(pl.multiple_of(core * MARGIN, MARGIN), HD // 2)


def combine_kernel(own_ref, first_ref, near_ref, plus_ref, across_ref, whole_ref, half_ref,
                   own_out, first_out):
    near = near_ref[...].astype(F32)
    plus = plus_ref[...].astype(F32)
    across = across_ref[...].astype(F32)
    n = STRIDE_ROWS
    own_out[n:] = own_ref[n:] + near[n:BLK]
    own_out[:n] = own_ref[:n] + near[:n] + plus[:n] + across[:n]
    first_out[n:BLK] = first_ref[n:].astype(BF16)
    first_out[:n] = (first_ref[:n] + near[BLK:] + plus[n:] + across[n:]).astype(BF16)
    row = BLK
    for ref, rows in ((whole_ref, slice(0, HD)), (half_ref, half_rows())):
        for c in range(0, ref.shape[1], PAIR):
            piece = ref[rows, c:c + PAIR]
            first_out[row:row + piece.shape[0]] = piece
            row += piece.shape[0]


def combine(own, first, near, plus, across, whole, half):
    extra = (HD + HD // 2) * whole.shape[1] // PAIR
    return pl.pallas_call(
        combine_kernel,
        out_shape=(shape(BLK, PAIR, kind=F32), shape(BLK + extra, PAIR)),
        in_specs=[VMEM] * 7,
        out_specs=(VMEM,) * 2,
        compiler_params=PARAMS,
        cost_estimate=cost(COMBINE_COST),
        name="combine",
    )(own, first, near, plus, across, whole, half)


def settle(total, lead, dk_ref, dv_ref):
    for ref, c in ((dk_ref, 0), (dv_ref, HD)):
        ref[:STRIDE_ROWS] = lead[:, c:c + HD].astype(ref.dtype)
        ref[STRIDE_ROWS:] = total[STRIDE_ROWS:, c:c + HD].astype(ref.dtype)


def finish_ring_kernel(*refs):
    att_ref, mine_ref, whole_ref, half_ref, first_ref, own_ref, dq_ref = refs[:7]
    mixed_hbm, dq_hbm, dk_hbm, dv_hbm, mixed_ref, dk_ref, dv_ref, sems = refs[7:]
    copies = []

    def send(src, dst):
        copy = pltpu.make_async_copy(src, dst, sems.at[len(copies)])
        copy.start()
        copies.append(copy)

    send(dq_ref, dq_hbm)
    total = own_ref[...] + first_ref[:BLK].astype(F32)
    settle(total, total[:STRIDE_ROWS], dk_ref, dv_ref)
    send(dk_ref, dk_hbm)
    send(dv_ref, dv_hbm)
    head = lax.axis_index("head")
    att = [att_ref[head ^ r] for r in range(4)]
    core = lax.axis_index("seq") & 1
    half = HD // 2
    here = jnp.where(core == 0, att[1], att[2])
    there = jnp.where(core == 0, att[2], att[1])
    here_half = jnp.where(core == 0, att[3][:, :half], att[3][:, half:])
    there_half = jnp.where(core == 0, att[3][:, half:], att[3][:, :half])
    whole_row = BLK
    half_row = BLK + (mine_ref.shape[1] // PAIR) * HD
    for i, c in enumerate(range(0, mine_ref.shape[1], PAIR)):
        span = slice(c, c + PAIR)
        other_whole = first_ref[whole_row + i * HD:whole_row + (i + 1) * HD]
        other_half = first_ref[half_row + i * half:half_row + (i + 1) * half]
        mixed = dot_nn(att[0], mine_ref[:, span]) + dot_nn(here, whole_ref[:, span])
        mixed = mixed + dot_nn(there, other_whole) + dot_nn(here_half, half_ref[half_rows(), span])
        mixed = mixed + dot_nn(there_half, other_half)
        mixed_ref[:, span] = mixed.astype(mixed_ref.dtype)
        send(mixed_ref.at[:, pl.ds(c, PAIR)], mixed_hbm.at[:, pl.ds(c, PAIR)])
    for copy in copies:
        copy.wait()


def finish_ring(attentions, mine, whole, half, first, own, dq):
    width = mine.shape[1]
    return pl.pallas_call(
        finish_ring_kernel,
        out_shape=(shape(BLK, width),) + (shape(BLK, HD),) * 3,
        in_specs=[VMEM] * 7,
        out_specs=(HBM,) * 4,
        scratch_shapes=[
            pltpu.VMEM((BLK, width), BF16),
            pltpu.VMEM((BLK, HD), BF16),
            pltpu.VMEM((BLK, HD), BF16),
            pltpu.SemaphoreType.DMA((3 + width // PAIR,)),
        ],
        compiler_params=PARAMS,
        name="finish",
    )(attentions, mine, whole, half, first, own, dq)


def finish_kernel(count, *refs):
    att_refs = refs[:count]
    w_refs = refs[count:2 * count]
    own_ref, first_ref, second_ref, side_ref, mixed_ref, dk_ref, dv_ref = refs[2 * count:]
    mixed = None
    for ref, w in zip(att_refs, w_refs):
        term = dot_nn(ref[...], w[...])
        mixed = term if mixed is None else mixed + term
    mixed_ref[...] = mixed.astype(mixed_ref.dtype)
    total = own_ref[...] + first_ref[...].astype(F32) + second_ref[...].astype(F32)
    lead = total[:STRIDE_ROWS]
    for i in range(side_ref.shape[0] // STRIDE_ROWS):
        lead = lead + side_ref[i * STRIDE_ROWS:(i + 1) * STRIDE_ROWS].astype(F32)
    settle(total, lead, dk_ref, dv_ref)


def finish(attentions, slices, own, first, second, side):
    width = slices[0].shape[1]
    count = len(attentions)

    def body(*refs):
        finish_kernel(count, *refs)

    return pl.pallas_call(
        body,
        out_shape=(shape(BLK, width), shape(BLK, HD), shape(BLK, HD)),
        in_specs=[VMEM] * (2 * count + 4),
        out_specs=(VMEM,) * 3,
        compiler_params=PARAMS,
        name="finish",
    )(*attentions, *slices, own, first, second, side)


def spread_slice(array):
    seq = lax.axis_size("seq")
    heads = lax.axis_size("head")
    pairs = [(b * heads + h, b * heads + (h ^ (1 + b % 2))) for b in range(seq)
             for h in range(heads)]
    return lax.ppermute(array, ("seq", "head"), pairs)


def shards(queries, key_rows, value_rows, out_weight, strided_index, cotangent):
    seq = lax.axis_size("seq")
    heads = lax.axis_size("head")
    ring = seq == 8 and heads == 4
    n = STRIDE_ROWS
    side_rows = seq * n
    columns = 3 * BLK + side_rows
    own = jnp.concatenate([key_rows, value_rows], axis=1)
    first = trade(own, 1)
    grad, mult, *slices = prepare(
        ring, strided_index, cotangent, out_weight, heads, columns, own
    )
    if ring:
        mine, whole, half = slices
        half = swap(half, 3)
        near, pair, whole = leads(own, first, mult, whole)
        whole = spread_slice(whole)
        near = trade(near, -1)
        blocks = (own, first, near, trade(pair, 3), trade(pair, 4))
        att, dq, own_sum, first_sum, to_near, to_plus, to_across = attend(
            mult, queries, grad, blocks, 2, heads
        )
        attentions = lax.all_to_all(att.reshape(heads, BLK, HD), "head", 0, 0)
        own_sum, to_first = combine(
            own_sum, first_sum, trade(to_near, -1), trade(to_plus, 3), trade(to_across, 4),
            whole, half,
        )
        mixed, dq, dk, dv = finish_ring(
            attentions, mine, whole, half, trade(to_first, 1), own_sum, dq
        )
    else:
        second = trade(own, -1)
        slices = [slices[0]] + [swap(slices[r], r) for r in range(1, heads)]
        spread = jnp.broadcast_to(own[None, :n], (seq, n, PAIR))
        side = lax.all_to_all(spread, "seq", 0, 0).reshape(side_rows, PAIR)
        att, dq, own_sum, to_first, to_second, to_side = attend(
            mult, queries, grad, (own, first, second, side), 1, 1
        )
        from_side = lax.all_to_all(to_side.reshape(seq, n, PAIR), "seq", 0, 0)
        mixed, dk, dv = finish(
            [att] + [swap(att, r) for r in range(1, heads)], slices, own_sum,
            trade(to_first, 1), trade(to_second, -1), from_side.reshape(side_rows, PAIR),
        )
    return (mixed, dq, dk, dv)


def solution(mesh):
    in_specs = (
        P("seq", "head"),
        P("seq", "head"),
        P("seq", "head"),
        P("head", None),
        P("seq", None),
        P("seq", None),
    )
    out_specs = (P("seq", "head"), P("seq", "head"), P("seq", "head"), P("seq", "head"))
    return jax.shard_map(shards, mesh=mesh, in_specs=in_specs, out_specs=out_specs, check_vma=False)
```

```python
import jax
import jax.numpy as jnp
from jax import lax
from jax.experimental import pallas as pl
from jax.experimental.pallas import tpu as pltpu
from jax.sharding import PartitionSpec as P

HD = 128
BLK = 128
STRIDE_ROWS = 32
MARGIN = 16
PAIR = 2 * HD
SCALE = HD ** (-0.5)
LOG2E = 1.4426950408889634
ABSENT = -1e30
VMEM = pl.BlockSpec(memory_space=pltpu.VMEM)
HBM = pl.BlockSpec(memory_space=pltpu.HBM)
PARAMS = pltpu.CompilerParams(vmem_limit_bytes=40 * 1024 * 1024)
FULL = pltpu.CompilerParams(vmem_limit_bytes=int(53.3 * 1024 * 1024))
BF16 = jnp.bfloat16
PREPARE_COST = 10**10
ATTEND_COST = 10**10
COMBINE_COST = 10**10
GATHER_COST = 10**10
F32 = jnp.float32


def dot_nt(a, b):
    return lax.dot_general(a, b, (((1,), (1,)), ((), ())), preferred_element_type=F32)


def dot_nn(a, b):
    return lax.dot_general(a, b, (((1,), (0,)), ((), ())), preferred_element_type=F32)


def dot_tn(a, b):
    return lax.dot_general(a, b, (((0,), (0,)), ((), ())), preferred_element_type=F32)


def shape(*dims, kind=BF16):
    return jax.ShapeDtypeStruct(dims, kind)


def trade(array, step):
    count = lax.axis_size("seq")
    return lax.ppermute(
        array, "seq", [(i, (i + (step if i % 2 == 0 else -step)) % count) for i in range(count)]
    )


def swap(array, mask):
    count = lax.axis_size("head")
    return lax.ppermute(array, "head", [(i, i ^ mask) for i in range(count)])


def count_of(picks, group):
    total = jnp.int32(0)
    for pick in picks:
        total = total + jnp.where(pick == group, 1, 0)
    return total.astype(F32)


def fill_multiplicity(ring, index_ref, mult_ref):
    per_block = BLK // STRIDE_ROWS
    picks = [index_ref[0, i] for i in range(index_ref.shape[1])]
    shape_of = mult_ref.shape
    lane = lax.broadcasted_iota(jnp.int32, shape_of, 1)
    mult = jnp.where(lane < 3 * BLK, 1.0, 0.0)
    if ring:
        b = lax.axis_index("seq")
        sign = 1 - 2 * (b & 1)
        counts = [count_of(picks, j) for j in range(2)]
        places = [(0, 0), (BLK, 1), (2 * BLK, -1)]
        places += [(3 * BLK + i * STRIDE_ROWS, o) for i, o in enumerate((-2, 3, 2, 4, 5))]
        for start, offset in places:
            owner = (b + 16 + sign * offset) & 7
            count = jnp.where(owner < per_block, counts[0], counts[1])
            inside = (lane >= start) & (lane < start + STRIDE_ROWS)
            mult = mult + jnp.where(inside, count, 0.0)
    else:
        for j in range((shape_of[1] - 3 * BLK) // BLK):
            start = (3 + j) * BLK
            inside = (lane >= start) & (lane < start + BLK)
            mult = mult + jnp.where(inside, count_of(picks, j), 0.0)
    mult_ref[...] = mult


def cost(flops):
    return pl.CostEstimate(flops=flops, bytes_accessed=0, transcendentals=0)


CHUNKS = 4


def prepare_kernel(ring, index_hbm, cot_hbm, w_hbm, after_ref, grad_ref, mult_ref, *refs):
    del after_ref
    index_ref, cot_ref, w_ref, sems = refs[-4:]
    slice_refs = refs[:-4]
    copies = [(index_hbm, index_ref)]
    depth = cot_ref.shape[1] // CHUNKS
    for i in range(CHUNKS):
        span = pl.ds(i * depth, depth)
        copies.append((w_hbm.at[:, span], w_ref.at[:, span]))
        copies.append((cot_hbm.at[:, span], cot_ref.at[:, span]))
    copies = [pltpu.make_async_copy(src, dst, sems.at[i]) for i, (src, dst) in enumerate(copies)]
    for copy in copies:
        copy.start()
    copies[0].wait()
    fill_multiplicity(ring, index_ref, mult_ref)
    total = None
    for i in range(CHUNKS):
        copies[1 + 2 * i].wait()
        copies[2 + 2 * i].wait()
        span = slice(i * depth, (i + 1) * depth)
        term = dot_nt(cot_ref[:, span], w_ref[:, span])
        total = term if total is None else total + term
    grad_ref[...] = total.astype(grad_ref.dtype)

    width = slice_refs[0].shape[1]
    head = lax.axis_index("head")

    def columns(h):
        return pl.ds(pl.multiple_of(h * width, width), width)

    if ring:
        core = lax.axis_index("seq") & 1
        half = HD // 2
        mine_ref, whole_ref, half_ref = slice_refs
        mine_ref[...] = w_ref[:, columns(head)]
        whole_ref[...] = w_ref[:, columns(head ^ (1 + core))]
        rows = pl.ds(pl.multiple_of(core * (half - MARGIN), MARGIN), half + MARGIN)
        half_ref[...] = w_ref[rows, columns(head ^ 3)]
    else:
        for r, ref in enumerate(slice_refs):
            ref[...] = w_ref[:, columns(head ^ r)]


def prepare(ring, index, cotangent, out_weight, heads, columns, after):
    width = out_weight.shape[1] // heads
    rows = (HD, HD, HD // 2 + MARGIN) if ring else (HD,) * heads

    def body(*refs):
        prepare_kernel(ring, *refs)

    return pl.pallas_call(
        body,
        out_shape=(shape(BLK, HD), shape(8, columns, kind=F32))
        + tuple(shape(r, width) for r in rows),
        in_specs=[HBM] * 3 + [VMEM],
        out_specs=(VMEM,) * (2 + len(rows)),
        scratch_shapes=[
            pltpu.SMEM(index.shape, jnp.int32),
            pltpu.VMEM(cotangent.shape, BF16),
            pltpu.VMEM(out_weight.shape, BF16),
            pltpu.SemaphoreType.DMA((1 + 2 * CHUNKS,)),
        ],
        compiler_params=FULL,
        cost_estimate=cost(PREPARE_COST),
        name="prepare",
    )(index, cotangent, out_weight, after)


def lead_kernel(own_ref, first_ref, mult_ref, whole_ref, near_ref, pair_ref, whole_out):
    del mult_ref
    n = STRIDE_ROWS
    near_ref[:BLK] = own_ref[...]
    near_ref[BLK:] = first_ref[:n]
    pair_ref[:n] = own_ref[:n]
    pair_ref[n:] = first_ref[:n]
    whole_out[...] = whole_ref[...]


def leads(own, first, mult, whole):
    n = STRIDE_ROWS
    return pl.pallas_call(
        lead_kernel,
        out_shape=(shape(BLK + n, PAIR), shape(2 * n, PAIR), shape(*whole.shape)),
        in_specs=[VMEM] * 4,
        out_specs=(VMEM,) * 3,
        compiler_params=PARAMS,
        name="leads",
    )(own, first, mult, whole)


def attend_kernel(blocks, mult_ref, q_ref, grad_ref, *refs):
    block_refs = refs[:blocks]
    att_ref, dq_ref = refs[blocks:blocks + 2]
    sum_refs = refs[blocks + 2:2 * blocks + 2]
    keys_ref = refs[-1]
    total_rows = keys_ref.shape[0]
    spans = []
    row = 0
    for ref in block_refs:
        spans.append((row, row + ref.shape[0]))
        keys_ref[row:row + ref.shape[0], :] = ref[...]
        row += ref.shape[0]
    if row < total_rows:
        keys_ref[row:, :] = jnp.zeros((total_rows - row, PAIR), BF16)
    keys = keys_ref[:, :HD]
    values = keys_ref[:, HD:]
    q = q_ref[...]
    grad = grad_ref[...]
    mult = mult_ref[0:1, :]

    scores = dot_nt(q, keys) + jnp.where(mult > 0.0, 0.0, ABSENT)
    top = jnp.max(scores, axis=1, keepdims=True)
    terms = jnp.exp2((scores - top) * (SCALE * LOG2E)) * mult
    probability = terms * (1.0 / jnp.sum(terms, axis=1, keepdims=True))
    weights = probability.astype(BF16)
    att_ref[...] = dot_nn(weights, values).astype(BF16)

    grad_weights = dot_nt(grad, values)
    delta = jnp.sum(probability * grad_weights, axis=1, keepdims=True)
    grad_scores = (probability * (grad_weights - delta) * SCALE).astype(BF16)
    dq_ref[...] = dot_nn(grad_scores, keys).astype(BF16)
    key_terms = dot_tn(grad_scores, q)
    value_terms = dot_tn(weights, grad)
    for (start, end), ref in zip(spans, sum_refs):
        ref[:, :HD] = key_terms[start:end].astype(ref.dtype)
        ref[:, HD:] = value_terms[start:end].astype(ref.dtype)


def attend(mult, q, grad, blocks, wide):
    def body(*refs):
        attend_kernel(len(blocks), *refs)

    return pl.pallas_call(
        body,
        out_shape=(shape(BLK, HD), shape(BLK, HD))
        + tuple(shape(*b.shape, kind=F32 if i < wide else BF16) for i, b in enumerate(blocks)),
        in_specs=[VMEM] * (3 + len(blocks)),
        out_specs=(VMEM,) * (2 + len(blocks)),
        scratch_shapes=[pltpu.VMEM((mult.shape[1], PAIR), BF16)],
        compiler_params=PARAMS,
        cost_estimate=cost(ATTEND_COST),
        name="attend",
    )(mult, q, grad, *blocks)


def half_rows():
    core = lax.axis_index("seq") & 1
    return pl.ds(pl.multiple_of(core * MARGIN, MARGIN), HD // 2)


def combine_kernel(own_ref, first_ref, near_ref, plus_ref, across_ref, whole_ref, half_ref,
                   att_ref, own_out, first_out, att_out):
    near = near_ref[...].astype(F32)
    plus = plus_ref[...].astype(F32)
    across = across_ref[...].astype(F32)
    n = STRIDE_ROWS
    own_out[n:] = own_ref[n:] + near[n:BLK]
    own_out[:n] = own_ref[:n] + near[:n] + plus[:n] + across[:n]
    first_out[n:BLK] = first_ref[n:].astype(BF16)
    first_out[:n] = (first_ref[:n] + near[BLK:] + plus[n:] + across[n:]).astype(BF16)
    att_out[...] = att_ref[...]
    row = BLK
    for ref, rows in ((whole_ref, slice(0, HD)), (half_ref, half_rows())):
        for c in range(0, ref.shape[1], PAIR):
            piece = ref[rows, c:c + PAIR]
            first_out[row:row + piece.shape[0]] = piece
            row += piece.shape[0]


def combine(own, first, near, plus, across, whole, half, att):
    extra = (HD + HD // 2) * whole.shape[1] // PAIR
    return pl.pallas_call(
        combine_kernel,
        out_shape=(shape(BLK, PAIR, kind=F32), shape(BLK + extra, PAIR), shape(BLK, HD)),
        in_specs=[VMEM] * 8,
        out_specs=(VMEM,) * 3,
        compiler_params=PARAMS,
        cost_estimate=cost(COMBINE_COST),
        name="combine",
    )(own, first, near, plus, across, whole, half, att)


def gather_kernel(*refs):
    for r, ref in enumerate(refs[:-1]):
        refs[-1][:, r * HD:(r + 1) * HD] = ref[...]


def gather(attentions):
    return pl.pallas_call(
        gather_kernel,
        out_shape=shape(BLK, len(attentions) * HD),
        in_specs=[VMEM] * len(attentions),
        out_specs=VMEM,
        compiler_params=PARAMS,
        cost_estimate=cost(GATHER_COST),
        name="gather",
    )(*attentions)


def settle(total, lead, dk_ref, dv_ref):
    for ref, c in ((dk_ref, 0), (dv_ref, HD)):
        ref[:STRIDE_ROWS] = lead[:, c:c + HD].astype(ref.dtype)
        ref[STRIDE_ROWS:] = total[STRIDE_ROWS:, c:c + HD].astype(ref.dtype)


def finish_ring_kernel(*refs):
    att_ref, beside_ref, far_ref = refs[:3]
    mine_ref, whole_ref, half_ref, first_ref, own_ref, dq_ref = refs[3:9]
    mixed_hbm, dq_hbm, dk_hbm, dv_hbm, mixed_ref, dk_ref, dv_ref, sems = refs[9:]
    copies = []

    def send(src, dst):
        copy = pltpu.make_async_copy(src, dst, sems.at[len(copies)])
        copy.start()
        copies.append(copy)

    send(dq_ref, dq_hbm)
    total = own_ref[...] + first_ref[:BLK].astype(F32)
    settle(total, total[:STRIDE_ROWS], dk_ref, dv_ref)
    send(dk_ref, dk_hbm)
    send(dv_ref, dv_hbm)
    att = [att_ref[...], beside_ref[...], far_ref[:, :HD], far_ref[:, HD:]]
    core = lax.axis_index("seq") & 1
    half = HD // 2
    here = jnp.where(core == 0, att[1], att[2])
    there = jnp.where(core == 0, att[2], att[1])
    here_half = jnp.where(core == 0, att[3][:, :half], att[3][:, half:])
    there_half = jnp.where(core == 0, att[3][:, half:], att[3][:, :half])
    whole_row = BLK
    half_row = BLK + (mine_ref.shape[1] // PAIR) * HD
    for i, c in enumerate(range(0, mine_ref.shape[1], PAIR)):
        span = slice(c, c + PAIR)
        other_whole = first_ref[whole_row + i * HD:whole_row + (i + 1) * HD]
        other_half = first_ref[half_row + i * half:half_row + (i + 1) * half]
        mixed = dot_nn(att[0], mine_ref[:, span]) + dot_nn(here, whole_ref[:, span])
        mixed = mixed + dot_nn(there, other_whole) + dot_nn(here_half, half_ref[half_rows(), span])
        mixed = mixed + dot_nn(there_half, other_half)
        mixed_ref[:, span] = mixed.astype(mixed_ref.dtype)
        send(mixed_ref.at[:, pl.ds(c, PAIR)], mixed_hbm.at[:, pl.ds(c, PAIR)])
    for copy in copies:
        copy.wait()


def finish_ring(attentions, mine, whole, half, first, own, dq):
    width = mine.shape[1]
    return pl.pallas_call(
        finish_ring_kernel,
        out_shape=(shape(BLK, width),) + (shape(BLK, HD),) * 3,
        in_specs=[VMEM] * 9,
        out_specs=(HBM,) * 4,
        scratch_shapes=[
            pltpu.VMEM((BLK, width), BF16),
            pltpu.VMEM((BLK, HD), BF16),
            pltpu.VMEM((BLK, HD), BF16),
            pltpu.SemaphoreType.DMA((3 + width // PAIR,)),
        ],
        compiler_params=PARAMS,
        name="finish",
    )(*attentions, mine, whole, half, first, own, dq)


def finish_kernel(count, *refs):
    att_refs = refs[:count]
    w_refs = refs[count:2 * count]
    own_ref, first_ref, second_ref, side_ref, mixed_ref, dk_ref, dv_ref = refs[2 * count:]
    mixed = None
    for ref, w in zip(att_refs, w_refs):
        term = dot_nn(ref[...], w[...])
        mixed = term if mixed is None else mixed + term
    mixed_ref[...] = mixed.astype(mixed_ref.dtype)
    total = own_ref[...] + first_ref[...].astype(F32) + second_ref[...].astype(F32)
    lead = total[:STRIDE_ROWS]
    for i in range(side_ref.shape[0] // STRIDE_ROWS):
        lead = lead + side_ref[i * STRIDE_ROWS:(i + 1) * STRIDE_ROWS].astype(F32)
    settle(total, lead, dk_ref, dv_ref)


def finish(attentions, slices, own, first, second, side):
    width = slices[0].shape[1]
    count = len(attentions)

    def body(*refs):
        finish_kernel(count, *refs)

    return pl.pallas_call(
        body,
        out_shape=(shape(BLK, width), shape(BLK, HD), shape(BLK, HD)),
        in_specs=[VMEM] * (2 * count + 4),
        out_specs=(VMEM,) * 3,
        compiler_params=PARAMS,
        name="finish",
    )(*attentions, *slices, own, first, second, side)


def spread_slice(array):
    seq = lax.axis_size("seq")
    heads = lax.axis_size("head")
    pairs = [(b * heads + h, b * heads + (h ^ (1 + b % 2))) for b in range(seq)
             for h in range(heads)]
    return lax.ppermute(array, ("seq", "head"), pairs)


def shards(queries, key_rows, value_rows, out_weight, strided_index, cotangent):
    seq = lax.axis_size("seq")
    heads = lax.axis_size("head")
    ring = seq == 8 and heads == 4
    n = STRIDE_ROWS
    side_rows = seq * n
    columns = 3 * BLK + side_rows
    own = jnp.concatenate([key_rows, value_rows], axis=1)
    first = trade(own, 1)
    grad, mult, *slices = prepare(
        ring, strided_index, cotangent, out_weight, heads, columns, own
    )
    if ring:
        mine, whole, half = slices
        half = swap(half, 3)
        near, pair, whole = leads(own, first, mult, whole)
        whole = spread_slice(whole)
        near = trade(near, -1)
        blocks = (own, first, near, trade(pair, 3), trade(pair, 4))
        att, dq, own_sum, first_sum, to_near, to_plus, to_across = attend(
            mult, queries, grad, blocks, 2
        )
        far = gather([swap(att, 2), swap(att, 3)])
        own_sum, to_first, last = combine(
            own_sum, first_sum, trade(to_near, -1), trade(to_plus, 3), trade(to_across, 4),
            whole, half, att,
        )
        mixed, dq, dk, dv = finish_ring(
            (att, swap(last, 1), far), mine, whole, half, trade(to_first, 1), own_sum, dq
        )
    else:
        second = trade(own, -1)
        slices = [slices[0]] + [swap(slices[r], r) for r in range(1, heads)]
        spread = jnp.broadcast_to(own[None, :n], (seq, n, PAIR))
        side = lax.all_to_all(spread, "seq", 0, 0).reshape(side_rows, PAIR)
        att, dq, own_sum, to_first, to_second, to_side = attend(
            mult, queries, grad, (own, first, second, side), 1
        )
        from_side = lax.all_to_all(to_side.reshape(seq, n, PAIR), "seq", 0, 0)
        mixed, dk, dv = finish(
            [att] + [swap(att, r) for r in range(1, heads)], slices, own_sum,
            trade(to_first, 1), trade(to_second, -1), from_side.reshape(side_rows, PAIR),
        )
    return (mixed, dq, dk, dv)


def solution(mesh):
    in_specs = (
        P("seq", "head"),
        P("seq", "head"),
        P("seq", "head"),
        P("head", None),
        P("seq", None),
        P("seq", None),
    )
    out_specs = (P("seq", "head"), P("seq", "head"), P("seq", "head"), P("seq", "head"))
    return jax.shard_map(shards, mesh=mesh, in_specs=in_specs, out_specs=out_specs, check_vma=False)
```

```python
import jax
import jax.numpy as jnp
from jax import lax
from jax.experimental import pallas as pl
from jax.experimental.pallas import tpu as pltpu
from jax.sharding import PartitionSpec as P

HD = 128
BLK = 128
STRIDE_ROWS = 32
MARGIN = 16
PAIR = 2 * HD
SCALE = HD ** (-0.5)
LOG2E = 1.4426950408889634
ABSENT = -1e30
VMEM = pl.BlockSpec(memory_space=pltpu.VMEM)
HBM = pl.BlockSpec(memory_space=pltpu.HBM)
PARAMS = pltpu.CompilerParams(vmem_limit_bytes=40 * 1024 * 1024)
FULL = pltpu.CompilerParams(vmem_limit_bytes=int(53.3 * 1024 * 1024))
BF16 = jnp.bfloat16
PREPARE_COST = 10**10
ATTEND_COST = 10**10
COMBINE_COST = 10**10
GATHER_COST = 10**10
F32 = jnp.float32


def dot_nt(a, b):
    return lax.dot_general(a, b, (((1,), (1,)), ((), ())), preferred_element_type=F32)


def dot_nn(a, b):
    return lax.dot_general(a, b, (((1,), (0,)), ((), ())), preferred_element_type=F32)


def dot_tn(a, b):
    return lax.dot_general(a, b, (((0,), (0,)), ((), ())), preferred_element_type=F32)


def shape(*dims, kind=BF16):
    return jax.ShapeDtypeStruct(dims, kind)


def trade(array, step):
    count = lax.axis_size("seq")
    return lax.ppermute(
        array, "seq", [(i, (i + (step if i % 2 == 0 else -step)) % count) for i in range(count)]
    )


def swap(array, mask):
    count = lax.axis_size("head")
    return lax.ppermute(array, "head", [(i, i ^ mask) for i in range(count)])


def count_of(picks, group):
    total = jnp.int32(0)
    for pick in picks:
        total = total + jnp.where(pick == group, 1, 0)
    return total.astype(F32)


def fill_multiplicity(ring, index_ref, mult_ref):
    per_block = BLK // STRIDE_ROWS
    picks = [index_ref[0, i] for i in range(index_ref.shape[1])]
    shape_of = mult_ref.shape
    lane = lax.broadcasted_iota(jnp.int32, shape_of, 1)
    mult = jnp.where(lane < 3 * BLK, 1.0, 0.0)
    if ring:
        b = lax.axis_index("seq")
        sign = 1 - 2 * (b & 1)
        counts = [count_of(picks, j) for j in range(2)]
        places = [(0, 0), (BLK, 1), (2 * BLK, -1)]
        places += [(3 * BLK + i * STRIDE_ROWS, o) for i, o in enumerate((-2, 3, 2, 4, 5))]
        for start, offset in places:
            owner = (b + 16 + sign * offset) & 7
            count = jnp.where(owner < per_block, counts[0], counts[1])
            inside = (lane >= start) & (lane < start + STRIDE_ROWS)
            mult = mult + jnp.where(inside, count, 0.0)
    else:
        for j in range((shape_of[1] - 3 * BLK) // BLK):
            start = (3 + j) * BLK
            inside = (lane >= start) & (lane < start + BLK)
            mult = mult + jnp.where(inside, count_of(picks, j), 0.0)
    mult_ref[...] = mult


def cost(flops):
    return pl.CostEstimate(flops=flops, bytes_accessed=0, transcendentals=0)


CHUNKS = 4


def prepare_kernel(ring, index_hbm, cot_hbm, w_hbm, after_ref, grad_ref, mult_ref, *refs):
    del after_ref
    index_ref, cot_ref, w_ref, sems = refs[-4:]
    slice_refs = refs[:-4]
    copies = [(index_hbm, index_ref)]
    depth = cot_ref.shape[1] // CHUNKS
    for i in range(CHUNKS):
        span = pl.ds(i * depth, depth)
        copies.append((w_hbm.at[:, span], w_ref.at[:, span]))
        copies.append((cot_hbm.at[:, span], cot_ref.at[:, span]))
    copies = [pltpu.make_async_copy(src, dst, sems.at[i]) for i, (src, dst) in enumerate(copies)]
    for copy in copies:
        copy.start()
    copies[0].wait()
    fill_multiplicity(ring, index_ref, mult_ref)
    total = None
    for i in range(CHUNKS):
        copies[1 + 2 * i].wait()
        copies[2 + 2 * i].wait()
        span = slice(i * depth, (i + 1) * depth)
        term = dot_nt(cot_ref[:, span], w_ref[:, span])
        total = term if total is None else total + term
    grad_ref[...] = total.astype(grad_ref.dtype)

    width = slice_refs[0].shape[1]
    head = lax.axis_index("head")

    def columns(h):
        return pl.ds(pl.multiple_of(h * width, width), width)

    if ring:
        core = lax.axis_index("seq") & 1
        half = HD // 2
        mine_ref, whole_ref, half_ref = slice_refs
        mine_ref[...] = w_ref[:, columns(head)]
        whole_ref[...] = w_ref[:, columns(head ^ (1 + core))]
        rows = pl.ds(pl.multiple_of(core * (half - MARGIN), MARGIN), half + MARGIN)
        half_ref[...] = w_ref[rows, columns(head ^ 3)]
    else:
        for r, ref in enumerate(slice_refs):
            ref[...] = w_ref[:, columns(head ^ r)]


def prepare(ring, index, cotangent, out_weight, heads, columns, after):
    width = out_weight.shape[1] // heads
    rows = (HD, HD, HD // 2 + MARGIN) if ring else (HD,) * heads

    def body(*refs):
        prepare_kernel(ring, *refs)

    return pl.pallas_call(
        body,
        out_shape=(shape(BLK, HD), shape(8, columns, kind=F32))
        + tuple(shape(r, width) for r in rows),
        in_specs=[HBM] * 3 + [VMEM],
        out_specs=(VMEM,) * (2 + len(rows)),
        scratch_shapes=[
            pltpu.SMEM(index.shape, jnp.int32),
            pltpu.VMEM(cotangent.shape, BF16),
            pltpu.VMEM(out_weight.shape, BF16),
            pltpu.SemaphoreType.DMA((1 + 2 * CHUNKS,)),
        ],
        compiler_params=FULL,
        cost_estimate=cost(PREPARE_COST),
        name="prepare",
    )(index, cotangent, out_weight, after)


def lead_kernel(own_ref, first_ref, mult_ref, whole_ref, near_ref, pair_ref, whole_out):
    del mult_ref
    n = STRIDE_ROWS
    near_ref[:BLK] = own_ref[...]
    near_ref[BLK:] = first_ref[:n]
    pair_ref[:n] = own_ref[:n]
    pair_ref[n:] = first_ref[:n]
    whole_out[...] = whole_ref[...]


def leads(own, first, mult, whole):
    n = STRIDE_ROWS
    return pl.pallas_call(
        lead_kernel,
        out_shape=(shape(BLK + n, PAIR), shape(2 * n, PAIR), shape(*whole.shape)),
        in_specs=[VMEM] * 4,
        out_specs=(VMEM,) * 3,
        compiler_params=PARAMS,
        name="leads",
    )(own, first, mult, whole)


def attend_kernel(blocks, pieces, mult_ref, q_ref, grad_ref, *refs):
    block_refs = refs[:blocks]
    att_ref, dq_ref = refs[blocks:blocks + 2]
    sum_refs = refs[blocks + 2:-1]
    keys_ref = refs[-1]
    total_rows = keys_ref.shape[0]
    row = 0
    for ref in block_refs:
        keys_ref[row:row + ref.shape[0], :] = ref[...]
        row += ref.shape[0]
    if row < total_rows:
        keys_ref[row:, :] = jnp.zeros((total_rows - row, PAIR), BF16)
    keys = keys_ref[:, :HD]
    values = keys_ref[:, HD:]
    q = q_ref[...]
    grad = grad_ref[...]
    mult = mult_ref[0:1, :]

    scores = dot_nt(q, keys) + jnp.where(mult > 0.0, 0.0, ABSENT)
    top = jnp.max(scores, axis=1, keepdims=True)
    terms = jnp.exp2((scores - top) * (SCALE * LOG2E)) * mult
    probability = terms * (1.0 / jnp.sum(terms, axis=1, keepdims=True))
    weights = probability.astype(BF16)
    att_ref[...] = dot_nn(weights, values).astype(BF16)

    grad_weights = dot_nt(grad, values)
    delta = jnp.sum(probability * grad_weights, axis=1, keepdims=True)
    grad_scores = (probability * (grad_weights - delta) * SCALE).astype(BF16)
    dq_ref[...] = dot_nn(grad_scores, keys).astype(BF16)
    key_terms = dot_tn(grad_scores, q)
    value_terms = dot_tn(weights, grad)
    for spans, ref in zip(pieces, sum_refs):
        row = 0
        for start, end in spans:
            rows = slice(row, row + end - start)
            ref[rows, :HD] = key_terms[start:end].astype(ref.dtype)
            ref[rows, HD:] = value_terms[start:end].astype(ref.dtype)
            row += end - start


def attend(mult, q, grad, blocks, pieces, wide):
    def body(*refs):
        attend_kernel(len(blocks), pieces, *refs)

    sums = []
    for i, spans in enumerate(pieces):
        rows = sum(end - start for start, end in spans)
        sums.append(shape(rows, PAIR, kind=F32 if i < wide else BF16))
    return pl.pallas_call(
        body,
        out_shape=(shape(BLK, HD), shape(BLK, HD), *sums),
        in_specs=[VMEM] * (3 + len(blocks)),
        out_specs=(VMEM,) * (2 + len(sums)),
        scratch_shapes=[pltpu.VMEM((mult.shape[1], PAIR), BF16)],
        compiler_params=PARAMS,
        cost_estimate=cost(ATTEND_COST),
        name="attend",
    )(mult, q, grad, *blocks)


def half_rows():
    core = lax.axis_index("seq") & 1
    return pl.ds(pl.multiple_of(core * MARGIN, MARGIN), HD // 2)


def combine_kernel(own_ref, first_ref, second_ref, plus_ref, minus_ref, whole_ref, half_ref,
                   att_ref, own_out, first_out, second_out, att_out):
    plus = plus_ref[...].astype(F32)
    minus = minus_ref[...].astype(F32)
    n = STRIDE_ROWS
    own_out[n:] = own_ref[n:]
    own_out[:n] = own_ref[:n] + plus[:n] + minus[:n]
    second_out[n:] = second_ref[n:].astype(BF16)
    second_out[:n] = (second_ref[:n] + plus[2 * n:] + minus[n:]).astype(BF16)
    first_out[n:BLK] = first_ref[n:].astype(BF16)
    first_out[:n] = (first_ref[:n] + plus[n:2 * n]).astype(BF16)
    att_out[...] = att_ref[...]
    row = BLK
    for ref, rows in ((whole_ref, slice(0, HD)), (half_ref, half_rows())):
        for c in range(0, ref.shape[1], PAIR):
            piece = ref[rows, c:c + PAIR]
            first_out[row:row + piece.shape[0]] = piece
            row += piece.shape[0]


def combine(own, first, second, plus, minus, whole, half, att):
    extra = (HD + HD // 2) * whole.shape[1] // PAIR
    return pl.pallas_call(
        combine_kernel,
        out_shape=(shape(BLK, PAIR, kind=F32), shape(BLK + extra, PAIR), shape(BLK, PAIR),
                   shape(BLK, HD)),
        in_specs=[VMEM] * 8,
        out_specs=(VMEM,) * 4,
        compiler_params=PARAMS,
        cost_estimate=cost(COMBINE_COST),
        name="combine",
    )(own, first, second, plus, minus, whole, half, att)


def gather_kernel(*refs):
    for r, ref in enumerate(refs[:-1]):
        refs[-1][:, r * HD:(r + 1) * HD] = ref[...]


def gather(attentions):
    return pl.pallas_call(
        gather_kernel,
        out_shape=shape(BLK, len(attentions) * HD),
        in_specs=[VMEM] * len(attentions),
        out_specs=VMEM,
        compiler_params=PARAMS,
        cost_estimate=cost(GATHER_COST),
        name="gather",
    )(*attentions)


def settle(total, lead, dk_ref, dv_ref):
    for ref, c in ((dk_ref, 0), (dv_ref, HD)):
        ref[:STRIDE_ROWS] = lead[:, c:c + HD].astype(ref.dtype)
        ref[STRIDE_ROWS:] = total[STRIDE_ROWS:, c:c + HD].astype(ref.dtype)


def finish_ring_kernel(*refs):
    att_ref, near_ref, far_ref, mine_ref, whole_ref, half_ref = refs[:6]
    first_ref, own_ref, second_ref, dq_ref = refs[6:10]
    mixed_hbm, dq_hbm, dk_hbm, dv_hbm, mixed_ref, dk_ref, dv_ref, sems = refs[10:]
    copies = []

    def send(src, dst):
        copy = pltpu.make_async_copy(src, dst, sems.at[len(copies)])
        copy.start()
        copies.append(copy)

    send(dq_ref, dq_hbm)
    total = own_ref[...] + first_ref[:BLK].astype(F32) + second_ref[...].astype(F32)
    settle(total, total[:STRIDE_ROWS], dk_ref, dv_ref)
    send(dk_ref, dk_hbm)
    send(dv_ref, dv_hbm)
    att = [att_ref[...], near_ref[...], far_ref[:, :HD], far_ref[:, HD:]]
    core = lax.axis_index("seq") & 1
    half = HD // 2
    here = jnp.where(core == 0, att[1], att[2])
    there = jnp.where(core == 0, att[2], att[1])
    here_half = jnp.where(core == 0, att[3][:, :half], att[3][:, half:])
    there_half = jnp.where(core == 0, att[3][:, half:], att[3][:, :half])
    whole_row = BLK
    half_row = BLK + (mine_ref.shape[1] // PAIR) * HD
    for i, c in enumerate(range(0, mine_ref.shape[1], PAIR)):
        span = slice(c, c + PAIR)
        other_whole = first_ref[whole_row + i * HD:whole_row + (i + 1) * HD]
        other_half = first_ref[half_row + i * half:half_row + (i + 1) * half]
        mixed = dot_nn(att[0], mine_ref[:, span]) + dot_nn(here, whole_ref[:, span])
        mixed = mixed + dot_nn(there, other_whole) + dot_nn(here_half, half_ref[half_rows(), span])
        mixed = mixed + dot_nn(there_half, other_half)
        mixed_ref[:, span] = mixed.astype(mixed_ref.dtype)
        send(mixed_ref.at[:, pl.ds(c, PAIR)], mixed_hbm.at[:, pl.ds(c, PAIR)])
    for copy in copies:
        copy.wait()


def finish_ring(attentions, mine, whole, half, first, own, second, dq):
    width = mine.shape[1]
    return pl.pallas_call(
        finish_ring_kernel,
        out_shape=(shape(BLK, width),) + (shape(BLK, HD),) * 3,
        in_specs=[VMEM] * 10,
        out_specs=(HBM,) * 4,
        scratch_shapes=[
            pltpu.VMEM((BLK, width), BF16),
            pltpu.VMEM((BLK, HD), BF16),
            pltpu.VMEM((BLK, HD), BF16),
            pltpu.SemaphoreType.DMA((3 + width // PAIR,)),
        ],
        compiler_params=PARAMS,
        name="finish",
    )(*attentions, mine, whole, half, first, own, second, dq)


def finish_kernel(count, *refs):
    att_refs = refs[:count]
    w_refs = refs[count:2 * count]
    own_ref, first_ref, second_ref, side_ref, mixed_ref, dk_ref, dv_ref = refs[2 * count:]
    mixed = None
    for ref, w in zip(att_refs, w_refs):
        term = dot_nn(ref[...], w[...])
        mixed = term if mixed is None else mixed + term
    mixed_ref[...] = mixed.astype(mixed_ref.dtype)
    total = own_ref[...] + first_ref[...].astype(F32) + second_ref[...].astype(F32)
    lead = total[:STRIDE_ROWS]
    for i in range(side_ref.shape[0] // STRIDE_ROWS):
        lead = lead + side_ref[i * STRIDE_ROWS:(i + 1) * STRIDE_ROWS].astype(F32)
    settle(total, lead, dk_ref, dv_ref)


def finish(attentions, slices, own, first, second, side):
    width = slices[0].shape[1]
    count = len(attentions)

    def body(*refs):
        finish_kernel(count, *refs)

    return pl.pallas_call(
        body,
        out_shape=(shape(BLK, width), shape(BLK, HD), shape(BLK, HD)),
        in_specs=[VMEM] * (2 * count + 4),
        out_specs=(VMEM,) * 3,
        compiler_params=PARAMS,
        name="finish",
    )(*attentions, *slices, own, first, second, side)


def spread_slice(array):
    seq = lax.axis_size("seq")
    heads = lax.axis_size("head")
    pairs = [(b * heads + h, b * heads + (h ^ (1 + b % 2))) for b in range(seq)
             for h in range(heads)]
    return lax.ppermute(array, ("seq", "head"), pairs)


def shards(queries, key_rows, value_rows, out_weight, strided_index, cotangent):
    seq = lax.axis_size("seq")
    heads = lax.axis_size("head")
    ring = seq == 8 and heads == 4
    n = STRIDE_ROWS
    side_rows = seq * n
    columns = 3 * BLK + side_rows
    own = jnp.concatenate([key_rows, value_rows], axis=1)
    first = trade(own, 1)
    grad, mult, *slices = prepare(
        ring, strided_index, cotangent, out_weight, heads, columns, own
    )
    if ring:
        mine, whole, half = slices
        half = swap(half, 3)
        near, pair, whole = leads(own, first, mult, whole)
        whole = spread_slice(whole)
        near = trade(near, -1)
        blocks = (own, first, near, trade(pair, 3), trade(pair, 4))
        side = 3 * BLK
        places = [side + i * n for i in range(6)]
        pieces = [[(i * BLK, (i + 1) * BLK)] for i in range(3)]
        pieces += [[(places[1], places[4])], [(places[4], places[5]), (places[0], places[1])]]
        att, dq, own_sum, first_sum, second_sum, to_plus, to_minus = attend(
            mult, queries, grad, blocks, pieces, 3
        )
        far = gather([swap(att, 2), swap(att, 3)])
        own_sum, to_first, to_second, last = combine(
            own_sum, first_sum, second_sum, trade(to_plus, 3), trade(to_minus, -3), whole, half,
            att,
        )
        mixed, dq, dk, dv = finish_ring(
            [att, swap(last, 1), far], mine, whole, half, trade(to_first, 1), own_sum,
            trade(to_second, -1), dq,
        )
    else:
        second = trade(own, -1)
        slices = [slices[0]] + [swap(slices[r], r) for r in range(1, heads)]
        spread = jnp.broadcast_to(own[None, :n], (seq, n, PAIR))
        side = lax.all_to_all(spread, "seq", 0, 0).reshape(side_rows, PAIR)
        pieces = [[(i * BLK, (i + 1) * BLK)] for i in range(3)] + [[(3 * BLK, columns)]]
        att, dq, own_sum, to_first, to_second, to_side = attend(
            mult, queries, grad, (own, first, second, side), pieces, 1
        )
        from_side = lax.all_to_all(to_side.reshape(seq, n, PAIR), "seq", 0, 0)
        mixed, dk, dv = finish(
            [att] + [swap(att, r) for r in range(1, heads)], slices, own_sum,
            trade(to_first, 1), trade(to_second, -1), from_side.reshape(side_rows, PAIR),
        )
    return (mixed, dq, dk, dv)


def solution(mesh):
    in_specs = (
        P("seq", "head"),
        P("seq", "head"),
        P("seq", "head"),
        P("head", None),
        P("seq", None),
        P("seq", None),
    )
    out_specs = (P("seq", "head"), P("seq", "head"), P("seq", "head"), P("seq", "head"))
    return jax.shard_map(shards, mesh=mesh, in_specs=in_specs, out_specs=out_specs, check_vma=False)
```

```python
import jax
import jax.numpy as jnp
from jax import lax
from jax.experimental import pallas as pl
from jax.experimental.pallas import tpu as pltpu
from jax.sharding import PartitionSpec as P

HD = 128
BLK = 128
STRIDE_ROWS = 32
MARGIN = 16
PAIR = 2 * HD
SCALE = HD ** (-0.5)
LOG2E = 1.4426950408889634
ABSENT = -1e30
VMEM = pl.BlockSpec(memory_space=pltpu.VMEM)
HBM = pl.BlockSpec(memory_space=pltpu.HBM)
PARAMS = pltpu.CompilerParams(vmem_limit_bytes=40 * 1024 * 1024)
FULL = pltpu.CompilerParams(vmem_limit_bytes=int(53.3 * 1024 * 1024))
BF16 = jnp.bfloat16
PREPARE_COST = 10**10
ATTEND_COST = 10**10
COMBINE_COST = 10**10
GATHER_COST = 10**10
PACK_COST = 10**10
F32 = jnp.float32


def dot_nt(a, b):
    return lax.dot_general(a, b, (((1,), (1,)), ((), ())), preferred_element_type=F32)


def dot_nn(a, b):
    return lax.dot_general(a, b, (((1,), (0,)), ((), ())), preferred_element_type=F32)


def dot_tn(a, b):
    return lax.dot_general(a, b, (((0,), (0,)), ((), ())), preferred_element_type=F32)


def shape(*dims, kind=BF16):
    return jax.ShapeDtypeStruct(dims, kind)


def trade(array, step):
    count = lax.axis_size("seq")
    return lax.ppermute(
        array, "seq", [(i, (i + (step if i % 2 == 0 else -step)) % count) for i in range(count)]
    )


def swap(array, mask):
    count = lax.axis_size("head")
    return lax.ppermute(array, "head", [(i, i ^ mask) for i in range(count)])


def count_of(picks, group):
    total = jnp.int32(0)
    for pick in picks:
        total = total + jnp.where(pick == group, 1, 0)
    return total.astype(F32)


def fill_multiplicity(ring, index_ref, mult_ref):
    per_block = BLK // STRIDE_ROWS
    picks = [index_ref[0, i] for i in range(index_ref.shape[1])]
    shape_of = mult_ref.shape
    lane = lax.broadcasted_iota(jnp.int32, shape_of, 1)
    mult = jnp.where(lane < 3 * BLK, 1.0, 0.0)
    if ring:
        b = lax.axis_index("seq")
        sign = 1 - 2 * (b & 1)
        counts = [count_of(picks, j) for j in range(2)]
        places = [(0, 0), (BLK, 1), (2 * BLK, -1)]
        places += [(3 * BLK + i * STRIDE_ROWS, o) for i, o in enumerate((-2, 3, 2, 4, 5))]
        for start, offset in places:
            owner = (b + 16 + sign * offset) & 7
            count = jnp.where(owner < per_block, counts[0], counts[1])
            inside = (lane >= start) & (lane < start + STRIDE_ROWS)
            mult = mult + jnp.where(inside, count, 0.0)
    else:
        for j in range((shape_of[1] - 3 * BLK) // BLK):
            start = (3 + j) * BLK
            inside = (lane >= start) & (lane < start + BLK)
            mult = mult + jnp.where(inside, count_of(picks, j), 0.0)
    mult_ref[...] = mult


def cost(flops):
    return pl.CostEstimate(flops=flops, bytes_accessed=0, transcendentals=0)


CHUNKS = 4


def prepare_kernel(ring, index_hbm, cot_hbm, w_hbm, after_ref, grad_ref, mult_ref, *refs):
    del after_ref
    index_ref, cot_ref, w_ref, sems = refs[-4:]
    slice_refs = refs[:-4]
    copies = [(index_hbm, index_ref)]
    depth = cot_ref.shape[1] // CHUNKS
    for i in range(CHUNKS):
        span = pl.ds(i * depth, depth)
        copies.append((w_hbm.at[:, span], w_ref.at[:, span]))
        copies.append((cot_hbm.at[:, span], cot_ref.at[:, span]))
    copies = [pltpu.make_async_copy(src, dst, sems.at[i]) for i, (src, dst) in enumerate(copies)]
    for copy in copies:
        copy.start()
    copies[0].wait()
    fill_multiplicity(ring, index_ref, mult_ref)
    total = None
    for i in range(CHUNKS):
        copies[1 + 2 * i].wait()
        copies[2 + 2 * i].wait()
        span = slice(i * depth, (i + 1) * depth)
        term = dot_nt(cot_ref[:, span], w_ref[:, span])
        total = term if total is None else total + term
    grad_ref[...] = total.astype(grad_ref.dtype)

    width = slice_refs[0].shape[1]
    head = lax.axis_index("head")

    def columns(h):
        return pl.ds(pl.multiple_of(h * width, width), width)

    if ring:
        core = lax.axis_index("seq") & 1
        half = HD // 2
        mine_ref, whole_ref, half_ref = slice_refs
        mine_ref[...] = w_ref[:, columns(head)]
        whole_ref[...] = w_ref[:, columns(head ^ (1 + core))]
        rows = pl.ds(pl.multiple_of(core * (half - MARGIN), MARGIN), half + MARGIN)
        half_ref[...] = w_ref[rows, columns(head ^ 3)]
    else:
        for r, ref in enumerate(slice_refs):
            ref[...] = w_ref[:, columns(head ^ r)]


def prepare(ring, index, cotangent, out_weight, heads, columns, after):
    width = out_weight.shape[1] // heads
    rows = (HD, HD, HD // 2 + MARGIN) if ring else (HD,) * heads

    def body(*refs):
        prepare_kernel(ring, *refs)

    return pl.pallas_call(
        body,
        out_shape=(shape(BLK, HD), shape(8, columns, kind=F32))
        + tuple(shape(r, width) for r in rows),
        in_specs=[HBM] * 3 + [VMEM],
        out_specs=(VMEM,) * (2 + len(rows)),
        scratch_shapes=[
            pltpu.SMEM(index.shape, jnp.int32),
            pltpu.VMEM(cotangent.shape, BF16),
            pltpu.VMEM(out_weight.shape, BF16),
            pltpu.SemaphoreType.DMA((1 + 2 * CHUNKS,)),
        ],
        compiler_params=FULL,
        cost_estimate=cost(PREPARE_COST),
        name="prepare",
    )(index, cotangent, out_weight, after)


def lead_kernel(own_ref, first_ref, mult_ref, whole_ref, near_ref, pair_ref, whole_out):
    del mult_ref
    n = STRIDE_ROWS
    near_ref[:BLK] = own_ref[...]
    near_ref[BLK:] = first_ref[:n]
    pair_ref[:n] = own_ref[:n]
    pair_ref[n:] = first_ref[:n]
    whole_out[...] = whole_ref[...]


def leads(own, first, mult, whole):
    n = STRIDE_ROWS
    return pl.pallas_call(
        lead_kernel,
        out_shape=(shape(BLK + n, PAIR), shape(2 * n, PAIR), shape(*whole.shape)),
        in_specs=[VMEM] * 4,
        out_specs=(VMEM,) * 3,
        compiler_params=PARAMS,
        name="leads",
    )(own, first, mult, whole)


def attend_kernel(blocks, pieces, mult_ref, q_ref, grad_ref, *refs):
    block_refs = refs[:blocks]
    att_ref, dq_ref = refs[blocks:blocks + 2]
    sum_refs = refs[blocks + 2:-1]
    keys_ref = refs[-1]
    total_rows = keys_ref.shape[0]
    row = 0
    for ref in block_refs:
        keys_ref[row:row + ref.shape[0], :] = ref[...]
        row += ref.shape[0]
    if row < total_rows:
        keys_ref[row:, :] = jnp.zeros((total_rows - row, PAIR), BF16)
    keys = keys_ref[:, :HD]
    values = keys_ref[:, HD:]
    q = q_ref[...]
    grad = grad_ref[...]
    mult = mult_ref[0:1, :]

    scores = dot_nt(q, keys) + jnp.where(mult > 0.0, 0.0, ABSENT)
    top = jnp.max(scores, axis=1, keepdims=True)
    terms = jnp.exp2((scores - top) * (SCALE * LOG2E)) * mult
    probability = terms * (1.0 / jnp.sum(terms, axis=1, keepdims=True))
    weights = probability.astype(BF16)
    att_ref[...] = dot_nn(weights, values).astype(BF16)

    grad_weights = dot_nt(grad, values)
    delta = jnp.sum(probability * grad_weights, axis=1, keepdims=True)
    grad_scores = (probability * (grad_weights - delta) * SCALE).astype(BF16)
    dq_ref[...] = dot_nn(grad_scores, keys).astype(BF16)
    key_terms = dot_tn(grad_scores, q)
    value_terms = dot_tn(weights, grad)
    for spans, ref in zip(pieces, sum_refs):
        row = 0
        for start, end in spans:
            rows = slice(row, row + end - start)
            ref[rows, :HD] = key_terms[start:end].astype(ref.dtype)
            ref[rows, HD:] = value_terms[start:end].astype(ref.dtype)
            row += end - start


def attend(mult, q, grad, blocks, pieces, wide):
    def body(*refs):
        attend_kernel(len(blocks), pieces, *refs)

    sums = []
    for i, spans in enumerate(pieces):
        rows = sum(end - start for start, end in spans)
        sums.append(shape(rows, PAIR, kind=F32 if i < wide else BF16))
    return pl.pallas_call(
        body,
        out_shape=(shape(BLK, HD), shape(BLK, HD), *sums),
        in_specs=[VMEM] * (3 + len(blocks)),
        out_specs=(VMEM,) * (2 + len(sums)),
        scratch_shapes=[pltpu.VMEM((mult.shape[1], PAIR), BF16)],
        compiler_params=PARAMS,
        cost_estimate=cost(ATTEND_COST),
        name="attend",
    )(mult, q, grad, *blocks)


def half_rows():
    core = lax.axis_index("seq") & 1
    return pl.ds(pl.multiple_of(core * MARGIN, MARGIN), HD // 2)


def combine_kernel(own_ref, first_ref, second_ref, plus_ref, minus_ref, whole_ref, half_ref,
                   att_ref, own_out, first_out, second_out, slices_out, att_out):
    plus = plus_ref[...].astype(F32)
    minus = minus_ref[...].astype(F32)
    n = STRIDE_ROWS
    own_out[n:] = own_ref[n:]
    own_out[:n] = own_ref[:n] + plus[:n] + minus[:n]
    second_out[n:] = second_ref[n:].astype(BF16)
    second_out[:n] = (second_ref[:n] + plus[2 * n:] + minus[n:]).astype(BF16)
    first_out[n:] = first_ref[n:].astype(BF16)
    first_out[:n] = (first_ref[:n] + plus[n:2 * n]).astype(BF16)
    att_out[...] = att_ref[...]
    row = 0
    for ref, rows in ((whole_ref, slice(0, HD)), (half_ref, half_rows())):
        for c in range(0, ref.shape[1], PAIR):
            piece = ref[rows, c:c + PAIR]
            slices_out[row:row + piece.shape[0]] = piece
            row += piece.shape[0]


def combine(own, first, second, plus, minus, whole, half, att):
    extra = (HD + HD // 2) * whole.shape[1] // PAIR
    return pl.pallas_call(
        combine_kernel,
        out_shape=(shape(BLK, PAIR, kind=F32), shape(BLK, PAIR), shape(BLK, PAIR),
                   shape(extra, PAIR), shape(BLK, HD)),
        in_specs=[VMEM] * 8,
        out_specs=(VMEM,) * 5,
        compiler_params=PARAMS,
        cost_estimate=cost(COMBINE_COST),
        name="combine",
    )(own, first, second, plus, minus, whole, half, att)


def pack_kernel(first_ref, slices_ref, after_ref, out_ref):
    del after_ref
    out_ref[:BLK] = first_ref[...]
    out_ref[BLK:] = slices_ref[...]


def pack(first, slices, after):
    return pl.pallas_call(
        pack_kernel,
        out_shape=shape(BLK + slices.shape[0], PAIR),
        in_specs=[VMEM] * 3,
        out_specs=VMEM,
        compiler_params=PARAMS,
        cost_estimate=cost(PACK_COST),
        name="pack",
    )(first, slices, after)


def gather_kernel(*refs):
    for r, ref in enumerate(refs[:-2]):
        refs[-1][:, r * HD:(r + 1) * HD] = ref[...]


def gather(attentions, after):
    return pl.pallas_call(
        gather_kernel,
        out_shape=shape(BLK, len(attentions) * HD),
        in_specs=[VMEM] * (len(attentions) + 1),
        out_specs=VMEM,
        compiler_params=PARAMS,
        cost_estimate=cost(GATHER_COST),
        name="gather",
    )(*attentions, after)


def settle(total, lead, dk_ref, dv_ref):
    for ref, c in ((dk_ref, 0), (dv_ref, HD)):
        ref[:STRIDE_ROWS] = lead[:, c:c + HD].astype(ref.dtype)
        ref[STRIDE_ROWS:] = total[STRIDE_ROWS:, c:c + HD].astype(ref.dtype)


def finish_ring_kernel(*refs):
    att_ref, others_ref, mine_ref, whole_ref, half_ref = refs[:5]
    first_ref, own_ref, second_ref, dq_ref = refs[5:9]
    mixed_hbm, dq_hbm, dk_hbm, dv_hbm, mixed_ref, dk_ref, dv_ref, sems = refs[9:]
    copies = []

    def send(src, dst):
        copy = pltpu.make_async_copy(src, dst, sems.at[len(copies)])
        copy.start()
        copies.append(copy)

    send(dq_ref, dq_hbm)
    total = own_ref[...] + first_ref[:BLK].astype(F32) + second_ref[...].astype(F32)
    settle(total, total[:STRIDE_ROWS], dk_ref, dv_ref)
    send(dk_ref, dk_hbm)
    send(dv_ref, dv_hbm)
    att = [att_ref[...]] + [others_ref[:, r * HD:(r + 1) * HD] for r in range(3)]
    core = lax.axis_index("seq") & 1
    half = HD // 2
    here = jnp.where(core == 0, att[1], att[2])
    there = jnp.where(core == 0, att[2], att[1])
    here_half = jnp.where(core == 0, att[3][:, :half], att[3][:, half:])
    there_half = jnp.where(core == 0, att[3][:, half:], att[3][:, :half])
    whole_row = BLK
    half_row = BLK + (mine_ref.shape[1] // PAIR) * HD
    for i, c in enumerate(range(0, mine_ref.shape[1], PAIR)):
        span = slice(c, c + PAIR)
        other_whole = first_ref[whole_row + i * HD:whole_row + (i + 1) * HD]
        other_half = first_ref[half_row + i * half:half_row + (i + 1) * half]
        mixed = dot_nn(att[0], mine_ref[:, span]) + dot_nn(here, whole_ref[:, span])
        mixed = mixed + dot_nn(there, other_whole) + dot_nn(here_half, half_ref[half_rows(), span])
        mixed = mixed + dot_nn(there_half, other_half)
        mixed_ref[:, span] = mixed.astype(mixed_ref.dtype)
        send(mixed_ref.at[:, pl.ds(c, PAIR)], mixed_hbm.at[:, pl.ds(c, PAIR)])
    for copy in copies:
        copy.wait()


def finish_ring(attentions, mine, whole, half, first, own, second, dq):
    width = mine.shape[1]
    return pl.pallas_call(
        finish_ring_kernel,
        out_shape=(shape(BLK, width),) + (shape(BLK, HD),) * 3,
        in_specs=[VMEM] * 9,
        out_specs=(HBM,) * 4,
        scratch_shapes=[
            pltpu.VMEM((BLK, width), BF16),
            pltpu.VMEM((BLK, HD), BF16),
            pltpu.VMEM((BLK, HD), BF16),
            pltpu.SemaphoreType.DMA((3 + width // PAIR,)),
        ],
        compiler_params=PARAMS,
        name="finish",
    )(*attentions, mine, whole, half, first, own, second, dq)


def finish_kernel(count, *refs):
    att_refs = refs[:count]
    w_refs = refs[count:2 * count]
    own_ref, first_ref, second_ref, side_ref, mixed_ref, dk_ref, dv_ref = refs[2 * count:]
    mixed = None
    for ref, w in zip(att_refs, w_refs):
        term = dot_nn(ref[...], w[...])
        mixed = term if mixed is None else mixed + term
    mixed_ref[...] = mixed.astype(mixed_ref.dtype)
    total = own_ref[...] + first_ref[...].astype(F32) + second_ref[...].astype(F32)
    lead = total[:STRIDE_ROWS]
    for i in range(side_ref.shape[0] // STRIDE_ROWS):
        lead = lead + side_ref[i * STRIDE_ROWS:(i + 1) * STRIDE_ROWS].astype(F32)
    settle(total, lead, dk_ref, dv_ref)


def finish(attentions, slices, own, first, second, side):
    width = slices[0].shape[1]
    count = len(attentions)

    def body(*refs):
        finish_kernel(count, *refs)

    return pl.pallas_call(
        body,
        out_shape=(shape(BLK, width), shape(BLK, HD), shape(BLK, HD)),
        in_specs=[VMEM] * (2 * count + 4),
        out_specs=(VMEM,) * 3,
        compiler_params=PARAMS,
        name="finish",
    )(*attentions, *slices, own, first, second, side)


def spread_slice(array):
    seq = lax.axis_size("seq")
    heads = lax.axis_size("head")
    pairs = [(b * heads + h, b * heads + (h ^ (1 + b % 2))) for b in range(seq)
             for h in range(heads)]
    return lax.ppermute(array, ("seq", "head"), pairs)


def shards(queries, key_rows, value_rows, out_weight, strided_index, cotangent):
    seq = lax.axis_size("seq")
    heads = lax.axis_size("head")
    ring = seq == 8 and heads == 4
    n = STRIDE_ROWS
    side_rows = seq * n
    columns = 3 * BLK + side_rows
    own = jnp.concatenate([key_rows, value_rows], axis=1)
    first = trade(own, 1)
    grad, mult, *slices = prepare(
        ring, strided_index, cotangent, out_weight, heads, columns, own
    )
    if ring:
        mine, whole, half = slices
        half = swap(half, 3)
        near, pair, whole = leads(own, first, mult, whole)
        whole = spread_slice(whole)
        near = trade(near, -1)
        blocks = (own, first, near, trade(pair, 3), trade(pair, 4))
        side = 3 * BLK
        places = [side + i * n for i in range(6)]
        pieces = [[(i * BLK, (i + 1) * BLK)] for i in range(3)]
        pieces += [[(places[1], places[4])], [(places[4], places[5]), (places[0], places[1])]]
        att, dq, own_sum, first_sum, second_sum, to_plus, to_minus = attend(
            mult, queries, grad, blocks, pieces, 3
        )
        far = [swap(att, 2), swap(att, 3)]
        own_sum, to_first, to_second, out_slices, last = combine(
            own_sum, first_sum, second_sum, trade(to_plus, 3), trade(to_minus, -3), whole, half,
            att,
        )
        from_second = trade(to_second, -1)
        packed = trade(pack(to_first, out_slices, far[1]), 1)
        others = gather([swap(last, 1)] + far, from_second)
        mixed, dq, dk, dv = finish_ring(
            [att, others], mine, whole, half, packed, own_sum, from_second, dq
        )
    else:
        second = trade(own, -1)
        slices = [slices[0]] + [swap(slices[r], r) for r in range(1, heads)]
        spread = jnp.broadcast_to(own[None, :n], (seq, n, PAIR))
        side = lax.all_to_all(spread, "seq", 0, 0).reshape(side_rows, PAIR)
        pieces = [[(i * BLK, (i + 1) * BLK)] for i in range(3)] + [[(3 * BLK, columns)]]
        att, dq, own_sum, to_first, to_second, to_side = attend(
            mult, queries, grad, (own, first, second, side), pieces, 1
        )
        from_side = lax.all_to_all(to_side.reshape(seq, n, PAIR), "seq", 0, 0)
        mixed, dk, dv = finish(
            [att] + [swap(att, r) for r in range(1, heads)], slices, own_sum,
            trade(to_first, 1), trade(to_second, -1), from_side.reshape(side_rows, PAIR),
        )
    return (mixed, dq, dk, dv)


def solution(mesh):
    in_specs = (
        P("seq", "head"),
        P("seq", "head"),
        P("seq", "head"),
        P("head", None),
        P("seq", None),
        P("seq", None),
    )
    out_specs = (P("seq", "head"), P("seq", "head"), P("seq", "head"), P("seq", "head"))
    return jax.shard_map(shards, mesh=mesh, in_specs=in_specs, out_specs=out_specs, check_vma=False)
```

```python
import jax
import jax.numpy as jnp
from jax import lax
from jax.experimental import pallas as pl
from jax.experimental.pallas import tpu as pltpu
from jax.sharding import PartitionSpec as P

HD = 128
BLK = 128
STRIDE_ROWS = 32
MARGIN = 16
PAIR = 2 * HD
SCALE = HD ** (-0.5)
LOG2E = 1.4426950408889634
ABSENT = -1e30
VMEM = pl.BlockSpec(memory_space=pltpu.VMEM)
HBM = pl.BlockSpec(memory_space=pltpu.HBM)
PARAMS = pltpu.CompilerParams(vmem_limit_bytes=40 * 1024 * 1024)
FULL = pltpu.CompilerParams(vmem_limit_bytes=int(53.3 * 1024 * 1024))
BF16 = jnp.bfloat16
PREPARE_COST = 10**10
ATTEND_COST = 10**10
COMBINE_COST = 10**10
GATHER_COST = 10**10
PACK_COST = 10**10
F32 = jnp.float32


def dot_nt(a, b):
    return lax.dot_general(a, b, (((1,), (1,)), ((), ())), preferred_element_type=F32)


def dot_nn(a, b):
    return lax.dot_general(a, b, (((1,), (0,)), ((), ())), preferred_element_type=F32)


def dot_tn(a, b):
    return lax.dot_general(a, b, (((0,), (0,)), ((), ())), preferred_element_type=F32)


def shape(*dims, kind=BF16):
    return jax.ShapeDtypeStruct(dims, kind)


def trade(array, step):
    count = lax.axis_size("seq")
    return lax.ppermute(
        array, "seq", [(i, (i + (step if i % 2 == 0 else -step)) % count) for i in range(count)]
    )


def swap(array, mask):
    count = lax.axis_size("head")
    return lax.ppermute(array, "head", [(i, i ^ mask) for i in range(count)])


def count_of(picks, group):
    total = jnp.int32(0)
    for pick in picks:
        total = total + jnp.where(pick == group, 1, 0)
    return total.astype(F32)


def fill_multiplicity(ring, index_ref, mult_ref):
    per_block = BLK // STRIDE_ROWS
    picks = [index_ref[0, i] for i in range(index_ref.shape[1])]
    shape_of = mult_ref.shape
    lane = lax.broadcasted_iota(jnp.int32, shape_of, 1)
    mult = jnp.where(lane < 3 * BLK, 1.0, 0.0)
    if ring:
        b = lax.axis_index("seq")
        sign = 1 - 2 * (b & 1)
        counts = [count_of(picks, j) for j in range(2)]
        places = [(0, 0), (BLK, 1), (2 * BLK, -1)]
        places += [(3 * BLK + i * STRIDE_ROWS, o) for i, o in enumerate((-2, 3, 2, 4, 5))]
        for start, offset in places:
            owner = (b + 16 + sign * offset) & 7
            count = jnp.where(owner < per_block, counts[0], counts[1])
            inside = (lane >= start) & (lane < start + STRIDE_ROWS)
            mult = mult + jnp.where(inside, count, 0.0)
    else:
        for j in range((shape_of[1] - 3 * BLK) // BLK):
            start = (3 + j) * BLK
            inside = (lane >= start) & (lane < start + BLK)
            mult = mult + jnp.where(inside, count_of(picks, j), 0.0)
    mult_ref[...] = mult


def cost(flops):
    return pl.CostEstimate(flops=flops, bytes_accessed=0, transcendentals=0)


CHUNKS = 4


def prepare_kernel(ring, index_hbm, cot_hbm, w_hbm, after_ref, grad_ref, mult_ref, *refs):
    del after_ref
    index_ref, cot_ref, w_ref, sems = refs[-4:]
    slice_refs = refs[:-4]
    copies = [(index_hbm, index_ref)]
    for src, dst in ((w_hbm, w_ref), (cot_hbm, cot_ref)):
        rows = dst.shape[0] // CHUNKS
        for i in range(CHUNKS):
            span = pl.ds(i * rows, rows)
            copies.append((src.at[span], dst.at[span]))
    copies = [pltpu.make_async_copy(src, dst, sems.at[i]) for i, (src, dst) in enumerate(copies)]
    for copy in copies:
        copy.start()
    copies[0].wait()
    fill_multiplicity(ring, index_ref, mult_ref)
    for copy in copies[1:1 + CHUNKS]:
        copy.wait()
    width = slice_refs[0].shape[1]
    head = lax.axis_index("head")

    def columns(h):
        return pl.ds(pl.multiple_of(h * width, width), width)

    if ring:
        core = lax.axis_index("seq") & 1
        half = HD // 2
        mine_ref, whole_ref, half_ref = slice_refs
        mine_ref[...] = w_ref[:, columns(head)]
        whole_ref[...] = w_ref[:, columns(head ^ (1 + core))]
        rows = pl.ds(pl.multiple_of(core * (half - MARGIN), MARGIN), half + MARGIN)
        half_ref[...] = w_ref[rows, columns(head ^ 3)]
    else:
        for r, ref in enumerate(slice_refs):
            ref[...] = w_ref[:, columns(head ^ r)]
    for copy in copies[1 + CHUNKS:]:
        copy.wait()
    grad_ref[...] = dot_nt(cot_ref[...], w_ref[...]).astype(grad_ref.dtype)


def prepare(ring, index, cotangent, out_weight, heads, columns, after):
    width = out_weight.shape[1] // heads
    rows = (HD, HD, HD // 2 + MARGIN) if ring else (HD,) * heads

    def body(*refs):
        prepare_kernel(ring, *refs)

    return pl.pallas_call(
        body,
        out_shape=(shape(BLK, HD), shape(8, columns, kind=F32))
        + tuple(shape(r, width) for r in rows),
        in_specs=[HBM] * 3 + [VMEM],
        out_specs=(VMEM,) * (2 + len(rows)),
        scratch_shapes=[
            pltpu.SMEM(index.shape, jnp.int32),
            pltpu.VMEM(cotangent.shape, BF16),
            pltpu.VMEM(out_weight.shape, BF16),
            pltpu.SemaphoreType.DMA((1 + 2 * CHUNKS,)),
        ],
        compiler_params=FULL,
        cost_estimate=cost(PREPARE_COST),
        name="prepare",
    )(index, cotangent, out_weight, after)


def lead_kernel(own_ref, first_ref, mult_ref, whole_ref, near_ref, pair_ref, whole_out):
    del mult_ref
    n = STRIDE_ROWS
    near_ref[:BLK] = own_ref[...]
    near_ref[BLK:] = first_ref[:n]
    pair_ref[:n] = own_ref[:n]
    pair_ref[n:] = first_ref[:n]
    whole_out[...] = whole_ref[...]


def leads(own, first, mult, whole):
    n = STRIDE_ROWS
    return pl.pallas_call(
        lead_kernel,
        out_shape=(shape(BLK + n, PAIR), shape(2 * n, PAIR), shape(*whole.shape)),
        in_specs=[VMEM] * 4,
        out_specs=(VMEM,) * 3,
        compiler_params=PARAMS,
        name="leads",
    )(own, first, mult, whole)


def attend_kernel(blocks, pieces, mult_ref, q_ref, grad_ref, *refs):
    block_refs = refs[:blocks]
    att_ref, dq_ref = refs[blocks:blocks + 2]
    sum_refs = refs[blocks + 2:-1]
    keys_ref = refs[-1]
    total_rows = keys_ref.shape[0]
    row = 0
    for ref in block_refs:
        keys_ref[row:row + ref.shape[0], :] = ref[...]
        row += ref.shape[0]
    if row < total_rows:
        keys_ref[row:, :] = jnp.zeros((total_rows - row, PAIR), BF16)
    keys = keys_ref[:, :HD]
    values = keys_ref[:, HD:]
    q = q_ref[...]
    grad = grad_ref[...]
    mult = mult_ref[0:1, :]

    scores = dot_nt(q, keys) + jnp.where(mult > 0.0, 0.0, ABSENT)
    top = jnp.max(scores, axis=1, keepdims=True)
    terms = jnp.exp2((scores - top) * (SCALE * LOG2E)) * mult
    probability = terms * (1.0 / jnp.sum(terms, axis=1, keepdims=True))
    weights = probability.astype(BF16)
    att_ref[...] = dot_nn(weights, values).astype(BF16)

    grad_weights = dot_nt(grad, values)
    delta = jnp.sum(probability * grad_weights, axis=1, keepdims=True)
    grad_scores = (probability * (grad_weights - delta) * SCALE).astype(BF16)
    dq_ref[...] = dot_nn(grad_scores, keys).astype(BF16)
    key_terms = dot_tn(grad_scores, q)
    value_terms = dot_tn(weights, grad)
    for spans, ref in zip(pieces, sum_refs):
        row = 0
        for start, end in spans:
            rows = slice(row, row + end - start)
            ref[rows, :HD] = key_terms[start:end].astype(ref.dtype)
            ref[rows, HD:] = value_terms[start:end].astype(ref.dtype)
            row += end - start


def attend(mult, q, grad, blocks, pieces, wide):
    def body(*refs):
        attend_kernel(len(blocks), pieces, *refs)

    sums = []
    for i, spans in enumerate(pieces):
        rows = sum(end - start for start, end in spans)
        sums.append(shape(rows, PAIR, kind=F32 if i < wide else BF16))
    return pl.pallas_call(
        body,
        out_shape=(shape(BLK, HD), shape(BLK, HD), *sums),
        in_specs=[VMEM] * (3 + len(blocks)),
        out_specs=(VMEM,) * (2 + len(sums)),
        scratch_shapes=[pltpu.VMEM((mult.shape[1], PAIR), BF16)],
        compiler_params=PARAMS,
        cost_estimate=cost(ATTEND_COST),
        name="attend",
    )(mult, q, grad, *blocks)


def half_rows():
    core = lax.axis_index("seq") & 1
    return pl.ds(pl.multiple_of(core * MARGIN, MARGIN), HD // 2)


def combine_kernel(own_ref, first_ref, second_ref, plus_ref, minus_ref, whole_ref, half_ref,
                   att_ref, own_out, first_out, second_out, slices_out, att_out):
    plus = plus_ref[...].astype(F32)
    minus = minus_ref[...].astype(F32)
    n = STRIDE_ROWS
    own_out[n:] = own_ref[n:]
    own_out[:n] = own_ref[:n] + plus[:n] + minus[:n]
    second_out[n:] = second_ref[n:].astype(BF16)
    second_out[:n] = (second_ref[:n] + plus[2 * n:] + minus[n:]).astype(BF16)
    first_out[n:] = first_ref[n:].astype(BF16)
    first_out[:n] = (first_ref[:n] + plus[n:2 * n]).astype(BF16)
    att_out[...] = att_ref[...]
    row = 0
    for ref, rows in ((whole_ref, slice(0, HD)), (half_ref, half_rows())):
        for c in range(0, ref.shape[1], PAIR):
            piece = ref[rows, c:c + PAIR]
            slices_out[row:row + piece.shape[0]] = piece
            row += piece.shape[0]


def combine(own, first, second, plus, minus, whole, half, att):
    extra = (HD + HD // 2) * whole.shape[1] // PAIR
    return pl.pallas_call(
        combine_kernel,
        out_shape=(shape(BLK, PAIR, kind=F32), shape(BLK, PAIR), shape(BLK, PAIR),
                   shape(extra, PAIR), shape(BLK, HD)),
        in_specs=[VMEM] * 8,
        out_specs=(VMEM,) * 5,
        compiler_params=PARAMS,
        cost_estimate=cost(COMBINE_COST),
        name="combine",
    )(own, first, second, plus, minus, whole, half, att)


def pack_kernel(first_ref, slices_ref, after_ref, out_ref):
    del after_ref
    out_ref[:BLK] = first_ref[...]
    out_ref[BLK:] = slices_ref[...]


def pack(first, slices, after):
    return pl.pallas_call(
        pack_kernel,
        out_shape=shape(BLK + slices.shape[0], PAIR),
        in_specs=[VMEM] * 3,
        out_specs=VMEM,
        compiler_params=PARAMS,
        cost_estimate=cost(PACK_COST),
        name="pack",
    )(first, slices, after)


def project_kernel(att_ref, two_ref, three_ref, mine_ref, whole_ref, half_ref, out_ref):
    core = lax.axis_index("seq") & 1
    half = HD // 2
    two = jnp.where(core == 0, jnp.zeros((BLK, HD), BF16), two_ref[...])
    three = jnp.where(core == 0, three_ref[:, :half], three_ref[:, half:])
    total = dot_nn(att_ref[...], mine_ref[...]) + dot_nn(two, whole_ref[...])
    out_ref[...] = total + dot_nn(three, half_ref[half_rows(), :])


def project(att, two, three, mine, whole, half):
    return pl.pallas_call(
        project_kernel,
        out_shape=shape(BLK, mine.shape[1], kind=F32),
        in_specs=[VMEM] * 6,
        out_specs=VMEM,
        compiler_params=PARAMS,
        name="project",
    )(att, two, three, mine, whole, half)


def gather_kernel(one_ref, second_ref, partial_ref, out_ref):
    del second_ref, partial_ref
    out_ref[...] = one_ref[...]


def gather(one, second, partial):
    return pl.pallas_call(
        gather_kernel,
        out_shape=shape(BLK, HD),
        in_specs=[VMEM] * 3,
        out_specs=VMEM,
        compiler_params=PARAMS,
        cost_estimate=cost(GATHER_COST),
        name="gather",
    )(one, second, partial)


def settle(total, lead, dk_ref, dv_ref):
    for ref, c in ((dk_ref, 0), (dv_ref, HD)):
        ref[:STRIDE_ROWS] = lead[:, c:c + HD].astype(ref.dtype)
        ref[STRIDE_ROWS:] = total[STRIDE_ROWS:, c:c + HD].astype(ref.dtype)


def finish_ring_kernel(partial_ref, one_ref, two_ref, three_ref, whole_ref, first_ref, own_ref,
                       second_ref, dq_ref, mixed_hbm, dq_hbm, dk_hbm, dv_hbm,
                       mixed_ref, dk_ref, dv_ref, sems):
    copies = []

    def send(src, dst):
        copy = pltpu.make_async_copy(src, dst, sems.at[len(copies)])
        copy.start()
        copies.append(copy)

    send(dq_ref, dq_hbm)
    core = lax.axis_index("seq") & 1
    half = HD // 2
    one, two, three = one_ref[...], two_ref[...], three_ref[...]
    here = jnp.where(core == 0, one, jnp.zeros_like(one))
    there = jnp.where(core == 0, two, one)
    there_half = jnp.where(core == 0, three[:, half:], three[:, :half])
    width = whole_ref.shape[1]
    half_row = BLK + (width // PAIR) * HD
    for i, c in enumerate(range(0, width, PAIR)):
        span = slice(c, c + PAIR)
        other_whole = first_ref[BLK + i * HD:BLK + (i + 1) * HD]
        other_half = first_ref[half_row + i * half:half_row + (i + 1) * half]
        mixed = partial_ref[:, span] + dot_nn(here, whole_ref[:, span])
        mixed = mixed + dot_nn(there, other_whole) + dot_nn(there_half, other_half)
        mixed_ref[:, span] = mixed.astype(mixed_ref.dtype)
        send(mixed_ref.at[:, pl.ds(c, PAIR)], mixed_hbm.at[:, pl.ds(c, PAIR)])
    total = own_ref[...] + first_ref[:BLK].astype(F32) + second_ref[...].astype(F32)
    settle(total, total[:STRIDE_ROWS], dk_ref, dv_ref)
    send(dk_ref, dk_hbm)
    send(dv_ref, dv_hbm)
    for copy in copies:
        copy.wait()


def finish_ring(*args):
    width = args[0].shape[1]
    return pl.pallas_call(
        finish_ring_kernel,
        out_shape=(shape(BLK, width),) + (shape(BLK, HD),) * 3,
        in_specs=[VMEM] * len(args),
        out_specs=(HBM,) * 4,
        scratch_shapes=[
            pltpu.VMEM((BLK, width), BF16),
            pltpu.VMEM((BLK, HD), BF16),
            pltpu.VMEM((BLK, HD), BF16),
            pltpu.SemaphoreType.DMA((3 + width // PAIR,)),
        ],
        compiler_params=PARAMS,
        name="finish",
    )(*args)


def finish_kernel(count, *refs):
    att_refs = refs[:count]
    w_refs = refs[count:2 * count]
    own_ref, first_ref, second_ref, side_ref, mixed_ref, dk_ref, dv_ref = refs[2 * count:]
    mixed = None
    for ref, w in zip(att_refs, w_refs):
        term = dot_nn(ref[...], w[...])
        mixed = term if mixed is None else mixed + term
    mixed_ref[...] = mixed.astype(mixed_ref.dtype)
    total = own_ref[...] + first_ref[...].astype(F32) + second_ref[...].astype(F32)
    lead = total[:STRIDE_ROWS]
    for i in range(side_ref.shape[0] // STRIDE_ROWS):
        lead = lead + side_ref[i * STRIDE_ROWS:(i + 1) * STRIDE_ROWS].astype(F32)
    settle(total, lead, dk_ref, dv_ref)


def finish(attentions, slices, own, first, second, side):
    width = slices[0].shape[1]
    count = len(attentions)

    def body(*refs):
        finish_kernel(count, *refs)

    return pl.pallas_call(
        body,
        out_shape=(shape(BLK, width), shape(BLK, HD), shape(BLK, HD)),
        in_specs=[VMEM] * (2 * count + 4),
        out_specs=(VMEM,) * 3,
        compiler_params=PARAMS,
        name="finish",
    )(*attentions, *slices, own, first, second, side)


def spread_slice(array):
    seq = lax.axis_size("seq")
    heads = lax.axis_size("head")
    pairs = [(b * heads + h, b * heads + (h ^ (1 + b % 2))) for b in range(seq)
             for h in range(heads)]
    return lax.ppermute(array, ("seq", "head"), pairs)


def shards(queries, key_rows, value_rows, out_weight, strided_index, cotangent):
    seq = lax.axis_size("seq")
    heads = lax.axis_size("head")
    ring = seq == 8 and heads == 4
    n = STRIDE_ROWS
    side_rows = seq * n
    columns = 3 * BLK + side_rows
    own = jnp.concatenate([key_rows, value_rows], axis=1)
    first = trade(own, 1)
    grad, mult, *slices = prepare(
        ring, strided_index, cotangent, out_weight, heads, columns, own
    )
    if ring:
        mine, whole, half = slices
        half = swap(half, 3)
        near, pair, whole = leads(own, first, mult, whole)
        whole = spread_slice(whole)
        near = trade(near, -1)
        blocks = (own, first, near, trade(pair, 3), trade(pair, 4))
        side = 3 * BLK
        places = [side + i * n for i in range(6)]
        pieces = [[(i * BLK, (i + 1) * BLK)] for i in range(3)]
        pieces += [[(places[1], places[4])], [(places[4], places[5]), (places[0], places[1])]]
        att, dq, own_sum, first_sum, second_sum, to_plus, to_minus = attend(
            mult, queries, grad, blocks, pieces, 3
        )
        far = [swap(att, 2), swap(att, 3)]
        own_sum, to_first, to_second, out_slices, last = combine(
            own_sum, first_sum, second_sum, trade(to_plus, 3), trade(to_minus, -3), whole, half,
            att,
        )
        from_second = trade(to_second, -1)
        packed = trade(pack(to_first, out_slices, far[1]), 1)
        partial = project(att, *far, mine, whole, half)
        one = gather(swap(last, 1), from_second, partial)
        mixed, dq, dk, dv = finish_ring(
            partial, one, *far, whole, packed, own_sum, from_second, dq
        )
    else:
        second = trade(own, -1)
        slices = [slices[0]] + [swap(slices[r], r) for r in range(1, heads)]
        spread = jnp.broadcast_to(own[None, :n], (seq, n, PAIR))
        side = lax.all_to_all(spread, "seq", 0, 0).reshape(side_rows, PAIR)
        pieces = [[(i * BLK, (i + 1) * BLK)] for i in range(3)] + [[(3 * BLK, columns)]]
        att, dq, own_sum, to_first, to_second, to_side = attend(
            mult, queries, grad, (own, first, second, side), pieces, 1
        )
        from_side = lax.all_to_all(to_side.reshape(seq, n, PAIR), "seq", 0, 0)
        mixed, dk, dv = finish(
            [att] + [swap(att, r) for r in range(1, heads)], slices, own_sum,
            trade(to_first, 1), trade(to_second, -1), from_side.reshape(side_rows, PAIR),
        )
    return (mixed, dq, dk, dv)


def solution(mesh):
    in_specs = (
        P("seq", "head"),
        P("seq", "head"),
        P("seq", "head"),
        P("head", None),
        P("seq", None),
        P("seq", None),
    )
    out_specs = (P("seq", "head"), P("seq", "head"), P("seq", "head"), P("seq", "head"))
    return jax.shard_map(shards, mesh=mesh, in_specs=in_specs, out_specs=out_specs, check_vma=False)
```

```python
import jax
import jax.numpy as jnp
from jax import lax
from jax.experimental import pallas as pl
from jax.experimental.pallas import tpu as pltpu
from jax.sharding import PartitionSpec as P

HD = 128
BLK = 128
STRIDE_ROWS = 32
MARGIN = 16
PAIR = 2 * HD
SCALE = HD ** (-0.5)
LOG2E = 1.4426950408889634
ABSENT = -1e30
VMEM = pl.BlockSpec(memory_space=pltpu.VMEM)
HBM = pl.BlockSpec(memory_space=pltpu.HBM)
PARAMS = pltpu.CompilerParams(vmem_limit_bytes=40 * 1024 * 1024)
FULL = pltpu.CompilerParams(vmem_limit_bytes=int(52.8 * 1024 * 1024))
BF16 = jnp.bfloat16
PREPARE_COST = 10**10
ATTEND_COST = 10**10
COMBINE_COST = 10**10
GATHER_COST = 10**10
PACK_COST = 10**10
F32 = jnp.float32


def dot_nt(a, b):
    return lax.dot_general(a, b, (((1,), (1,)), ((), ())), preferred_element_type=F32)


def dot_nn(a, b):
    return lax.dot_general(a, b, (((1,), (0,)), ((), ())), preferred_element_type=F32)


def dot_tn(a, b):
    return lax.dot_general(a, b, (((0,), (0,)), ((), ())), preferred_element_type=F32)


def shape(*dims, kind=BF16):
    return jax.ShapeDtypeStruct(dims, kind)


def trade(array, step):
    count = lax.axis_size("seq")
    return lax.ppermute(
        array, "seq", [(i, (i + (step if i % 2 == 0 else -step)) % count) for i in range(count)]
    )


def swap(array, mask):
    count = lax.axis_size("head")
    return lax.ppermute(array, "head", [(i, i ^ mask) for i in range(count)])


def count_of(picks, group):
    total = jnp.int32(0)
    for pick in picks:
        total = total + jnp.where(pick == group, 1, 0)
    return total.astype(F32)


def fill_multiplicity(ring, index_ref, mult_ref):
    per_block = BLK // STRIDE_ROWS
    picks = [index_ref[0, i] for i in range(index_ref.shape[1])]
    shape_of = mult_ref.shape
    lane = lax.broadcasted_iota(jnp.int32, shape_of, 1)
    mult = jnp.where(lane < 3 * BLK, 1.0, 0.0)
    if ring:
        b = lax.axis_index("seq")
        sign = 1 - 2 * (b & 1)
        counts = [count_of(picks, j) for j in range(2)]
        places = [(0, 0), (BLK, 1), (2 * BLK, -1)]
        places += [(3 * BLK + i * STRIDE_ROWS, o) for i, o in enumerate((-2, 3, 2, 4, 5))]
        for start, offset in places:
            owner = (b + 16 + sign * offset) & 7
            count = jnp.where(owner < per_block, counts[0], counts[1])
            inside = (lane >= start) & (lane < start + STRIDE_ROWS)
            mult = mult + jnp.where(inside, count, 0.0)
    else:
        for j in range((shape_of[1] - 3 * BLK) // BLK):
            start = (3 + j) * BLK
            inside = (lane >= start) & (lane < start + BLK)
            mult = mult + jnp.where(inside, count_of(picks, j), 0.0)
    mult_ref[...] = mult


def cost(flops):
    return pl.CostEstimate(flops=flops, bytes_accessed=0, transcendentals=0)


CHUNKS = 4


def row_copies(src, dst, sems, first):
    rows = dst.shape[0] // CHUNKS
    spans = [pl.ds(i * rows, rows) for i in range(CHUNKS)]
    return [pltpu.make_async_copy(src.at[span], dst.at[span], sems.at[first + i])
            for i, span in enumerate(spans)]


def slices_kernel(ring, index_hbm, w_hbm, after_ref, mult_ref, w_ref, *refs):
    del after_ref
    index_ref, sems = refs[-2:]
    slice_refs = refs[:-2]
    copies = [pltpu.make_async_copy(index_hbm, index_ref, sems.at[CHUNKS])]
    copies += row_copies(w_hbm, w_ref, sems, 0)
    for copy in copies:
        copy.start()
    copies[0].wait()
    fill_multiplicity(ring, index_ref, mult_ref)
    for copy in copies[1:]:
        copy.wait()
    width = slice_refs[0].shape[1]
    head = lax.axis_index("head")

    def columns(h):
        return pl.ds(pl.multiple_of(h * width, width), width)

    if ring:
        core = lax.axis_index("seq") & 1
        half = HD // 2
        mine_ref, whole_ref, half_ref = slice_refs
        mine_ref[...] = w_ref[:, columns(head)]
        whole_ref[...] = w_ref[:, columns(head ^ (3 - core))]
        rows = pl.ds(pl.multiple_of(core * (half - MARGIN), MARGIN), half + MARGIN)
        half_ref[...] = w_ref[rows, columns(head ^ 1)]
    else:
        for r, ref in enumerate(slice_refs):
            ref[...] = w_ref[:, columns(head ^ r)]


def weight_slices(ring, index, out_weight, heads, columns, after):
    width = out_weight.shape[1] // heads
    rows = (HD, HD, HD // 2 + MARGIN) if ring else (HD,) * heads

    def body(*refs):
        slices_kernel(ring, *refs)

    return pl.pallas_call(
        body,
        out_shape=(shape(8, columns, kind=F32), shape(*out_weight.shape))
        + tuple(shape(r, width) for r in rows),
        in_specs=[HBM] * 2 + [VMEM],
        out_specs=(VMEM,) * (2 + len(rows)),
        scratch_shapes=[
            pltpu.SMEM(index.shape, jnp.int32),
            pltpu.SemaphoreType.DMA((1 + CHUNKS,)),
        ],
        compiler_params=FULL,
        cost_estimate=cost(PREPARE_COST),
        name="slices",
    )(index, out_weight, after)


def prepare_kernel(cot_ref, w_ref, after_ref, grad_ref):
    del after_ref
    grad_ref[...] = dot_nt(cot_ref[...], w_ref[...]).astype(grad_ref.dtype)


def prepare(cotangent, out_weight, after):
    return pl.pallas_call(
        prepare_kernel,
        out_shape=shape(BLK, HD),
        in_specs=[VMEM] * 3,
        out_specs=VMEM,
        compiler_params=PARAMS,
        cost_estimate=cost(PREPARE_COST),
        name="prepare",
    )(cotangent, out_weight, after)


def lead_kernel(own_ref, first_ref, mult_ref, whole_ref, near_ref, pair_ref, whole_out):
    del mult_ref
    n = STRIDE_ROWS
    near_ref[:BLK] = own_ref[...]
    near_ref[BLK:] = first_ref[:n]
    pair_ref[:n] = own_ref[:n]
    pair_ref[n:] = first_ref[:n]
    whole_out[...] = whole_ref[...]


def leads(own, first, mult, whole):
    n = STRIDE_ROWS
    return pl.pallas_call(
        lead_kernel,
        out_shape=(shape(BLK + n, PAIR), shape(2 * n, PAIR), shape(*whole.shape)),
        in_specs=[VMEM] * 4,
        out_specs=(VMEM,) * 3,
        compiler_params=PARAMS,
        name="leads",
    )(own, first, mult, whole)


def attend_kernel(blocks, pieces, mult_ref, q_ref, grad_ref, *refs):
    block_refs = refs[:blocks]
    att_ref, dq_ref = refs[blocks:blocks + 2]
    sum_refs = refs[blocks + 2:-1]
    keys_ref = refs[-1]
    total_rows = keys_ref.shape[0]
    row = 0
    for ref in block_refs:
        keys_ref[row:row + ref.shape[0], :] = ref[...]
        row += ref.shape[0]
    if row < total_rows:
        keys_ref[row:, :] = jnp.zeros((total_rows - row, PAIR), BF16)
    keys = keys_ref[:, :HD]
    values = keys_ref[:, HD:]
    q = q_ref[...]
    grad = grad_ref[...]
    mult = mult_ref[0:1, :]

    scores = dot_nt(q, keys) + jnp.where(mult > 0.0, 0.0, ABSENT)
    top = jnp.max(scores, axis=1, keepdims=True)
    terms = jnp.exp2((scores - top) * (SCALE * LOG2E)) * mult
    probability = terms * (1.0 / jnp.sum(terms, axis=1, keepdims=True))
    weights = probability.astype(BF16)
    att_ref[...] = dot_nn(weights, values).astype(BF16)

    grad_weights = dot_nt(grad, values)
    delta = jnp.sum(probability * grad_weights, axis=1, keepdims=True)
    grad_scores = (probability * (grad_weights - delta) * SCALE).astype(BF16)
    dq_ref[...] = dot_nn(grad_scores, keys).astype(BF16)
    key_terms = dot_tn(grad_scores, q)
    value_terms = dot_tn(weights, grad)
    for spans, ref in zip(pieces, sum_refs):
        row = 0
        for start, end in spans:
            rows = slice(row, row + end - start)
            ref[rows, :HD] = key_terms[start:end].astype(ref.dtype)
            ref[rows, HD:] = value_terms[start:end].astype(ref.dtype)
            row += end - start


def attend(mult, q, grad, blocks, pieces, wide):
    def body(*refs):
        attend_kernel(len(blocks), pieces, *refs)

    sums = []
    for i, spans in enumerate(pieces):
        rows = sum(end - start for start, end in spans)
        sums.append(shape(rows, PAIR, kind=F32 if i < wide else BF16))
    return pl.pallas_call(
        body,
        out_shape=(shape(BLK, HD), shape(BLK, HD), *sums),
        in_specs=[VMEM] * (3 + len(blocks)),
        out_specs=(VMEM,) * (2 + len(sums)),
        scratch_shapes=[pltpu.VMEM((mult.shape[1], PAIR), BF16)],
        compiler_params=PARAMS,
        cost_estimate=cost(ATTEND_COST),
        name="attend",
    )(mult, q, grad, *blocks)


def half_rows():
    core = lax.axis_index("seq") & 1
    return pl.ds(pl.multiple_of(core * MARGIN, MARGIN), HD // 2)


def combine_kernel(own_ref, first_ref, second_ref, plus_ref, minus_ref, whole_ref, half_ref,
                   att_ref, own_out, first_out, second_out, slices_out, att_out):
    plus = plus_ref[...].astype(F32)
    minus = minus_ref[...].astype(F32)
    n = STRIDE_ROWS
    own_out[n:] = own_ref[n:]
    own_out[:n] = own_ref[:n] + plus[:n] + minus[:n]
    second_out[n:] = second_ref[n:].astype(BF16)
    second_out[:n] = (second_ref[:n] + plus[2 * n:] + minus[n:]).astype(BF16)
    first_out[n:] = first_ref[n:].astype(BF16)
    first_out[:n] = (first_ref[:n] + plus[n:2 * n]).astype(BF16)
    att_out[...] = att_ref[...]
    row = 0
    for ref, rows in ((whole_ref, slice(0, HD)), (half_ref, half_rows())):
        for c in range(0, ref.shape[1], PAIR):
            piece = ref[rows, c:c + PAIR]
            slices_out[row:row + piece.shape[0]] = piece
            row += piece.shape[0]


def combine(own, first, second, plus, minus, whole, half, att):
    extra = (HD + HD // 2) * whole.shape[1] // PAIR
    return pl.pallas_call(
        combine_kernel,
        out_shape=(shape(BLK, PAIR, kind=F32), shape(BLK, PAIR), shape(BLK, PAIR),
                   shape(extra, PAIR), shape(BLK, HD)),
        in_specs=[VMEM] * 8,
        out_specs=(VMEM,) * 5,
        compiler_params=PARAMS,
        cost_estimate=cost(COMBINE_COST),
        name="combine",
    )(own, first, second, plus, minus, whole, half, att)


def pack_kernel(first_ref, slices_ref, after_ref, out_ref):
    del after_ref
    out_ref[:BLK] = first_ref[...]
    out_ref[BLK:] = slices_ref[...]


def pack(first, slices, after):
    return pl.pallas_call(
        pack_kernel,
        out_shape=shape(BLK + slices.shape[0], PAIR),
        in_specs=[VMEM] * 3,
        out_specs=VMEM,
        compiler_params=PARAMS,
        cost_estimate=cost(PACK_COST),
        name="pack",
    )(first, slices, after)


def project_kernel(att_ref, two_ref, three_ref, mine_ref, whole_ref, out_ref):
    core = lax.axis_index("seq") & 1
    here = jnp.where(core == 0, three_ref[...], two_ref[...])
    out_ref[...] = dot_nn(att_ref[...], mine_ref[...]) + dot_nn(here, whole_ref[...])


def project(att, two, three, mine, whole):
    return pl.pallas_call(
        project_kernel,
        out_shape=shape(BLK, mine.shape[1], kind=F32),
        in_specs=[VMEM] * 5,
        out_specs=VMEM,
        compiler_params=PARAMS,
        name="project",
    )(att, two, three, mine, whole)


def gather_kernel(one_ref, second_ref, partial_ref, out_ref):
    del second_ref, partial_ref
    out_ref[...] = one_ref[...]


def gather(one, second, partial):
    return pl.pallas_call(
        gather_kernel,
        out_shape=shape(BLK, HD),
        in_specs=[VMEM] * 3,
        out_specs=VMEM,
        compiler_params=PARAMS,
        cost_estimate=cost(GATHER_COST),
        name="gather",
    )(one, second, partial)


def settle(total, lead, dk_ref, dv_ref):
    for ref, c in ((dk_ref, 0), (dv_ref, HD)):
        ref[:STRIDE_ROWS] = lead[:, c:c + HD].astype(ref.dtype)
        ref[STRIDE_ROWS:] = total[STRIDE_ROWS:, c:c + HD].astype(ref.dtype)


def finish_ring_kernel(partial_ref, one_ref, two_ref, three_ref, half_ref, first_ref, own_ref,
                       second_ref, dq_ref, mixed_hbm, dq_hbm, dk_hbm, dv_hbm,
                       mixed_ref, dk_ref, dv_ref, sems):
    copies = []

    def send(src, dst):
        copy = pltpu.make_async_copy(src, dst, sems.at[len(copies)])
        copy.start()
        copies.append(copy)

    send(dq_ref, dq_hbm)
    core = lax.axis_index("seq") & 1
    half = HD // 2
    one = one_ref[...]
    there = jnp.where(core == 0, two_ref[...], three_ref[...])
    here_half = jnp.where(core == 0, one[:, :half], one[:, half:])
    there_half = jnp.where(core == 0, one[:, half:], one[:, :half])
    width = half_ref.shape[1]
    half_row = BLK + (width // PAIR) * HD
    for r in range(0, BLK, half):
        rows = slice(r, r + half)
        for i, c in enumerate(range(0, width, PAIR)):
            span = slice(c, c + PAIR)
            other_whole = first_ref[BLK + i * HD:BLK + (i + 1) * HD]
            other_half = first_ref[half_row + i * half:half_row + (i + 1) * half]
            mixed = partial_ref[rows, span] + dot_nn(there[rows], other_whole)
            mixed = mixed + dot_nn(here_half[rows], half_ref[half_rows(), span])
            mixed = mixed + dot_nn(there_half[rows], other_half)
            mixed_ref[rows, span] = mixed.astype(mixed_ref.dtype)
        send(mixed_ref.at[pl.ds(r, half)], mixed_hbm.at[pl.ds(r, half)])
    total = own_ref[...] + first_ref[:BLK].astype(F32) + second_ref[...].astype(F32)
    settle(total, total[:STRIDE_ROWS], dk_ref, dv_ref)
    send(dk_ref, dk_hbm)
    send(dv_ref, dv_hbm)
    for copy in copies:
        copy.wait()


def finish_ring(*args):
    width = args[0].shape[1]
    return pl.pallas_call(
        finish_ring_kernel,
        out_shape=(shape(BLK, width),) + (shape(BLK, HD),) * 3,
        in_specs=[VMEM] * len(args),
        out_specs=(HBM,) * 4,
        scratch_shapes=[
            pltpu.VMEM((BLK, width), BF16),
            pltpu.VMEM((BLK, HD), BF16),
            pltpu.VMEM((BLK, HD), BF16),
            pltpu.SemaphoreType.DMA((5,)),
        ],
        compiler_params=PARAMS,
        name="finish",
    )(*args)


def finish_kernel(count, *refs):
    att_refs = refs[:count]
    w_refs = refs[count:2 * count]
    own_ref, first_ref, second_ref, side_ref, mixed_ref, dk_ref, dv_ref = refs[2 * count:]
    mixed = None
    for ref, w in zip(att_refs, w_refs):
        term = dot_nn(ref[...], w[...])
        mixed = term if mixed is None else mixed + term
    mixed_ref[...] = mixed.astype(mixed_ref.dtype)
    total = own_ref[...] + first_ref[...].astype(F32) + second_ref[...].astype(F32)
    lead = total[:STRIDE_ROWS]
    for i in range(side_ref.shape[0] // STRIDE_ROWS):
        lead = lead + side_ref[i * STRIDE_ROWS:(i + 1) * STRIDE_ROWS].astype(F32)
    settle(total, lead, dk_ref, dv_ref)


def finish(attentions, slices, own, first, second, side):
    width = slices[0].shape[1]
    count = len(attentions)

    def body(*refs):
        finish_kernel(count, *refs)

    return pl.pallas_call(
        body,
        out_shape=(shape(BLK, width), shape(BLK, HD), shape(BLK, HD)),
        in_specs=[VMEM] * (2 * count + 4),
        out_specs=(VMEM,) * 3,
        compiler_params=PARAMS,
        name="finish",
    )(*attentions, *slices, own, first, second, side)


def spread_slice(array):
    seq = lax.axis_size("seq")
    heads = lax.axis_size("head")
    pairs = [(b * heads + h, b * heads + (h ^ (3 - b % 2))) for b in range(seq)
             for h in range(heads)]
    return lax.ppermute(array, ("seq", "head"), pairs)


def shards(queries, key_rows, value_rows, out_weight, strided_index, cotangent):
    seq = lax.axis_size("seq")
    heads = lax.axis_size("head")
    ring = seq == 8 and heads == 4
    n = STRIDE_ROWS
    side_rows = seq * n
    columns = 3 * BLK + side_rows
    own = jnp.concatenate([key_rows, value_rows], axis=1)
    first = trade(own, 1)
    mult, weight, *slices = weight_slices(
        ring, strided_index, out_weight, heads, columns, own
    )
    if ring:
        mine, whole, half = slices
        half = swap(half, 1)
        near, pair, whole = leads(own, first, mult, whole)
        grad = prepare(cotangent, weight, pair)
        whole = spread_slice(whole)
        near = trade(near, -1)
        blocks = (own, first, near, trade(pair, 3), trade(pair, 4))
        side = 3 * BLK
        places = [side + i * n for i in range(6)]
        pieces = [[(i * BLK, (i + 1) * BLK)] for i in range(3)]
        pieces += [[(places[1], places[4])], [(places[4], places[5]), (places[0], places[1])]]
        att, dq, own_sum, first_sum, second_sum, to_plus, to_minus = attend(
            mult, queries, grad, blocks, pieces, 3
        )
        far = [swap(att, 2), swap(att, 3)]
        own_sum, to_first, to_second, out_slices, last = combine(
            own_sum, first_sum, second_sum, trade(to_plus, 3), trade(to_minus, -3), whole, half,
            att,
        )
        from_second = trade(to_second, -1)
        packed = trade(pack(to_first, out_slices, far[1]), 1)
        partial = project(att, *far, mine, whole)
        one = gather(swap(last, 1), from_second, partial)
        mixed, dq, dk, dv = finish_ring(
            partial, one, *far, half, packed, own_sum, from_second, dq
        )
    else:
        second = trade(own, -1)
        grad = prepare(cotangent, weight, own)
        slices = [slices[0]] + [swap(slices[r], r) for r in range(1, heads)]
        spread = jnp.broadcast_to(own[None, :n], (seq, n, PAIR))
        side = lax.all_to_all(spread, "seq", 0, 0).reshape(side_rows, PAIR)
        pieces = [[(i * BLK, (i + 1) * BLK)] for i in range(3)] + [[(3 * BLK, columns)]]
        att, dq, own_sum, to_first, to_second, to_side = attend(
            mult, queries, grad, (own, first, second, side), pieces, 1
        )
        from_side = lax.all_to_all(to_side.reshape(seq, n, PAIR), "seq", 0, 0)
        mixed, dk, dv = finish(
            [att] + [swap(att, r) for r in range(1, heads)], slices, own_sum,
            trade(to_first, 1), trade(to_second, -1), from_side.reshape(side_rows, PAIR),
        )
    return (mixed, dq, dk, dv)


def solution(mesh):
    in_specs = (
        P("seq", "head"),
        P("seq", "head"),
        P("seq", "head"),
        P("head", None),
        P("seq", None),
        P("seq", None),
    )
    out_specs = (P("seq", "head"), P("seq", "head"), P("seq", "head"), P("seq", "head"))
    return jax.shard_map(shards, mesh=mesh, in_specs=in_specs, out_specs=out_specs, check_vma=False)
```

```python
import jax
import jax.numpy as jnp
from jax import lax
from jax.experimental import pallas as pl
from jax.experimental.pallas import tpu as pltpu
from jax.sharding import PartitionSpec as P

HD = 128
BLK = 128
STRIDE_ROWS = 32
MARGIN = 16
PAIR = 2 * HD
SCALE = HD ** (-0.5)
LOG2E = 1.4426950408889634
ABSENT = -1e30
VMEM = pl.BlockSpec(memory_space=pltpu.VMEM)
HBM = pl.BlockSpec(memory_space=pltpu.HBM)
PARAMS = pltpu.CompilerParams(vmem_limit_bytes=40 * 1024 * 1024)
FULL = pltpu.CompilerParams(vmem_limit_bytes=int(52.8 * 1024 * 1024))
BF16 = jnp.bfloat16
PREPARE_COST = 10**10
ATTEND_COST = 10**10
GRAD_COST = 0
COMBINE_COST = 10**10
GATHER_COST = 10**10
PACK_COST = 10**10
F32 = jnp.float32


def dot_nt(a, b):
    return lax.dot_general(a, b, (((1,), (1,)), ((), ())), preferred_element_type=F32)


def dot_nn(a, b):
    return lax.dot_general(a, b, (((1,), (0,)), ((), ())), preferred_element_type=F32)


def dot_tn(a, b):
    return lax.dot_general(a, b, (((0,), (0,)), ((), ())), preferred_element_type=F32)


def shape(*dims, kind=BF16):
    return jax.ShapeDtypeStruct(dims, kind)


def trade(array, step):
    count = lax.axis_size("seq")
    return lax.ppermute(
        array, "seq", [(i, (i + (step if i % 2 == 0 else -step)) % count) for i in range(count)]
    )


def swap(array, mask):
    count = lax.axis_size("head")
    return lax.ppermute(array, "head", [(i, i ^ mask) for i in range(count)])


def count_of(picks, group):
    total = jnp.int32(0)
    for pick in picks:
        total = total + jnp.where(pick == group, 1, 0)
    return total.astype(F32)


def fill_multiplicity(ring, index_ref, mult_ref):
    per_block = BLK // STRIDE_ROWS
    picks = [index_ref[0, i] for i in range(index_ref.shape[1])]
    shape_of = mult_ref.shape
    lane = lax.broadcasted_iota(jnp.int32, shape_of, 1)
    mult = jnp.where(lane < 3 * BLK, 1.0, 0.0)
    if ring:
        b = lax.axis_index("seq")
        sign = 1 - 2 * (b & 1)
        counts = [count_of(picks, j) for j in range(2)]
        places = [(0, 0), (BLK, 1), (2 * BLK, -1)]
        places += [(3 * BLK + i * STRIDE_ROWS, o) for i, o in enumerate((-2, 3, 2, 4, 5))]
        for start, offset in places:
            owner = (b + 16 + sign * offset) & 7
            count = jnp.where(owner < per_block, counts[0], counts[1])
            inside = (lane >= start) & (lane < start + STRIDE_ROWS)
            mult = mult + jnp.where(inside, count, 0.0)
    else:
        for j in range((shape_of[1] - 3 * BLK) // BLK):
            start = (3 + j) * BLK
            inside = (lane >= start) & (lane < start + BLK)
            mult = mult + jnp.where(inside, count_of(picks, j), 0.0)
    mult_ref[...] = mult


def cost(flops):
    return pl.CostEstimate(flops=flops, bytes_accessed=0, transcendentals=0)


CHUNKS = 4


def row_copies(src, dst, sems, first):
    rows = dst.shape[0] // CHUNKS
    spans = [pl.ds(i * rows, rows) for i in range(CHUNKS)]
    return [pltpu.make_async_copy(src.at[span], dst.at[span], sems.at[first + i])
            for i, span in enumerate(spans)]


def slices_kernel(ring, index_hbm, w_hbm, after_ref, mult_ref, w_ref, *refs):
    del after_ref
    index_ref, sems = refs[-2:]
    slice_refs = refs[:-2]
    copies = [pltpu.make_async_copy(index_hbm, index_ref, sems.at[CHUNKS])]
    copies += row_copies(w_hbm, w_ref, sems, 0)
    for copy in copies:
        copy.start()
    copies[0].wait()
    fill_multiplicity(ring, index_ref, mult_ref)
    for copy in copies[1:]:
        copy.wait()
    width = slice_refs[0].shape[1]
    head = lax.axis_index("head")

    def columns(h):
        return pl.ds(pl.multiple_of(h * width, width), width)

    if ring:
        core = lax.axis_index("seq") & 1
        half = HD // 2
        mine_ref, whole_ref, half_ref = slice_refs
        mine_ref[...] = w_ref[:, columns(head)]
        whole_ref[...] = w_ref[:, columns(head ^ (3 - core))]
        rows = pl.ds(pl.multiple_of(core * (half - MARGIN), MARGIN), half + MARGIN)
        half_ref[...] = w_ref[rows, columns(head ^ 1)]
    else:
        for r, ref in enumerate(slice_refs):
            ref[...] = w_ref[:, columns(head ^ r)]


def weight_slices(ring, index, out_weight, heads, columns, after):
    width = out_weight.shape[1] // heads
    rows = (HD, HD, HD // 2 + MARGIN) if ring else (HD,) * heads

    def body(*refs):
        slices_kernel(ring, *refs)

    return pl.pallas_call(
        body,
        out_shape=(shape(8, columns, kind=F32), shape(*out_weight.shape))
        + tuple(shape(r, width) for r in rows),
        in_specs=[HBM] * 2 + [VMEM],
        out_specs=(VMEM,) * (2 + len(rows)),
        scratch_shapes=[
            pltpu.SMEM(index.shape, jnp.int32),
            pltpu.SemaphoreType.DMA((1 + CHUNKS,)),
        ],
        compiler_params=FULL,
        cost_estimate=cost(PREPARE_COST),
        name="slices",
    )(index, out_weight, after)


def prepare_kernel(cot_ref, w_ref, after_ref, grad_ref):
    del after_ref
    grad_ref[...] = dot_nt(cot_ref[...], w_ref[...]).astype(grad_ref.dtype)


def prepare(cotangent, out_weight, after):
    return pl.pallas_call(
        prepare_kernel,
        out_shape=shape(BLK, HD),
        in_specs=[VMEM] * 3,
        out_specs=VMEM,
        compiler_params=PARAMS,
        cost_estimate=cost(GRAD_COST),
        name="prepare",
    )(cotangent, out_weight, after)


def lead_kernel(own_ref, first_ref, mult_ref, whole_ref, near_ref, pair_ref, whole_out):
    del mult_ref
    n = STRIDE_ROWS
    near_ref[:BLK] = own_ref[...]
    near_ref[BLK:] = first_ref[:n]
    pair_ref[:n] = own_ref[:n]
    pair_ref[n:] = first_ref[:n]
    whole_out[...] = whole_ref[...]


def leads(own, first, mult, whole):
    n = STRIDE_ROWS
    return pl.pallas_call(
        lead_kernel,
        out_shape=(shape(BLK + n, PAIR), shape(2 * n, PAIR), shape(*whole.shape)),
        in_specs=[VMEM] * 4,
        out_specs=(VMEM,) * 3,
        compiler_params=PARAMS,
        name="leads",
    )(own, first, mult, whole)


def attend_kernel(blocks, pieces, mult_ref, q_ref, grad_ref, *refs):
    block_refs = refs[:blocks]
    att_ref, dq_ref = refs[blocks:blocks + 2]
    sum_refs = refs[blocks + 2:-1]
    keys_ref = refs[-1]
    total_rows = keys_ref.shape[0]
    row = 0
    for ref in block_refs:
        keys_ref[row:row + ref.shape[0], :] = ref[...]
        row += ref.shape[0]
    if row < total_rows:
        keys_ref[row:, :] = jnp.zeros((total_rows - row, PAIR), BF16)
    keys = keys_ref[:, :HD]
    values = keys_ref[:, HD:]
    q = q_ref[...]
    grad = grad_ref[...]
    mult = mult_ref[0:1, :]

    scores = dot_nt(q, keys) + jnp.where(mult > 0.0, 0.0, ABSENT)
    top = jnp.max(scores, axis=1, keepdims=True)
    terms = jnp.exp2((scores - top) * (SCALE * LOG2E)) * mult
    probability = terms * (1.0 / jnp.sum(terms, axis=1, keepdims=True))
    weights = probability.astype(BF16)
    att_ref[...] = dot_nn(weights, values).astype(BF16)

    grad_weights = dot_nt(grad, values)
    delta = jnp.sum(probability * grad_weights, axis=1, keepdims=True)
    grad_scores = (probability * (grad_weights - delta) * SCALE).astype(BF16)
    dq_ref[...] = dot_nn(grad_scores, keys).astype(BF16)
    key_terms = dot_tn(grad_scores, q)
    value_terms = dot_tn(weights, grad)
    for spans, ref in zip(pieces, sum_refs):
        row = 0
        for start, end in spans:
            rows = slice(row, row + end - start)
            ref[rows, :HD] = key_terms[start:end].astype(ref.dtype)
            ref[rows, HD:] = value_terms[start:end].astype(ref.dtype)
            row += end - start


def attend(mult, q, grad, blocks, pieces, wide):
    def body(*refs):
        attend_kernel(len(blocks), pieces, *refs)

    sums = []
    for i, spans in enumerate(pieces):
        rows = sum(end - start for start, end in spans)
        sums.append(shape(rows, PAIR, kind=F32 if i < wide else BF16))
    return pl.pallas_call(
        body,
        out_shape=(shape(BLK, HD), shape(BLK, HD), *sums),
        in_specs=[VMEM] * (3 + len(blocks)),
        out_specs=(VMEM,) * (2 + len(sums)),
        scratch_shapes=[pltpu.VMEM((mult.shape[1], PAIR), BF16)],
        compiler_params=PARAMS,
        cost_estimate=cost(ATTEND_COST),
        name="attend",
    )(mult, q, grad, *blocks)


def half_rows():
    core = lax.axis_index("seq") & 1
    return pl.ds(pl.multiple_of(core * MARGIN, MARGIN), HD // 2)


def combine_kernel(own_ref, first_ref, second_ref, plus_ref, minus_ref, whole_ref, half_ref,
                   att_ref, own_out, first_out, second_out, slices_out, att_out):
    plus = plus_ref[...].astype(F32)
    minus = minus_ref[...].astype(F32)
    n = STRIDE_ROWS
    own_out[n:] = own_ref[n:]
    own_out[:n] = own_ref[:n] + plus[:n] + minus[:n]
    second_out[n:] = second_ref[n:].astype(BF16)
    second_out[:n] = (second_ref[:n] + plus[2 * n:] + minus[n:]).astype(BF16)
    first_out[n:] = first_ref[n:].astype(BF16)
    first_out[:n] = (first_ref[:n] + plus[n:2 * n]).astype(BF16)
    att_out[...] = att_ref[...]
    row = 0
    for ref, rows in ((whole_ref, slice(0, HD)), (half_ref, half_rows())):
        for c in range(0, ref.shape[1], PAIR):
            piece = ref[rows, c:c + PAIR]
            slices_out[row:row + piece.shape[0]] = piece
            row += piece.shape[0]


def combine(own, first, second, plus, minus, whole, half, att):
    extra = (HD + HD // 2) * whole.shape[1] // PAIR
    return pl.pallas_call(
        combine_kernel,
        out_shape=(shape(BLK, PAIR, kind=F32), shape(BLK, PAIR), shape(BLK, PAIR),
                   shape(extra, PAIR), shape(BLK, HD)),
        in_specs=[VMEM] * 8,
        out_specs=(VMEM,) * 5,
        compiler_params=PARAMS,
        cost_estimate=cost(COMBINE_COST),
        name="combine",
    )(own, first, second, plus, minus, whole, half, att)


def pack_kernel(first_ref, slices_ref, after_ref, out_ref):
    del after_ref
    out_ref[:BLK] = first_ref[...]
    out_ref[BLK:] = slices_ref[...]


def pack(first, slices, after):
    return pl.pallas_call(
        pack_kernel,
        out_shape=shape(BLK + slices.shape[0], PAIR),
        in_specs=[VMEM] * 3,
        out_specs=VMEM,
        compiler_params=PARAMS,
        cost_estimate=cost(PACK_COST),
        name="pack",
    )(first, slices, after)


def project_kernel(att_ref, two_ref, three_ref, mine_ref, whole_ref, out_ref):
    core = lax.axis_index("seq") & 1
    here = jnp.where(core == 0, three_ref[...], two_ref[...])
    out_ref[...] = dot_nn(att_ref[...], mine_ref[...]) + dot_nn(here, whole_ref[...])


def project(att, two, three, mine, whole):
    return pl.pallas_call(
        project_kernel,
        out_shape=shape(BLK, mine.shape[1], kind=F32),
        in_specs=[VMEM] * 5,
        out_specs=VMEM,
        compiler_params=PARAMS,
        name="project",
    )(att, two, three, mine, whole)


def gather_kernel(one_ref, second_ref, partial_ref, out_ref):
    del second_ref, partial_ref
    out_ref[...] = one_ref[...]


def gather(one, second, partial):
    return pl.pallas_call(
        gather_kernel,
        out_shape=shape(BLK, HD),
        in_specs=[VMEM] * 3,
        out_specs=VMEM,
        compiler_params=PARAMS,
        cost_estimate=cost(GATHER_COST),
        name="gather",
    )(one, second, partial)


def settle(total, lead, dk_ref, dv_ref):
    for ref, c in ((dk_ref, 0), (dv_ref, HD)):
        ref[:STRIDE_ROWS] = lead[:, c:c + HD].astype(ref.dtype)
        ref[STRIDE_ROWS:] = total[STRIDE_ROWS:, c:c + HD].astype(ref.dtype)


def finish_ring_kernel(partial_ref, one_ref, two_ref, three_ref, half_ref, first_ref, own_ref,
                       second_ref, dq_ref, mixed_hbm, dq_hbm, dk_hbm, dv_hbm,
                       mixed_ref, dk_ref, dv_ref, sems):
    copies = []

    def send(src, dst):
        copy = pltpu.make_async_copy(src, dst, sems.at[len(copies)])
        copy.start()
        copies.append(copy)

    send(dq_ref, dq_hbm)
    core = lax.axis_index("seq") & 1
    half = HD // 2
    one = one_ref[...]
    there = jnp.where(core == 0, two_ref[...], three_ref[...])
    here_half = jnp.where(core == 0, one[:, :half], one[:, half:])
    there_half = jnp.where(core == 0, one[:, half:], one[:, :half])
    width = half_ref.shape[1]
    half_row = BLK + (width // PAIR) * HD
    for r in range(0, BLK, half):
        rows = slice(r, r + half)
        for i, c in enumerate(range(0, width, PAIR)):
            span = slice(c, c + PAIR)
            other_whole = first_ref[BLK + i * HD:BLK + (i + 1) * HD]
            other_half = first_ref[half_row + i * half:half_row + (i + 1) * half]
            mixed = partial_ref[rows, span] + dot_nn(there[rows], other_whole)
            mixed = mixed + dot_nn(here_half[rows], half_ref[half_rows(), span])
            mixed = mixed + dot_nn(there_half[rows], other_half)
            mixed_ref[rows, span] = mixed.astype(mixed_ref.dtype)
        send(mixed_ref.at[pl.ds(r, half)], mixed_hbm.at[pl.ds(r, half)])
    total = own_ref[...] + first_ref[:BLK].astype(F32) + second_ref[...].astype(F32)
    settle(total, total[:STRIDE_ROWS], dk_ref, dv_ref)
    send(dk_ref, dk_hbm)
    send(dv_ref, dv_hbm)
    for copy in copies:
        copy.wait()


def finish_ring(*args):
    width = args[0].shape[1]
    return pl.pallas_call(
        finish_ring_kernel,
        out_shape=(shape(BLK, width),) + (shape(BLK, HD),) * 3,
        in_specs=[VMEM] * len(args),
        out_specs=(HBM,) * 4,
        scratch_shapes=[
            pltpu.VMEM((BLK, width), BF16),
            pltpu.VMEM((BLK, HD), BF16),
            pltpu.VMEM((BLK, HD), BF16),
            pltpu.SemaphoreType.DMA((5,)),
        ],
        compiler_params=PARAMS,
        name="finish",
    )(*args)


def finish_kernel(count, *refs):
    att_refs = refs[:count]
    w_refs = refs[count:2 * count]
    own_ref, first_ref, second_ref, side_ref, mixed_ref, dk_ref, dv_ref = refs[2 * count:]
    mixed = None
    for ref, w in zip(att_refs, w_refs):
        term = dot_nn(ref[...], w[...])
        mixed = term if mixed is None else mixed + term
    mixed_ref[...] = mixed.astype(mixed_ref.dtype)
    total = own_ref[...] + first_ref[...].astype(F32) + second_ref[...].astype(F32)
    lead = total[:STRIDE_ROWS]
    for i in range(side_ref.shape[0] // STRIDE_ROWS):
        lead = lead + side_ref[i * STRIDE_ROWS:(i + 1) * STRIDE_ROWS].astype(F32)
    settle(total, lead, dk_ref, dv_ref)


def finish(attentions, slices, own, first, second, side):
    width = slices[0].shape[1]
    count = len(attentions)

    def body(*refs):
        finish_kernel(count, *refs)

    return pl.pallas_call(
        body,
        out_shape=(shape(BLK, width), shape(BLK, HD), shape(BLK, HD)),
        in_specs=[VMEM] * (2 * count + 4),
        out_specs=(VMEM,) * 3,
        compiler_params=PARAMS,
        name="finish",
    )(*attentions, *slices, own, first, second, side)


def spread_slice(array):
    seq = lax.axis_size("seq")
    heads = lax.axis_size("head")
    pairs = [(b * heads + h, b * heads + (h ^ (3 - b % 2))) for b in range(seq)
             for h in range(heads)]
    return lax.ppermute(array, ("seq", "head"), pairs)


def shards(queries, key_rows, value_rows, out_weight, strided_index, cotangent):
    seq = lax.axis_size("seq")
    heads = lax.axis_size("head")
    ring = seq == 8 and heads == 4
    n = STRIDE_ROWS
    side_rows = seq * n
    columns = 3 * BLK + side_rows
    own = jnp.concatenate([key_rows, value_rows], axis=1)
    first = trade(own, 1)
    mult, weight, *slices = weight_slices(
        ring, strided_index, out_weight, heads, columns, own
    )
    if ring:
        mine, whole, half = slices
        half = swap(half, 1)
        near, pair, whole = leads(own, first, mult, whole)
        grad = prepare(cotangent, weight, pair)
        whole = spread_slice(whole)
        near = trade(near, -1)
        blocks = (own, first, near, trade(pair, 3), trade(pair, 4))
        side = 3 * BLK
        places = [side + i * n for i in range(6)]
        pieces = [[(i * BLK, (i + 1) * BLK)] for i in range(3)]
        pieces += [[(places[1], places[4])], [(places[4], places[5]), (places[0], places[1])]]
        att, dq, own_sum, first_sum, second_sum, to_plus, to_minus = attend(
            mult, queries, grad, blocks, pieces, 3
        )
        far = [swap(att, 2), swap(att, 3)]
        own_sum, to_first, to_second, out_slices, last = combine(
            own_sum, first_sum, second_sum, trade(to_plus, 3), trade(to_minus, -3), whole, half,
            att,
        )
        from_second = trade(to_second, -1)
        packed = trade(pack(to_first, out_slices, far[1]), 1)
        partial = project(att, *far, mine, whole)
        one = gather(swap(last, 1), from_second, partial)
        mixed, dq, dk, dv = finish_ring(
            partial, one, *far, half, packed, own_sum, from_second, dq
        )
    else:
        second = trade(own, -1)
        grad = prepare(cotangent, weight, own)
        slices = [slices[0]] + [swap(slices[r], r) for r in range(1, heads)]
        spread = jnp.broadcast_to(own[None, :n], (seq, n, PAIR))
        side = lax.all_to_all(spread, "seq", 0, 0).reshape(side_rows, PAIR)
        pieces = [[(i * BLK, (i + 1) * BLK)] for i in range(3)] + [[(3 * BLK, columns)]]
        att, dq, own_sum, to_first, to_second, to_side = attend(
            mult, queries, grad, (own, first, second, side), pieces, 1
        )
        from_side = lax.all_to_all(to_side.reshape(seq, n, PAIR), "seq", 0, 0)
        mixed, dk, dv = finish(
            [att] + [swap(att, r) for r in range(1, heads)], slices, own_sum,
            trade(to_first, 1), trade(to_second, -1), from_side.reshape(side_rows, PAIR),
        )
    return (mixed, dq, dk, dv)


def solution(mesh):
    in_specs = (
        P("seq", "head"),
        P("seq", "head"),
        P("seq", "head"),
        P("head", None),
        P("seq", None),
        P("seq", None),
    )
    out_specs = (P("seq", "head"), P("seq", "head"), P("seq", "head"), P("seq", "head"))
    return jax.shard_map(shards, mesh=mesh, in_specs=in_specs, out_specs=out_specs, check_vma=False)
```

```python
import jax
import jax.numpy as jnp
from jax import lax
from jax.experimental import pallas as pl
from jax.experimental.pallas import tpu as pltpu
from jax.sharding import PartitionSpec as P

HD = 128
BLK = 128
STRIDE_ROWS = 32
MARGIN = 16
PAIR = 2 * HD
SCALE = HD ** (-0.5)
LOG2E = 1.4426950408889634
ABSENT = -1e30
VMEM = pl.BlockSpec(memory_space=pltpu.VMEM)
HBM = pl.BlockSpec(memory_space=pltpu.HBM)
PARAMS = pltpu.CompilerParams(vmem_limit_bytes=40 * 1024 * 1024)
FULL = pltpu.CompilerParams(vmem_limit_bytes=int(52.8 * 1024 * 1024))
BF16 = jnp.bfloat16
PREPARE_COST = 10**10
ATTEND_COST = 10**10
GRAD_COST = 0
COMBINE_COST = 10**10
GATHER_COST = 10**10
PACK_COST = 10**10
F32 = jnp.float32


def dot_nt(a, b):
    return lax.dot_general(a, b, (((1,), (1,)), ((), ())), preferred_element_type=F32)


def dot_nn(a, b):
    return lax.dot_general(a, b, (((1,), (0,)), ((), ())), preferred_element_type=F32)


def dot_tn(a, b):
    return lax.dot_general(a, b, (((0,), (0,)), ((), ())), preferred_element_type=F32)


def shape(*dims, kind=BF16):
    return jax.ShapeDtypeStruct(dims, kind)


def trade(array, step):
    count = lax.axis_size("seq")
    return lax.ppermute(
        array, "seq", [(i, (i + (step if i % 2 == 0 else -step)) % count) for i in range(count)]
    )


def swap(array, mask):
    count = lax.axis_size("head")
    return lax.ppermute(array, "head", [(i, i ^ mask) for i in range(count)])


def count_of(picks, group):
    total = jnp.int32(0)
    for pick in picks:
        total = total + jnp.where(pick == group, 1, 0)
    return total.astype(F32)


def fill_multiplicity(ring, index_ref, mult_ref):
    per_block = BLK // STRIDE_ROWS
    picks = [index_ref[0, i] for i in range(index_ref.shape[1])]
    shape_of = mult_ref.shape
    lane = lax.broadcasted_iota(jnp.int32, shape_of, 1)
    mult = jnp.where(lane < 3 * BLK, 1.0, 0.0)
    if ring:
        b = lax.axis_index("seq")
        sign = 1 - 2 * (b & 1)
        counts = [count_of(picks, j) for j in range(2)]
        places = [(0, 0), (BLK, 1), (2 * BLK, -1)]
        places += [(3 * BLK + i * STRIDE_ROWS, o) for i, o in enumerate((-2, 3, 2, 4, 5))]
        for start, offset in places:
            owner = (b + 16 + sign * offset) & 7
            count = jnp.where(owner < per_block, counts[0], counts[1])
            inside = (lane >= start) & (lane < start + STRIDE_ROWS)
            mult = mult + jnp.where(inside, count, 0.0)
    else:
        for j in range((shape_of[1] - 3 * BLK) // BLK):
            start = (3 + j) * BLK
            inside = (lane >= start) & (lane < start + BLK)
            mult = mult + jnp.where(inside, count_of(picks, j), 0.0)
    mult_ref[...] = mult


def cost(flops):
    return pl.CostEstimate(flops=flops, bytes_accessed=0, transcendentals=0)


CHUNKS = 4


def row_copies(src, dst, sems, first):
    rows = dst.shape[0] // CHUNKS
    spans = [pl.ds(i * rows, rows) for i in range(CHUNKS)]
    return [pltpu.make_async_copy(src.at[span], dst.at[span], sems.at[first + i])
            for i, span in enumerate(spans)]


def slices_kernel(ring, index_hbm, q_hbm, w_hbm, after_ref, mult_ref, q_ref, w_ref, *refs):
    del after_ref
    index_ref, sems = refs[-2:]
    slice_refs = refs[:-2]
    copies = [pltpu.make_async_copy(index_hbm, index_ref, sems.at[CHUNKS])]
    copies += row_copies(w_hbm, w_ref, sems, 0)
    copies.append(pltpu.make_async_copy(q_hbm, q_ref, sems.at[CHUNKS + 1]))
    for copy in copies:
        copy.start()
    copies[0].wait()
    fill_multiplicity(ring, index_ref, mult_ref)
    for copy in copies[1:]:
        copy.wait()
    width = slice_refs[0].shape[1]
    head = lax.axis_index("head")

    def columns(h):
        return pl.ds(pl.multiple_of(h * width, width), width)

    if ring:
        core = lax.axis_index("seq") & 1
        half = HD // 2
        mine_ref, whole_ref, half_ref = slice_refs
        mine_ref[...] = w_ref[:, columns(head)]
        whole_ref[...] = w_ref[:, columns(head ^ (3 - core))]
        rows = pl.ds(pl.multiple_of(core * (half - MARGIN), MARGIN), half + MARGIN)
        half_ref[...] = w_ref[rows, columns(head ^ 1)]
    else:
        for r, ref in enumerate(slice_refs):
            ref[...] = w_ref[:, columns(head ^ r)]


def weight_slices(ring, index, queries, out_weight, heads, columns, after):
    width = out_weight.shape[1] // heads
    rows = (HD, HD, HD // 2 + MARGIN) if ring else (HD,) * heads

    def body(*refs):
        slices_kernel(ring, *refs)

    return pl.pallas_call(
        body,
        out_shape=(shape(8, columns, kind=F32), shape(BLK, HD), shape(*out_weight.shape))
        + tuple(shape(r, width) for r in rows),
        in_specs=[HBM] * 3 + [VMEM],
        out_specs=(VMEM,) * (3 + len(rows)),
        scratch_shapes=[
            pltpu.SMEM(index.shape, jnp.int32),
            pltpu.SemaphoreType.DMA((2 + CHUNKS,)),
        ],
        compiler_params=FULL,
        cost_estimate=cost(PREPARE_COST),
        name="slices",
    )(index, queries, out_weight, after)


def prepare_kernel(cot_ref, w_ref, after_ref, grad_ref):
    del after_ref
    grad_ref[...] = dot_nt(cot_ref[...], w_ref[...]).astype(grad_ref.dtype)


def prepare(cotangent, out_weight, after):
    return pl.pallas_call(
        prepare_kernel,
        out_shape=shape(BLK, HD),
        in_specs=[VMEM] * 3,
        out_specs=VMEM,
        compiler_params=PARAMS,
        cost_estimate=cost(GRAD_COST),
        name="prepare",
    )(cotangent, out_weight, after)


def lead_kernel(own_ref, first_ref, mult_ref, whole_ref, near_ref, pair_ref, whole_out):
    del mult_ref
    n = STRIDE_ROWS
    near_ref[:BLK] = own_ref[...]
    near_ref[BLK:] = first_ref[:n]
    pair_ref[:n] = own_ref[:n]
    pair_ref[n:] = first_ref[:n]
    whole_out[...] = whole_ref[...]


def leads(own, first, mult, whole):
    n = STRIDE_ROWS
    return pl.pallas_call(
        lead_kernel,
        out_shape=(shape(BLK + n, PAIR), shape(2 * n, PAIR), shape(*whole.shape)),
        in_specs=[VMEM] * 4,
        out_specs=(VMEM,) * 3,
        compiler_params=PARAMS,
        name="leads",
    )(own, first, mult, whole)


def attend_kernel(blocks, pieces, mult_ref, q_ref, grad_ref, *refs):
    block_refs = refs[:blocks]
    att_ref, dq_ref = refs[blocks:blocks + 2]
    sum_refs = refs[blocks + 2:-1]
    keys_ref = refs[-1]
    total_rows = keys_ref.shape[0]
    row = 0
    for ref in block_refs:
        keys_ref[row:row + ref.shape[0], :] = ref[...]
        row += ref.shape[0]
    if row < total_rows:
        keys_ref[row:, :] = jnp.zeros((total_rows - row, PAIR), BF16)
    keys = keys_ref[:, :HD]
    values = keys_ref[:, HD:]
    q = q_ref[...]
    grad = grad_ref[...]
    mult = mult_ref[0:1, :]

    scores = dot_nt(q, keys) + jnp.where(mult > 0.0, 0.0, ABSENT)
    top = jnp.max(scores, axis=1, keepdims=True)
    terms = jnp.exp2((scores - top) * (SCALE * LOG2E)) * mult
    probability = terms * (1.0 / jnp.sum(terms, axis=1, keepdims=True))
    weights = probability.astype(BF16)
    att_ref[...] = dot_nn(weights, values).astype(BF16)

    grad_weights = dot_nt(grad, values)
    delta = jnp.sum(probability * grad_weights, axis=1, keepdims=True)
    grad_scores = (probability * (grad_weights - delta) * SCALE).astype(BF16)
    dq_ref[...] = dot_nn(grad_scores, keys).astype(BF16)
    key_terms = dot_tn(grad_scores, q)
    value_terms = dot_tn(weights, grad)
    for spans, ref in zip(pieces, sum_refs):
        row = 0
        for start, end in spans:
            rows = slice(row, row + end - start)
            ref[rows, :HD] = key_terms[start:end].astype(ref.dtype)
            ref[rows, HD:] = value_terms[start:end].astype(ref.dtype)
            row += end - start


def attend(mult, q, grad, blocks, pieces, wide):
    def body(*refs):
        attend_kernel(len(blocks), pieces, *refs)

    sums = []
    for i, spans in enumerate(pieces):
        rows = sum(end - start for start, end in spans)
        sums.append(shape(rows, PAIR, kind=F32 if i < wide else BF16))
    return pl.pallas_call(
        body,
        out_shape=(shape(BLK, HD), shape(BLK, HD), *sums),
        in_specs=[VMEM] * (3 + len(blocks)),
        out_specs=(VMEM,) * (2 + len(sums)),
        scratch_shapes=[pltpu.VMEM((mult.shape[1], PAIR), BF16)],
        compiler_params=PARAMS,
        cost_estimate=cost(ATTEND_COST),
        name="attend",
    )(mult, q, grad, *blocks)


def half_rows():
    core = lax.axis_index("seq") & 1
    return pl.ds(pl.multiple_of(core * MARGIN, MARGIN), HD // 2)


def combine_kernel(own_ref, first_ref, second_ref, plus_ref, minus_ref, whole_ref, half_ref,
                   att_ref, own_out, first_out, second_out, slices_out, att_out):
    plus = plus_ref[...].astype(F32)
    minus = minus_ref[...].astype(F32)
    n = STRIDE_ROWS
    own_out[n:] = own_ref[n:]
    own_out[:n] = own_ref[:n] + plus[:n] + minus[:n]
    second_out[n:] = second_ref[n:].astype(BF16)
    second_out[:n] = (second_ref[:n] + plus[2 * n:] + minus[n:]).astype(BF16)
    first_out[n:] = first_ref[n:].astype(BF16)
    first_out[:n] = (first_ref[:n] + plus[n:2 * n]).astype(BF16)
    att_out[...] = att_ref[...]
    row = 0
    for ref, rows in ((whole_ref, slice(0, HD)), (half_ref, half_rows())):
        for c in range(0, ref.shape[1], PAIR):
            piece = ref[rows, c:c + PAIR]
            slices_out[row:row + piece.shape[0]] = piece
            row += piece.shape[0]


def combine(own, first, second, plus, minus, whole, half, att):
    extra = (HD + HD // 2) * whole.shape[1] // PAIR
    return pl.pallas_call(
        combine_kernel,
        out_shape=(shape(BLK, PAIR, kind=F32), shape(BLK, PAIR), shape(BLK, PAIR),
                   shape(extra, PAIR), shape(BLK, HD)),
        in_specs=[VMEM] * 8,
        out_specs=(VMEM,) * 5,
        compiler_params=PARAMS,
        cost_estimate=cost(COMBINE_COST),
        name="combine",
    )(own, first, second, plus, minus, whole, half, att)


def pack_kernel(first_ref, slices_ref, after_ref, out_ref):
    del after_ref
    out_ref[:BLK] = first_ref[...]
    out_ref[BLK:] = slices_ref[...]


def pack(first, slices, after):
    return pl.pallas_call(
        pack_kernel,
        out_shape=shape(BLK + slices.shape[0], PAIR),
        in_specs=[VMEM] * 3,
        out_specs=VMEM,
        compiler_params=PARAMS,
        cost_estimate=cost(PACK_COST),
        name="pack",
    )(first, slices, after)


def project_kernel(att_ref, two_ref, three_ref, mine_ref, whole_ref, out_ref):
    core = lax.axis_index("seq") & 1
    here = jnp.where(core == 0, three_ref[...], two_ref[...])
    out_ref[...] = dot_nn(att_ref[...], mine_ref[...]) + dot_nn(here, whole_ref[...])


def project(att, two, three, mine, whole):
    return pl.pallas_call(
        project_kernel,
        out_shape=shape(BLK, mine.shape[1], kind=F32),
        in_specs=[VMEM] * 5,
        out_specs=VMEM,
        compiler_params=PARAMS,
        name="project",
    )(att, two, three, mine, whole)


def gather_kernel(one_ref, second_ref, partial_ref, out_ref):
    del second_ref, partial_ref
    out_ref[...] = one_ref[...]


def gather(one, second, partial):
    return pl.pallas_call(
        gather_kernel,
        out_shape=shape(BLK, HD),
        in_specs=[VMEM] * 3,
        out_specs=VMEM,
        compiler_params=PARAMS,
        cost_estimate=cost(GATHER_COST),
        name="gather",
    )(one, second, partial)


def settle(total, lead, dk_ref, dv_ref):
    for ref, c in ((dk_ref, 0), (dv_ref, HD)):
        ref[:STRIDE_ROWS] = lead[:, c:c + HD].astype(ref.dtype)
        ref[STRIDE_ROWS:] = total[STRIDE_ROWS:, c:c + HD].astype(ref.dtype)


def finish_ring_kernel(partial_ref, one_ref, two_ref, three_ref, half_ref, first_ref, own_ref,
                       second_ref, dq_ref, mixed_hbm, dq_hbm, dk_hbm, dv_hbm,
                       mixed_ref, dk_ref, dv_ref, sems):
    copies = []

    def send(src, dst):
        copy = pltpu.make_async_copy(src, dst, sems.at[len(copies)])
        copy.start()
        copies.append(copy)

    send(dq_ref, dq_hbm)
    core = lax.axis_index("seq") & 1
    half = HD // 2
    one = one_ref[...]
    there = jnp.where(core == 0, two_ref[...], three_ref[...])
    here_half = jnp.where(core == 0, one[:, :half], one[:, half:])
    there_half = jnp.where(core == 0, one[:, half:], one[:, :half])
    width = half_ref.shape[1]
    half_row = BLK + (width // PAIR) * HD
    for r in range(0, BLK, half):
        rows = slice(r, r + half)
        for i, c in enumerate(range(0, width, PAIR)):
            span = slice(c, c + PAIR)
            other_whole = first_ref[BLK + i * HD:BLK + (i + 1) * HD]
            other_half = first_ref[half_row + i * half:half_row + (i + 1) * half]
            mixed = partial_ref[rows, span] + dot_nn(there[rows], other_whole)
            mixed = mixed + dot_nn(here_half[rows], half_ref[half_rows(), span])
            mixed = mixed + dot_nn(there_half[rows], other_half)
            mixed_ref[rows, span] = mixed.astype(mixed_ref.dtype)
        send(mixed_ref.at[pl.ds(r, half)], mixed_hbm.at[pl.ds(r, half)])
    total = own_ref[...] + first_ref[:BLK].astype(F32) + second_ref[...].astype(F32)
    settle(total, total[:STRIDE_ROWS], dk_ref, dv_ref)
    send(dk_ref, dk_hbm)
    send(dv_ref, dv_hbm)
    for copy in copies:
        copy.wait()


def finish_ring(*args):
    width = args[0].shape[1]
    return pl.pallas_call(
        finish_ring_kernel,
        out_shape=(shape(BLK, width),) + (shape(BLK, HD),) * 3,
        in_specs=[VMEM] * len(args),
        out_specs=(HBM,) * 4,
        scratch_shapes=[
            pltpu.VMEM((BLK, width), BF16),
            pltpu.VMEM((BLK, HD), BF16),
            pltpu.VMEM((BLK, HD), BF16),
            pltpu.SemaphoreType.DMA((5,)),
        ],
        compiler_params=PARAMS,
        name="finish",
    )(*args)


def finish_kernel(count, *refs):
    att_refs = refs[:count]
    w_refs = refs[count:2 * count]
    own_ref, first_ref, second_ref, side_ref, mixed_ref, dk_ref, dv_ref = refs[2 * count:]
    mixed = None
    for ref, w in zip(att_refs, w_refs):
        term = dot_nn(ref[...], w[...])
        mixed = term if mixed is None else mixed + term
    mixed_ref[...] = mixed.astype(mixed_ref.dtype)
    total = own_ref[...] + first_ref[...].astype(F32) + second_ref[...].astype(F32)
    lead = total[:STRIDE_ROWS]
    for i in range(side_ref.shape[0] // STRIDE_ROWS):
        lead = lead + side_ref[i * STRIDE_ROWS:(i + 1) * STRIDE_ROWS].astype(F32)
    settle(total, lead, dk_ref, dv_ref)


def finish(attentions, slices, own, first, second, side):
    width = slices[0].shape[1]
    count = len(attentions)

    def body(*refs):
        finish_kernel(count, *refs)

    return pl.pallas_call(
        body,
        out_shape=(shape(BLK, width), shape(BLK, HD), shape(BLK, HD)),
        in_specs=[VMEM] * (2 * count + 4),
        out_specs=(VMEM,) * 3,
        compiler_params=PARAMS,
        name="finish",
    )(*attentions, *slices, own, first, second, side)


def spread_slice(array):
    seq = lax.axis_size("seq")
    heads = lax.axis_size("head")
    pairs = [(b * heads + h, b * heads + (h ^ (3 - b % 2))) for b in range(seq)
             for h in range(heads)]
    return lax.ppermute(array, ("seq", "head"), pairs)


def shards(queries, key_rows, value_rows, out_weight, strided_index, cotangent):
    seq = lax.axis_size("seq")
    heads = lax.axis_size("head")
    ring = seq == 8 and heads == 4
    n = STRIDE_ROWS
    side_rows = seq * n
    columns = 3 * BLK + side_rows
    own = jnp.concatenate([key_rows, value_rows], axis=1)
    first = trade(own, 1)
    mult, queries, weight, *slices = weight_slices(
        ring, strided_index, queries, out_weight, heads, columns, own
    )
    if ring:
        mine, whole, half = slices
        half = swap(half, 1)
        near, pair, whole = leads(own, first, mult, whole)
        grad = prepare(cotangent, weight, pair)
        whole = spread_slice(whole)
        near = trade(near, -1)
        blocks = (own, first, near, trade(pair, 3), trade(pair, 4))
        side = 3 * BLK
        places = [side + i * n for i in range(6)]
        pieces = [[(i * BLK, (i + 1) * BLK)] for i in range(3)]
        pieces += [[(places[1], places[4])], [(places[4], places[5]), (places[0], places[1])]]
        att, dq, own_sum, first_sum, second_sum, to_plus, to_minus = attend(
            mult, queries, grad, blocks, pieces, 3
        )
        far = [swap(att, 2), swap(att, 3)]
        own_sum, to_first, to_second, out_slices, last = combine(
            own_sum, first_sum, second_sum, trade(to_plus, 3), trade(to_minus, -3), whole, half,
            att,
        )
        from_second = trade(to_second, -1)
        packed = trade(pack(to_first, out_slices, far[1]), 1)
        partial = project(att, *far, mine, whole)
        one = gather(swap(last, 1), from_second, partial)
        mixed, dq, dk, dv = finish_ring(
            partial, one, *far, half, packed, own_sum, from_second, dq
        )
    else:
        second = trade(own, -1)
        grad = prepare(cotangent, weight, own)
        slices = [slices[0]] + [swap(slices[r], r) for r in range(1, heads)]
        spread = jnp.broadcast_to(own[None, :n], (seq, n, PAIR))
        side = lax.all_to_all(spread, "seq", 0, 0).reshape(side_rows, PAIR)
        pieces = [[(i * BLK, (i + 1) * BLK)] for i in range(3)] + [[(3 * BLK, columns)]]
        att, dq, own_sum, to_first, to_second, to_side = attend(
            mult, queries, grad, (own, first, second, side), pieces, 1
        )
        from_side = lax.all_to_all(to_side.reshape(seq, n, PAIR), "seq", 0, 0)
        mixed, dk, dv = finish(
            [att] + [swap(att, r) for r in range(1, heads)], slices, own_sum,
            trade(to_first, 1), trade(to_second, -1), from_side.reshape(side_rows, PAIR),
        )
    return (mixed, dq, dk, dv)


def solution(mesh):
    in_specs = (
        P("seq", "head"),
        P("seq", "head"),
        P("seq", "head"),
        P("head", None),
        P("seq", None),
        P("seq", None),
    )
    out_specs = (P("seq", "head"), P("seq", "head"), P("seq", "head"), P("seq", "head"))
    return jax.shard_map(shards, mesh=mesh, in_specs=in_specs, out_specs=out_specs, check_vma=False)
```

```python
import jax
import jax.numpy as jnp
from jax import lax
from jax.experimental import pallas as pl
from jax.experimental.pallas import tpu as pltpu
from jax.sharding import PartitionSpec as P

HD = 128
BLK = 128
STRIDE_ROWS = 32
MARGIN = 16
PAIR = 2 * HD
SCALE = HD ** (-0.5)
LOG2E = 1.4426950408889634
ABSENT = -1e30
VMEM = pl.BlockSpec(memory_space=pltpu.VMEM)
HBM = pl.BlockSpec(memory_space=pltpu.HBM)
PARAMS = pltpu.CompilerParams(vmem_limit_bytes=40 * 1024 * 1024)
FULL = pltpu.CompilerParams(vmem_limit_bytes=int(52.8 * 1024 * 1024))
BF16 = jnp.bfloat16
PREPARE_COST = 10**10
ATTEND_COST = 10**10
GRAD_COST = 0
COMBINE_COST = 10**10
GATHER_COST = 10**10
PACK_COST = 6*10**8
F32 = jnp.float32


def dot_nt(a, b):
    return lax.dot_general(a, b, (((1,), (1,)), ((), ())), preferred_element_type=F32)


def dot_nn(a, b):
    return lax.dot_general(a, b, (((1,), (0,)), ((), ())), preferred_element_type=F32)


def dot_tn(a, b):
    return lax.dot_general(a, b, (((0,), (0,)), ((), ())), preferred_element_type=F32)


def shape(*dims, kind=BF16):
    return jax.ShapeDtypeStruct(dims, kind)


def trade(array, step):
    count = lax.axis_size("seq")
    return lax.ppermute(
        array, "seq", [(i, (i + (step if i % 2 == 0 else -step)) % count) for i in range(count)]
    )


def swap(array, mask):
    count = lax.axis_size("head")
    return lax.ppermute(array, "head", [(i, i ^ mask) for i in range(count)])


def count_of(picks, group):
    total = jnp.int32(0)
    for pick in picks:
        total = total + jnp.where(pick == group, 1, 0)
    return total.astype(F32)


def fill_multiplicity(ring, index_ref, mult_ref):
    per_block = BLK // STRIDE_ROWS
    picks = [index_ref[0, i] for i in range(index_ref.shape[1])]
    shape_of = mult_ref.shape
    lane = lax.broadcasted_iota(jnp.int32, shape_of, 1)
    mult = jnp.where(lane < 3 * BLK, 1.0, 0.0)
    if ring:
        b = lax.axis_index("seq")
        sign = 1 - 2 * (b & 1)
        counts = [count_of(picks, j) for j in range(2)]
        places = [(0, 0), (BLK, 1), (2 * BLK, -1)]
        places += [(3 * BLK + i * STRIDE_ROWS, o) for i, o in enumerate((-2, 3, 2, 4, 5))]
        for start, offset in places:
            owner = (b + 16 + sign * offset) & 7
            count = jnp.where(owner < per_block, counts[0], counts[1])
            inside = (lane >= start) & (lane < start + STRIDE_ROWS)
            mult = mult + jnp.where(inside, count, 0.0)
    else:
        for j in range((shape_of[1] - 3 * BLK) // BLK):
            start = (3 + j) * BLK
            inside = (lane >= start) & (lane < start + BLK)
            mult = mult + jnp.where(inside, count_of(picks, j), 0.0)
    mult_ref[...] = mult


def cost(flops):
    return pl.CostEstimate(flops=flops, bytes_accessed=0, transcendentals=0)


CHUNKS = 4


def row_copies(src, dst, sems, first):
    rows = dst.shape[0] // CHUNKS
    spans = [pl.ds(i * rows, rows) for i in range(CHUNKS)]
    return [pltpu.make_async_copy(src.at[span], dst.at[span], sems.at[first + i])
            for i, span in enumerate(spans)]


def slices_kernel(ring, index_hbm, q_hbm, w_hbm, after_ref, mult_ref, q_ref, w_ref, *refs):
    del after_ref
    index_ref, sems = refs[-2:]
    slice_refs = refs[:-2]
    copies = [pltpu.make_async_copy(index_hbm, index_ref, sems.at[CHUNKS])]
    copies += row_copies(w_hbm, w_ref, sems, 0)
    copies.append(pltpu.make_async_copy(q_hbm, q_ref, sems.at[CHUNKS + 1]))
    for copy in copies:
        copy.start()
    copies[0].wait()
    fill_multiplicity(ring, index_ref, mult_ref)
    for copy in copies[1:]:
        copy.wait()
    width = slice_refs[0].shape[1]
    head = lax.axis_index("head")

    def columns(h):
        return pl.ds(pl.multiple_of(h * width, width), width)

    if ring:
        core = lax.axis_index("seq") & 1
        half = HD // 2
        mine_ref, whole_ref, half_ref = slice_refs
        mine_ref[...] = w_ref[:, columns(head)]
        whole_ref[...] = w_ref[:, columns(head ^ (3 - core))]
        rows = pl.ds(pl.multiple_of(core * (half - MARGIN), MARGIN), half + MARGIN)
        half_ref[...] = w_ref[rows, columns(head ^ 1)]
    else:
        for r, ref in enumerate(slice_refs):
            ref[...] = w_ref[:, columns(head ^ r)]


def weight_slices(ring, index, queries, out_weight, heads, columns, after):
    width = out_weight.shape[1] // heads
    rows = (HD, HD, HD // 2 + MARGIN) if ring else (HD,) * heads

    def body(*refs):
        slices_kernel(ring, *refs)

    return pl.pallas_call(
        body,
        out_shape=(shape(8, columns, kind=F32), shape(BLK, HD), shape(*out_weight.shape))
        + tuple(shape(r, width) for r in rows),
        in_specs=[HBM] * 3 + [VMEM],
        out_specs=(VMEM,) * (3 + len(rows)),
        scratch_shapes=[
            pltpu.SMEM(index.shape, jnp.int32),
            pltpu.SemaphoreType.DMA((2 + CHUNKS,)),
        ],
        compiler_params=FULL,
        cost_estimate=cost(PREPARE_COST),
        name="slices",
    )(index, queries, out_weight, after)


def prepare_kernel(cot_ref, w_ref, after_ref, mult_ref, q_ref, own_ref, first_ref,
                   grad_ref, *near_refs):
    del after_ref
    grad_ref[...] = dot_nt(cot_ref[...], w_ref[...]).astype(grad_ref.dtype)
    near_kernel(mult_ref, q_ref, grad_ref, own_ref, first_ref, *near_refs)


def prepare(cotangent, out_weight, after, mult, q, own, first):
    return pl.pallas_call(
        prepare_kernel,
        out_shape=(shape(BLK, HD), shape(BLK, 2 * BLK, kind=F32), shape(BLK, 2 * BLK, kind=F32),
                   shape(BLK, HD, kind=F32), shape(3, BLK, HD, kind=F32)),
        in_specs=[VMEM] * 7,
        out_specs=(VMEM,) * 5,
        compiler_params=PARAMS,
        cost_estimate=cost(GRAD_COST),
        name="prepare",
    )(cotangent, out_weight, after, mult, q, own, first)


def lead_kernel(own_ref, first_ref, mult_ref, whole_ref, near_ref, pair_ref, whole_out):
    del mult_ref
    n = STRIDE_ROWS
    near_ref[:BLK] = own_ref[...]
    near_ref[BLK:] = first_ref[:n]
    pair_ref[:n] = own_ref[:n]
    pair_ref[n:] = first_ref[:n]
    whole_out[...] = whole_ref[...]


def leads(own, first, mult, whole):
    n = STRIDE_ROWS
    return pl.pallas_call(
        lead_kernel,
        out_shape=(shape(BLK + n, PAIR), shape(2 * n, PAIR), shape(*whole.shape)),
        in_specs=[VMEM] * 4,
        out_specs=(VMEM,) * 3,
        compiler_params=PARAMS,
        name="leads",
    )(own, first, mult, whole)


def near_kernel(mult_ref, q_ref, grad_ref, own_ref, first_ref,
                terms_ref, products_ref, sum_ref, stats_ref):
    q = q_ref[...]
    grad = grad_ref[...]
    keys = jnp.concatenate([own_ref[:, :HD], first_ref[:, :HD]], axis=0)
    values = jnp.concatenate([own_ref[:, HD:], first_ref[:, HD:]], axis=0)
    scores = dot_nt(q, keys)
    top = jnp.max(scores, axis=1, keepdims=True)
    terms = jnp.exp2((scores - top) * (SCALE * LOG2E)) * mult_ref[0:1, :2 * BLK]
    products = dot_nt(grad, values)
    terms_ref[...] = terms
    products_ref[...] = products
    sum_ref[...] = dot_nn(terms.astype(BF16), values)
    stats_ref[0] = jnp.broadcast_to(top, (BLK, HD))
    stats_ref[1] = jnp.broadcast_to(jnp.sum(terms, axis=1, keepdims=True), (BLK, HD))
    delta = jnp.sum(terms * products, axis=1, keepdims=True)
    stats_ref[2] = jnp.broadcast_to(delta, (BLK, HD))


def attend_kernel(blocks, pieces, mult_ref, q_ref, grad_ref, terms_ref, products_ref, sum_ref,
                  stats_ref, *refs):
    block_refs = refs[:blocks]
    att_ref, dq_ref = refs[blocks:blocks + 2]
    out_refs = refs[blocks + 2:-1]
    keys_ref = refs[-1]
    total_rows = keys_ref.shape[0]
    row = 0
    for ref in block_refs[2:]:
        keys_ref[row:row + ref.shape[0], :] = ref[...]
        row += ref.shape[0]
    if row < total_rows:
        keys_ref[row:, :] = jnp.zeros((total_rows - row, PAIR), BF16)
    keys = keys_ref[:, :HD]
    values = keys_ref[:, HD:]
    q = q_ref[...]
    grad = grad_ref[...]
    mult = mult_ref[0:1, 2 * BLK:]

    scores = dot_nt(q, keys) + jnp.where(mult > 0.0, 0.0, ABSENT)
    grad_weights = dot_nt(grad, values)
    near_top = stats_ref[0, :, 0:1]
    top = jnp.maximum(near_top, jnp.max(scores, axis=1, keepdims=True))
    terms = jnp.exp2((scores - top) * (SCALE * LOG2E)) * mult
    near_factor = jnp.exp2((near_top - top) * (SCALE * LOG2E))
    total = near_factor * stats_ref[1, :, 0:1] + jnp.sum(terms, axis=1, keepdims=True)
    inverse = 1.0 / total
    near_scale = near_factor * inverse
    probability = terms * inverse
    weights = probability.astype(BF16)
    att_ref[...] = (dot_nn(weights, values) + sum_ref[...] * near_scale).astype(BF16)

    delta = jnp.sum(probability * grad_weights, axis=1, keepdims=True)
    delta = delta + near_scale * stats_ref[2, :, 0:1]
    near_probability = terms_ref[...] * near_scale
    near_weights = near_probability.astype(BF16)
    near_scores = (near_probability * (products_ref[...] - delta) * SCALE).astype(BF16)
    grad_scores = (probability * (grad_weights - delta) * SCALE).astype(BF16)
    dq = dot_nn(grad_scores, keys)
    dq = dq + dot_nn(near_scores[:, :BLK], block_refs[0][:, :HD])
    dq = dq + dot_nn(near_scores[:, BLK:], block_refs[1][:, :HD])
    dq_ref[...] = dq.astype(BF16)
    key_terms = (dot_tn(near_scores, q), dot_tn(grad_scores, q))
    value_terms = (dot_tn(near_weights, grad), dot_tn(weights, grad))
    for spans, ref in zip(pieces, out_refs):
        row = 0
        for start, end in spans:
            rows = slice(row, row + end - start)
            part = 0 if start < 2 * BLK else 1
            source = slice(start - part * 2 * BLK, end - part * 2 * BLK)
            ref[rows, :HD] = key_terms[part][source].astype(ref.dtype)
            ref[rows, HD:] = value_terms[part][source].astype(ref.dtype)
            row += end - start


def attend(mult, q, grad, near, blocks, pieces, wide):
    def body(*refs):
        attend_kernel(len(blocks), pieces, *refs)

    sums = []
    for i, spans in enumerate(pieces):
        rows = sum(end - start for start, end in spans)
        sums.append(shape(rows, PAIR, kind=F32 if i < wide else BF16))
    return pl.pallas_call(
        body,
        out_shape=(shape(BLK, HD), shape(BLK, HD), *sums),
        in_specs=[VMEM] * (7 + len(blocks)),
        out_specs=(VMEM,) * (2 + len(sums)),
        scratch_shapes=[pltpu.VMEM((mult.shape[1] - 2 * BLK, PAIR), BF16)],
        compiler_params=PARAMS,
        cost_estimate=cost(ATTEND_COST),
        name="attend",
    )(mult, q, grad, *near, *blocks)


def half_rows():
    core = lax.axis_index("seq") & 1
    return pl.ds(pl.multiple_of(core * MARGIN, MARGIN), HD // 2)


def combine_kernel(own_ref, first_ref, second_ref, plus_ref, minus_ref, whole_ref, half_ref,
                   att_ref, own_out, first_out, second_out, slices_out, att_out):
    plus = plus_ref[...].astype(F32)
    minus = minus_ref[...].astype(F32)
    n = STRIDE_ROWS
    own_out[n:] = own_ref[n:]
    own_out[:n] = own_ref[:n] + plus[:n] + minus[:n]
    second_out[n:] = second_ref[n:].astype(BF16)
    second_out[:n] = (second_ref[:n] + plus[2 * n:] + minus[n:]).astype(BF16)
    first_out[n:] = first_ref[n:].astype(BF16)
    first_out[:n] = (first_ref[:n] + plus[n:2 * n]).astype(BF16)
    att_out[...] = att_ref[...]
    row = 0
    for ref, rows in ((whole_ref, slice(0, HD)), (half_ref, half_rows())):
        for c in range(0, ref.shape[1], PAIR):
            piece = ref[rows, c:c + PAIR]
            slices_out[row:row + piece.shape[0]] = piece
            row += piece.shape[0]


def combine(own, first, second, plus, minus, whole, half, att):
    extra = (HD + HD // 2) * whole.shape[1] // PAIR
    return pl.pallas_call(
        combine_kernel,
        out_shape=(shape(BLK, PAIR, kind=F32), shape(BLK, PAIR), shape(BLK, PAIR),
                   shape(extra, PAIR), shape(BLK, HD)),
        in_specs=[VMEM] * 8,
        out_specs=(VMEM,) * 5,
        compiler_params=PARAMS,
        cost_estimate=cost(COMBINE_COST),
        name="combine",
    )(own, first, second, plus, minus, whole, half, att)


def pack_kernel(first_ref, slices_ref, *refs):
    out_ref = refs[-1]
    out_ref[:BLK] = first_ref[...]
    out_ref[BLK:] = slices_ref[...]


def pack(first, slices, after):
    return pl.pallas_call(
        pack_kernel,
        out_shape=shape(BLK + slices.shape[0], PAIR),
        in_specs=[VMEM] * (2 + len(after)),
        out_specs=VMEM,
        compiler_params=PARAMS,
        cost_estimate=cost(PACK_COST),
        name="pack",
    )(first, slices, *after)


def project_kernel(att_ref, two_ref, three_ref, mine_ref, whole_ref, out_ref):
    core = lax.axis_index("seq") & 1
    here = jnp.where(core == 0, three_ref[...], two_ref[...])
    out_ref[...] = dot_nn(att_ref[...], mine_ref[...]) + dot_nn(here, whole_ref[...])


def project(att, two, three, mine, whole):
    return pl.pallas_call(
        project_kernel,
        out_shape=shape(BLK, mine.shape[1], kind=F32),
        in_specs=[VMEM] * 5,
        out_specs=VMEM,
        compiler_params=PARAMS,
        name="project",
    )(att, two, three, mine, whole)


def gather_kernel(one_ref, second_ref, partial_ref, out_ref):
    del second_ref, partial_ref
    out_ref[...] = one_ref[...]


def gather(one, second, partial):
    return pl.pallas_call(
        gather_kernel,
        out_shape=shape(BLK, HD),
        in_specs=[VMEM] * 3,
        out_specs=VMEM,
        compiler_params=PARAMS,
        cost_estimate=cost(GATHER_COST),
        name="gather",
    )(one, second, partial)


def settle(total, lead, dk_ref, dv_ref):
    for ref, c in ((dk_ref, 0), (dv_ref, HD)):
        ref[:STRIDE_ROWS] = lead[:, c:c + HD].astype(ref.dtype)
        ref[STRIDE_ROWS:] = total[STRIDE_ROWS:, c:c + HD].astype(ref.dtype)


def finish_ring_kernel(partial_ref, one_ref, two_ref, three_ref, half_ref, first_ref, own_ref,
                       second_ref, dq_ref, mixed_hbm, dq_hbm, dk_hbm, dv_hbm,
                       mixed_ref, dk_ref, dv_ref, sems):
    copies = []

    def send(src, dst):
        copy = pltpu.make_async_copy(src, dst, sems.at[len(copies)])
        copy.start()
        copies.append(copy)

    send(dq_ref, dq_hbm)
    core = lax.axis_index("seq") & 1
    half = HD // 2
    one = one_ref[...]
    there = jnp.where(core == 0, two_ref[...], three_ref[...])
    here_half = jnp.where(core == 0, one[:, :half], one[:, half:])
    there_half = jnp.where(core == 0, one[:, half:], one[:, :half])
    width = half_ref.shape[1]
    half_row = BLK + (width // PAIR) * HD
    for r in range(0, BLK, half):
        rows = slice(r, r + half)
        for i, c in enumerate(range(0, width, PAIR)):
            span = slice(c, c + PAIR)
            other_whole = first_ref[BLK + i * HD:BLK + (i + 1) * HD]
            other_half = first_ref[half_row + i * half:half_row + (i + 1) * half]
            mixed = partial_ref[rows, span] + dot_nn(there[rows], other_whole)
            mixed = mixed + dot_nn(here_half[rows], half_ref[half_rows(), span])
            mixed = mixed + dot_nn(there_half[rows], other_half)
            mixed_ref[rows, span] = mixed.astype(mixed_ref.dtype)
        send(mixed_ref.at[pl.ds(r, half)], mixed_hbm.at[pl.ds(r, half)])
    total = own_ref[...] + first_ref[:BLK].astype(F32) + second_ref[...].astype(F32)
    settle(total, total[:STRIDE_ROWS], dk_ref, dv_ref)
    send(dk_ref, dk_hbm)
    send(dv_ref, dv_hbm)
    for copy in copies:
        copy.wait()


def finish_ring(*args):
    width = args[0].shape[1]
    return pl.pallas_call(
        finish_ring_kernel,
        out_shape=(shape(BLK, width),) + (shape(BLK, HD),) * 3,
        in_specs=[VMEM] * len(args),
        out_specs=(HBM,) * 4,
        scratch_shapes=[
            pltpu.VMEM((BLK, width), BF16),
            pltpu.VMEM((BLK, HD), BF16),
            pltpu.VMEM((BLK, HD), BF16),
            pltpu.SemaphoreType.DMA((5,)),
        ],
        compiler_params=PARAMS,
        name="finish",
    )(*args)


def finish_kernel(count, *refs):
    att_refs = refs[:count]
    w_refs = refs[count:2 * count]
    own_ref, first_ref, second_ref, side_ref, mixed_ref, dk_ref, dv_ref = refs[2 * count:]
    mixed = None
    for ref, w in zip(att_refs, w_refs):
        term = dot_nn(ref[...], w[...])
        mixed = term if mixed is None else mixed + term
    mixed_ref[...] = mixed.astype(mixed_ref.dtype)
    total = own_ref[...] + first_ref[...].astype(F32) + second_ref[...].astype(F32)
    lead = total[:STRIDE_ROWS]
    for i in range(side_ref.shape[0] // STRIDE_ROWS):
        lead = lead + side_ref[i * STRIDE_ROWS:(i + 1) * STRIDE_ROWS].astype(F32)
    settle(total, lead, dk_ref, dv_ref)


def finish(attentions, slices, own, first, second, side):
    width = slices[0].shape[1]
    count = len(attentions)

    def body(*refs):
        finish_kernel(count, *refs)

    return pl.pallas_call(
        body,
        out_shape=(shape(BLK, width), shape(BLK, HD), shape(BLK, HD)),
        in_specs=[VMEM] * (2 * count + 4),
        out_specs=(VMEM,) * 3,
        compiler_params=PARAMS,
        name="finish",
    )(*attentions, *slices, own, first, second, side)


def spread_slice(array):
    seq = lax.axis_size("seq")
    heads = lax.axis_size("head")
    pairs = [(b * heads + h, b * heads + (h ^ (3 - b % 2))) for b in range(seq)
             for h in range(heads)]
    return lax.ppermute(array, ("seq", "head"), pairs)


def shards(queries, key_rows, value_rows, out_weight, strided_index, cotangent):
    seq = lax.axis_size("seq")
    heads = lax.axis_size("head")
    ring = seq == 8 and heads == 4
    n = STRIDE_ROWS
    side_rows = seq * n
    columns = 3 * BLK + side_rows
    own = jnp.concatenate([key_rows, value_rows], axis=1)
    first = trade(own, 1)
    mult, queries, weight, *slices = weight_slices(
        ring, strided_index, queries, out_weight, heads, columns, own
    )
    if ring:
        mine, whole, half = slices
        half = swap(half, 1)
        near, pair, whole = leads(own, first, mult, whole)
        grad, *terms = prepare(cotangent, weight, pair, mult, queries, own, first)
        whole = spread_slice(whole)
        near = trade(near, -1)
        blocks = (own, first, near, trade(pair, 3), trade(pair, 4))
        side = 3 * BLK
        places = [side + i * n for i in range(6)]
        pieces = [[(i * BLK, (i + 1) * BLK)] for i in range(3)]
        pieces += [[(places[1], places[4])], [(places[4], places[5]), (places[0], places[1])]]
        att, dq, own_sum, first_sum, second_sum, to_plus, to_minus = attend(
            mult, queries, grad, terms, blocks, pieces, 3
        )
        far = [swap(att, 2), swap(att, 3)]
        own_sum, to_first, to_second, out_slices, last = combine(
            own_sum, first_sum, second_sum, trade(to_plus, 3), trade(to_minus, -3), whole, half,
            att,
        )
        from_second = trade(to_second, -1)
        packed = trade(pack(to_first, out_slices, far), 1)
        partial = project(att, *far, mine, whole)
        one = gather(swap(last, 1), from_second, partial)
        mixed, dq, dk, dv = finish_ring(
            partial, one, *far, half, packed, own_sum, from_second, dq
        )
    else:
        second = trade(own, -1)
        grad, *terms = prepare(cotangent, weight, own, mult, queries, own, first)
        slices = [slices[0]] + [swap(slices[r], r) for r in range(1, heads)]
        spread = jnp.broadcast_to(own[None, :n], (seq, n, PAIR))
        side = lax.all_to_all(spread, "seq", 0, 0).reshape(side_rows, PAIR)
        pieces = [[(i * BLK, (i + 1) * BLK)] for i in range(3)] + [[(3 * BLK, columns)]]
        att, dq, own_sum, to_first, to_second, to_side = attend(
            mult, queries, grad, terms, (own, first, second, side), pieces, 1
        )
        from_side = lax.all_to_all(to_side.reshape(seq, n, PAIR), "seq", 0, 0)
        mixed, dk, dv = finish(
            [att] + [swap(att, r) for r in range(1, heads)], slices, own_sum,
            trade(to_first, 1), trade(to_second, -1), from_side.reshape(side_rows, PAIR),
        )
    return (mixed, dq, dk, dv)


def solution(mesh):
    in_specs = (
        P("seq", "head"),
        P("seq", "head"),
        P("seq", "head"),
        P("head", None),
        P("seq", None),
        P("seq", None),
    )
    out_specs = (P("seq", "head"), P("seq", "head"), P("seq", "head"), P("seq", "head"))
    return jax.shard_map(shards, mesh=mesh, in_specs=in_specs, out_specs=out_specs, check_vma=False)
```

```python
import jax
import jax.numpy as jnp
from jax import lax
from jax.experimental import pallas as pl
from jax.experimental.pallas import tpu as pltpu
from jax.sharding import PartitionSpec as P

HD = 128
BLK = 128
STRIDE_ROWS = 32
MARGIN = 16
PAIR = 2 * HD
SCALE = HD ** (-0.5)
LOG2E = 1.4426950408889634
ABSENT = -1e30
VMEM = pl.BlockSpec(memory_space=pltpu.VMEM)
HBM = pl.BlockSpec(memory_space=pltpu.HBM)
PARAMS = pltpu.CompilerParams(vmem_limit_bytes=40 * 1024 * 1024)
FULL = pltpu.CompilerParams(vmem_limit_bytes=int(52.8 * 1024 * 1024))
BF16 = jnp.bfloat16
PREPARE_COST = 10**10
ATTEND_COST = 10**10
GRAD_COST = 0
COMBINE_COST = 10**10
GATHER_COST = 10**10
PACK_COST = 10**10
F32 = jnp.float32


def dot_nt(a, b):
    return lax.dot_general(a, b, (((1,), (1,)), ((), ())), preferred_element_type=F32)


def dot_nn(a, b):
    return lax.dot_general(a, b, (((1,), (0,)), ((), ())), preferred_element_type=F32)


def dot_tn(a, b):
    return lax.dot_general(a, b, (((0,), (0,)), ((), ())), preferred_element_type=F32)


def shape(*dims, kind=BF16):
    return jax.ShapeDtypeStruct(dims, kind)


def trade(array, step):
    count = lax.axis_size("seq")
    return lax.ppermute(
        array, "seq", [(i, (i + (step if i % 2 == 0 else -step)) % count) for i in range(count)]
    )


def swap(array, mask):
    count = lax.axis_size("head")
    return lax.ppermute(array, "head", [(i, i ^ mask) for i in range(count)])


def count_of(picks, group):
    total = jnp.int32(0)
    for pick in picks:
        total = total + jnp.where(pick == group, 1, 0)
    return total.astype(F32)


def fill_multiplicity(ring, index_ref, mult_ref):
    per_block = BLK // STRIDE_ROWS
    picks = [index_ref[0, i] for i in range(index_ref.shape[1])]
    shape_of = mult_ref.shape
    lane = lax.broadcasted_iota(jnp.int32, shape_of, 1)
    mult = jnp.where(lane < 3 * BLK, 1.0, 0.0)
    if ring:
        b = lax.axis_index("seq")
        sign = 1 - 2 * (b & 1)
        counts = [count_of(picks, j) for j in range(2)]
        places = [(0, 0), (BLK, 1), (2 * BLK, -1)]
        places += [(3 * BLK + i * STRIDE_ROWS, o) for i, o in enumerate((-2, 3, 2, 4, 5))]
        for start, offset in places:
            owner = (b + 16 + sign * offset) & 7
            count = jnp.where(owner < per_block, counts[0], counts[1])
            inside = (lane >= start) & (lane < start + STRIDE_ROWS)
            mult = mult + jnp.where(inside, count, 0.0)
    else:
        for j in range((shape_of[1] - 3 * BLK) // BLK):
            start = (3 + j) * BLK
            inside = (lane >= start) & (lane < start + BLK)
            mult = mult + jnp.where(inside, count_of(picks, j), 0.0)
    mult_ref[...] = mult


def cost(flops):
    return pl.CostEstimate(flops=flops, bytes_accessed=0, transcendentals=0)


CHUNKS = 8


def row_copies(src, dst, sems, first):
    rows = dst.shape[0] // CHUNKS
    spans = [pl.ds(i * rows, rows) for i in range(CHUNKS)]
    return [pltpu.make_async_copy(src.at[span], dst.at[span], sems.at[first + i])
            for i, span in enumerate(spans)]


def slices_kernel(ring, index_hbm, q_hbm, w_hbm, after_ref, mult_ref, q_ref, w_ref, *refs):
    del after_ref
    index_ref, sems = refs[-2:]
    slice_refs = refs[:-2]
    copies = [pltpu.make_async_copy(index_hbm, index_ref, sems.at[CHUNKS])]
    copies += row_copies(w_hbm, w_ref, sems, 0)
    copies.append(pltpu.make_async_copy(q_hbm, q_ref, sems.at[CHUNKS + 1]))
    for copy in copies:
        copy.start()
    copies[0].wait()
    fill_multiplicity(ring, index_ref, mult_ref)
    for copy in copies[1:]:
        copy.wait()
    width = slice_refs[0].shape[1]
    head = lax.axis_index("head")

    def columns(h):
        return pl.ds(pl.multiple_of(h * width, width), width)

    if ring:
        core = lax.axis_index("seq") & 1
        half = HD // 2
        mine_ref, whole_ref, half_ref = slice_refs
        mine_ref[...] = w_ref[:, columns(head)]
        whole_ref[...] = w_ref[:, columns(head ^ (3 - core))]
        rows = pl.ds(pl.multiple_of(core * (half - MARGIN), MARGIN), half + MARGIN)
        half_ref[...] = w_ref[rows, columns(head ^ 1)]
    else:
        for r, ref in enumerate(slice_refs):
            ref[...] = w_ref[:, columns(head ^ r)]


def weight_slices(ring, index, queries, out_weight, heads, columns, after):
    width = out_weight.shape[1] // heads
    rows = (HD, HD, HD // 2 + MARGIN) if ring else (HD,) * heads

    def body(*refs):
        slices_kernel(ring, *refs)

    return pl.pallas_call(
        body,
        out_shape=(shape(8, columns, kind=F32), shape(BLK, HD), shape(*out_weight.shape))
        + tuple(shape(r, width) for r in rows),
        in_specs=[HBM] * 3 + [VMEM],
        out_specs=(VMEM,) * (3 + len(rows)),
        scratch_shapes=[
            pltpu.SMEM(index.shape, jnp.int32),
            pltpu.SemaphoreType.DMA((2 + CHUNKS,)),
        ],
        compiler_params=FULL,
        cost_estimate=cost(PREPARE_COST),
        name="slices",
    )(index, queries, out_weight, after)


def prepare_kernel(cot_ref, w_ref, after_ref, grad_ref):
    del after_ref
    grad_ref[...] = dot_nt(cot_ref[...], w_ref[...]).astype(grad_ref.dtype)


def prepare(cotangent, out_weight, after):
    return pl.pallas_call(
        prepare_kernel,
        out_shape=shape(BLK, HD),
        in_specs=[VMEM] * 3,
        out_specs=VMEM,
        compiler_params=PARAMS,
        cost_estimate=cost(GRAD_COST),
        name="prepare",
    )(cotangent, out_weight, after)


def lead_kernel(own_ref, first_ref, mult_ref, whole_ref, near_ref, pair_ref, whole_out):
    del mult_ref
    n = STRIDE_ROWS
    near_ref[:BLK] = own_ref[...]
    near_ref[BLK:] = first_ref[:n]
    pair_ref[:n] = own_ref[:n]
    pair_ref[n:] = first_ref[:n]
    whole_out[...] = whole_ref[...]


def leads(own, first, mult, whole):
    n = STRIDE_ROWS
    return pl.pallas_call(
        lead_kernel,
        out_shape=(shape(BLK + n, PAIR), shape(2 * n, PAIR), shape(*whole.shape)),
        in_specs=[VMEM] * 4,
        out_specs=(VMEM,) * 3,
        compiler_params=PARAMS,
        name="leads",
    )(own, first, mult, whole)


def attend_kernel(blocks, pieces, mult_ref, q_ref, grad_ref, *refs):
    block_refs = refs[:blocks]
    att_ref, dq_ref = refs[blocks:blocks + 2]
    sum_refs = refs[blocks + 2:-1]
    keys_ref = refs[-1]
    total_rows = keys_ref.shape[0]
    row = 0
    for ref in block_refs:
        keys_ref[row:row + ref.shape[0], :] = ref[...]
        row += ref.shape[0]
    if row < total_rows:
        keys_ref[row:, :] = jnp.zeros((total_rows - row, PAIR), BF16)
    keys = keys_ref[:, :HD]
    values = keys_ref[:, HD:]
    q = q_ref[...]
    grad = grad_ref[...]
    mult = mult_ref[0:1, :]

    scores = dot_nt(q, keys) + jnp.where(mult > 0.0, 0.0, ABSENT)
    top = jnp.max(scores, axis=1, keepdims=True)
    terms = jnp.exp2((scores - top) * (SCALE * LOG2E)) * mult
    probability = terms * (1.0 / jnp.sum(terms, axis=1, keepdims=True))
    weights = probability.astype(BF16)
    att_ref[...] = dot_nn(weights, values).astype(BF16)

    grad_weights = dot_nt(grad, values)
    delta = jnp.sum(probability * grad_weights, axis=1, keepdims=True)
    grad_scores = (probability * (grad_weights - delta) * SCALE).astype(BF16)
    dq_ref[...] = dot_nn(grad_scores, keys).astype(BF16)
    key_terms = dot_tn(grad_scores, q)
    value_terms = dot_tn(weights, grad)
    for spans, ref in zip(pieces, sum_refs):
        row = 0
        for start, end in spans:
            rows = slice(row, row + end - start)
            ref[rows, :HD] = key_terms[start:end].astype(ref.dtype)
            ref[rows, HD:] = value_terms[start:end].astype(ref.dtype)
            row += end - start


def attend(mult, q, grad, blocks, pieces, wide):
    def body(*refs):
        attend_kernel(len(blocks), pieces, *refs)

    sums = []
    for i, spans in enumerate(pieces):
        rows = sum(end - start for start, end in spans)
        sums.append(shape(rows, PAIR, kind=F32 if i < wide else BF16))
    return pl.pallas_call(
        body,
        out_shape=(shape(BLK, HD), shape(BLK, HD), *sums),
        in_specs=[VMEM] * (3 + len(blocks)),
        out_specs=(VMEM,) * (2 + len(sums)),
        scratch_shapes=[pltpu.VMEM((mult.shape[1], PAIR), BF16)],
        compiler_params=PARAMS,
        cost_estimate=cost(ATTEND_COST),
        name="attend",
    )(mult, q, grad, *blocks)


def half_rows():
    core = lax.axis_index("seq") & 1
    return pl.ds(pl.multiple_of(core * MARGIN, MARGIN), HD // 2)


def combine_kernel(own_ref, first_ref, second_ref, plus_ref, minus_ref, whole_ref, half_ref,
                   att_ref, own_out, first_out, second_out, slices_out, att_out):
    plus = plus_ref[...].astype(F32)
    minus = minus_ref[...].astype(F32)
    n = STRIDE_ROWS
    own_out[n:] = own_ref[n:]
    own_out[:n] = own_ref[:n] + plus[:n] + minus[:n]
    second_out[n:] = second_ref[n:].astype(BF16)
    second_out[:n] = (second_ref[:n] + plus[2 * n:] + minus[n:]).astype(BF16)
    first_out[n:] = first_ref[n:].astype(BF16)
    first_out[:n] = (first_ref[:n] + plus[n:2 * n]).astype(BF16)
    att_out[...] = att_ref[...]
    row = 0
    for ref, rows in ((whole_ref, slice(0, HD)), (half_ref, half_rows())):
        for c in range(0, ref.shape[1], PAIR):
            piece = ref[rows, c:c + PAIR]
            slices_out[row:row + piece.shape[0]] = piece
            row += piece.shape[0]


def combine(own, first, second, plus, minus, whole, half, att):
    extra = (HD + HD // 2) * whole.shape[1] // PAIR
    return pl.pallas_call(
        combine_kernel,
        out_shape=(shape(BLK, PAIR, kind=F32), shape(BLK, PAIR), shape(BLK, PAIR),
                   shape(extra, PAIR), shape(BLK, HD)),
        in_specs=[VMEM] * 8,
        out_specs=(VMEM,) * 5,
        compiler_params=PARAMS,
        cost_estimate=cost(COMBINE_COST),
        name="combine",
    )(own, first, second, plus, minus, whole, half, att)


def pack_kernel(first_ref, slices_ref, after_ref, out_ref):
    del after_ref
    out_ref[:BLK] = first_ref[...]
    out_ref[BLK:] = slices_ref[...]


def pack(first, slices, after):
    return pl.pallas_call(
        pack_kernel,
        out_shape=shape(BLK + slices.shape[0], PAIR),
        in_specs=[VMEM] * 3,
        out_specs=VMEM,
        compiler_params=PARAMS,
        cost_estimate=cost(PACK_COST),
        name="pack",
    )(first, slices, after)


def project_kernel(att_ref, two_ref, three_ref, mine_ref, whole_ref, out_ref):
    core = lax.axis_index("seq") & 1
    here = jnp.where(core == 0, three_ref[...], two_ref[...])
    out_ref[...] = dot_nn(att_ref[...], mine_ref[...]) + dot_nn(here, whole_ref[...])


def project(att, two, three, mine, whole):
    return pl.pallas_call(
        project_kernel,
        out_shape=shape(BLK, mine.shape[1], kind=F32),
        in_specs=[VMEM] * 5,
        out_specs=VMEM,
        compiler_params=PARAMS,
        name="project",
    )(att, two, three, mine, whole)


def gather_kernel(one_ref, second_ref, partial_ref, out_ref):
    del second_ref, partial_ref
    out_ref[...] = one_ref[...]


def gather(one, second, partial):
    return pl.pallas_call(
        gather_kernel,
        out_shape=shape(BLK, HD),
        in_specs=[VMEM] * 3,
        out_specs=VMEM,
        compiler_params=PARAMS,
        cost_estimate=cost(GATHER_COST),
        name="gather",
    )(one, second, partial)


def settle(total, lead, dk_ref, dv_ref):
    for ref, c in ((dk_ref, 0), (dv_ref, HD)):
        ref[:STRIDE_ROWS] = lead[:, c:c + HD].astype(ref.dtype)
        ref[STRIDE_ROWS:] = total[STRIDE_ROWS:, c:c + HD].astype(ref.dtype)


def finish_ring_kernel(partial_ref, one_ref, two_ref, three_ref, half_ref, first_ref, own_ref,
                       second_ref, dq_ref, mixed_hbm, dq_hbm, dk_hbm, dv_hbm,
                       mixed_ref, dk_ref, dv_ref, sems):
    copies = []

    def send(src, dst):
        copy = pltpu.make_async_copy(src, dst, sems.at[len(copies)])
        copy.start()
        copies.append(copy)

    send(dq_ref, dq_hbm)
    core = lax.axis_index("seq") & 1
    half = HD // 2
    one = one_ref[...]
    there = jnp.where(core == 0, two_ref[...], three_ref[...])
    here_half = jnp.where(core == 0, one[:, :half], one[:, half:])
    there_half = jnp.where(core == 0, one[:, half:], one[:, :half])
    width = half_ref.shape[1]
    half_row = BLK + (width // PAIR) * HD
    for r in range(0, BLK, half):
        rows = slice(r, r + half)
        for i, c in enumerate(range(0, width, PAIR)):
            span = slice(c, c + PAIR)
            other_whole = first_ref[BLK + i * HD:BLK + (i + 1) * HD]
            other_half = first_ref[half_row + i * half:half_row + (i + 1) * half]
            mixed = partial_ref[rows, span] + dot_nn(there[rows], other_whole)
            mixed = mixed + dot_nn(here_half[rows], half_ref[half_rows(), span])
            mixed = mixed + dot_nn(there_half[rows], other_half)
            mixed_ref[rows, span] = mixed.astype(mixed_ref.dtype)
        send(mixed_ref.at[pl.ds(r, half)], mixed_hbm.at[pl.ds(r, half)])
    total = own_ref[...] + first_ref[:BLK].astype(F32) + second_ref[...].astype(F32)
    settle(total, total[:STRIDE_ROWS], dk_ref, dv_ref)
    send(dk_ref, dk_hbm)
    send(dv_ref, dv_hbm)
    for copy in copies:
        copy.wait()


def finish_ring(*args):
    width = args[0].shape[1]
    return pl.pallas_call(
        finish_ring_kernel,
        out_shape=(shape(BLK, width),) + (shape(BLK, HD),) * 3,
        in_specs=[VMEM] * len(args),
        out_specs=(HBM,) * 4,
        scratch_shapes=[
            pltpu.VMEM((BLK, width), BF16),
            pltpu.VMEM((BLK, HD), BF16),
            pltpu.VMEM((BLK, HD), BF16),
            pltpu.SemaphoreType.DMA((5,)),
        ],
        compiler_params=PARAMS,
        name="finish",
    )(*args)


def finish_kernel(count, *refs):
    att_refs = refs[:count]
    w_refs = refs[count:2 * count]
    own_ref, first_ref, second_ref, side_ref, mixed_ref, dk_ref, dv_ref = refs[2 * count:]
    mixed = None
    for ref, w in zip(att_refs, w_refs):
        term = dot_nn(ref[...], w[...])
        mixed = term if mixed is None else mixed + term
    mixed_ref[...] = mixed.astype(mixed_ref.dtype)
    total = own_ref[...] + first_ref[...].astype(F32) + second_ref[...].astype(F32)
    lead = total[:STRIDE_ROWS]
    for i in range(side_ref.shape[0] // STRIDE_ROWS):
        lead = lead + side_ref[i * STRIDE_ROWS:(i + 1) * STRIDE_ROWS].astype(F32)
    settle(total, lead, dk_ref, dv_ref)


def finish(attentions, slices, own, first, second, side):
    width = slices[0].shape[1]
    count = len(attentions)

    def body(*refs):
        finish_kernel(count, *refs)

    return pl.pallas_call(
        body,
        out_shape=(shape(BLK, width), shape(BLK, HD), shape(BLK, HD)),
        in_specs=[VMEM] * (2 * count + 4),
        out_specs=(VMEM,) * 3,
        compiler_params=PARAMS,
        name="finish",
    )(*attentions, *slices, own, first, second, side)


def spread_slice(array):
    seq = lax.axis_size("seq")
    heads = lax.axis_size("head")
    pairs = [(b * heads + h, b * heads + (h ^ (3 - b % 2))) for b in range(seq)
             for h in range(heads)]
    return lax.ppermute(array, ("seq", "head"), pairs)


def shards(queries, key_rows, value_rows, out_weight, strided_index, cotangent):
    seq = lax.axis_size("seq")
    heads = lax.axis_size("head")
    ring = seq == 8 and heads == 4
    n = STRIDE_ROWS
    side_rows = seq * n
    columns = 3 * BLK + side_rows
    own = jnp.concatenate([key_rows, value_rows], axis=1)
    first = trade(own, 1)
    mult, queries, weight, *slices = weight_slices(
        ring, strided_index, queries, out_weight, heads, columns, own
    )
    if ring:
        mine, whole, half = slices
        half = swap(half, 1)
        near, pair, whole = leads(own, first, mult, whole)
        grad = prepare(cotangent, weight, pair)
        whole = spread_slice(whole)
        near = trade(near, -1)
        blocks = (own, first, near, trade(pair, 3), trade(pair, 4))
        side = 3 * BLK
        places = [side + i * n for i in range(6)]
        pieces = [[(i * BLK, (i + 1) * BLK)] for i in range(3)]
        pieces += [[(places[1], places[4])], [(places[4], places[5]), (places[0], places[1])]]
        att, dq, own_sum, first_sum, second_sum, to_plus, to_minus = attend(
            mult, queries, grad, blocks, pieces, 3
        )
        far = [swap(att, 2), swap(att, 3)]
        own_sum, to_first, to_second, out_slices, last = combine(
            own_sum, first_sum, second_sum, trade(to_plus, 3), trade(to_minus, -3), whole, half,
            att,
        )
        from_second = trade(to_second, -1)
        packed = trade(pack(to_first, out_slices, far[1]), 1)
        partial = project(att, *far, mine, whole)
        one = gather(swap(last, 1), from_second, partial)
        mixed, dq, dk, dv = finish_ring(
            partial, one, *far, half, packed, own_sum, from_second, dq
        )
    else:
        second = trade(own, -1)
        grad = prepare(cotangent, weight, own)
        slices = [slices[0]] + [swap(slices[r], r) for r in range(1, heads)]
        spread = jnp.broadcast_to(own[None, :n], (seq, n, PAIR))
        side = lax.all_to_all(spread, "seq", 0, 0).reshape(side_rows, PAIR)
        pieces = [[(i * BLK, (i + 1) * BLK)] for i in range(3)] + [[(3 * BLK, columns)]]
        att, dq, own_sum, to_first, to_second, to_side = attend(
            mult, queries, grad, (own, first, second, side), pieces, 1
        )
        from_side = lax.all_to_all(to_side.reshape(seq, n, PAIR), "seq", 0, 0)
        mixed, dk, dv = finish(
            [att] + [swap(att, r) for r in range(1, heads)], slices, own_sum,
            trade(to_first, 1), trade(to_second, -1), from_side.reshape(side_rows, PAIR),
        )
    return (mixed, dq, dk, dv)


def solution(mesh):
    in_specs = (
        P("seq", "head"),
        P("seq", "head"),
        P("seq", "head"),
        P("head", None),
        P("seq", None),
        P("seq", None),
    )
    out_specs = (P("seq", "head"), P("seq", "head"), P("seq", "head"), P("seq", "head"))
    return jax.shard_map(shards, mesh=mesh, in_specs=in_specs, out_specs=out_specs, check_vma=False)
```
